128 devices in a mesh: dom: 128 (over y, z, x, core).
Axes of the slice: x: 4, y: 4, z: 4, core: 2. Of those that a mesh axis runs over, the one named last changes fastest.
Arguments:
- primal: float32 [81, 262144], P(None, 'dom'), may hold values from -6 to 6
- dual: float32 [81, 262144], P(None, 'dom'), may hold values from -6 to 6
- load: float32 [81, 262144], P(None, 'dom'), may hold values from -6 to 6
- cell_size: float32 [262144], P('dom'), may hold values from 0.05 to 1.5
- cell_count: int32 [128], replicated, may hold values from 256 to 2048, as said below
- ghost_send: int32 [128, 8, 256], P('dom'), may hold values from 0 to 2047, as said below
- face_cell: int32 [786432], P('dom'), may hold values from 0 to 2047, as said below
- face_other: int32 [786432], P('dom'), may hold values from 0 to 4095, as said below
- face_dir: int32 [786432], P('dom'), may hold values from 0 to 5
- hanging: int32 [786432], P('dom'), may hold values 0 or 1
- stiffness: float32 [81, 81], replicated, may hold values from -0.625 to 0.625
- recon: float32 [648, 648], replicated, may hold values from -0.25 to 0.25
- traction: float32 [162, 81], replicated, may hold values from -0.15625 to 0.15625
- trace: float32 [162, 81], replicated, may hold values from -0.625 to 0.625
Outputs:
- indicator: float32 [262144], P('dom')
- share: float32 [262144], P('dom')
The draws below stay inside these ranges and needn't reach their ends.
Inputs may be any that keep to these rules, and one draw needn't show every extreme that they name: `cell_count`: the sum over partitions is a multiple of 8. ghost_send[s, k] holds 256 distinct live slots of partition s. `face_cell`: a live slot of the face's partition. `face_other`: below 2048: a live slot of the face's partition other than face_cell; otherwise a ghost entry whose source partition r - o_k lies in 0 to 127.
All inputs are finite; a program needn't handle non-finite values. No bound on the sum of `hanging` on one device may be relied on, other than what follows from the above.
Results may differ from the reference program's by a relative error of at most 0.0003.
Values sent between devices are 32-bit elements; how exact they have to be, the bound alone decides.
A program may use at most 192 MiB of HBM per device.

```python
import jax
import jax.numpy as jnp
from jax import lax

DOF = 81
FACE_DOF = 27
DIRS = 6
CHILD = 8
NEIGH = 8
CELL_DEV = 2048
GHOST = 256
RANKS = 128
CELLS = 262144
FACE_DEV = 6144
FACES = 786432
FAM_DOF = 648


def rank_counts(key):
    rank_ids = jnp.arange(RANKS, dtype=jnp.int32)
    last_rank = RANKS - 1
    base_load = CELL_DEV // 8 + 7 * CELL_DEV // 8 * rank_ids * rank_ids // (last_rank * last_rank)
    jitter = jax.random.randint(jax.random.fold_in(key, 101), (RANKS,), 0, CELL_DEV // 8 + 1)
    counts = jnp.minimum(base_load + jitter, CELL_DEV)
    counts = counts.at[0].set(CELL_DEV // 8 + 3)
    counts = counts.at[1].set(CELL_DEV // 8)
    counts = counts.at[RANKS - 2].set(CELL_DEV)
    before_last = jnp.sum(counts[:RANKS - 1])
    counts = counts.at[RANKS - 1].set(CELL_DEV - before_last % 8)
    return counts.astype(jnp.int32)


def face_cells(key, counts):
    live_limit = jnp.repeat(counts, FACE_DEV)
    return jax.random.randint(jax.random.fold_in(key, 103), (FACES,), 0, live_limit).astype(jnp.int32)


def draw_cell_count(key, part):
    return rank_counts(key)


def draw_ghost_send(key, part):
    counts = rank_counts(key)
    key = jax.random.fold_in(key, 2)
    scores = jax.random.randint(key, (RANKS * NEIGH, CELL_DEV), 0, 16384)
    position = jnp.arange(CELL_DEV, dtype=jnp.int32)
    owner_count = jnp.repeat(counts, NEIGH)[:, None]
    sort_keys = jnp.where(position[None, :] < owner_count, scores * CELL_DEV + position[None, :], 2147483647)
    chosen = jnp.argsort(sort_keys, axis=1, stable=True)[:, :GHOST]
    return chosen.reshape(RANKS, NEIGH, GHOST).astype(jnp.int32)


def draw_face_cell(key, part):
    counts = rank_counts(key)
    return face_cells(key, counts)


def draw_face_other(key, part):
    counts = rank_counts(key)
    own_cells = face_cells(key, counts)
    key = jax.random.fold_in(key, 4)
    key_step, key_list, key_slot, key_far = jax.random.split(key, 4)
    face_rank = jnp.arange(FACES, dtype=jnp.int32) // FACE_DEV
    live_limit = jnp.repeat(counts, FACE_DEV)
    step_ahead = jax.random.randint(key_step, (FACES,), 1, live_limit)
    local_other = (own_cells + step_ahead) % live_limit
    list_index = jax.random.randint(key_list, (FACES,), 0, NEIGH)
    ghost_slot = jax.random.randint(key_slot, (FACES,), 0, GHOST)
    is_remote = jax.random.randint(key_far, (FACES,), 0, 2)
    offset = jnp.left_shift(jnp.int32(1), list_index // 2) * (1 - 2 * (list_index % 2))
    sender = face_rank - offset
    use_ghost = (is_remote == 1) & (sender >= 0) & (sender < RANKS)
    return jnp.where(use_ghost, CELL_DEV + list_index * GHOST + ghost_slot, local_other).astype(jnp.int32)


def draw_cell_size(key, part):
    key = jax.random.fold_in(key, 5)
    uniform_draw = jax.random.uniform(key, (CELLS,), jnp.float32)
    cell_sizes = 0.05 * jnp.exp(uniform_draw * jnp.log(10.0))
    return cell_sizes.astype(jnp.float32)


def set_ends(values, own_key, low, top_value):
    extent = values.shape
    spot = [jax.random.randint(jax.random.fold_in(own_key, axis), (), 0, extent[axis]) for axis in range(len(extent))]
    values = values.at[tuple(spot)].set(low)
    longest = extent.index(max(extent))
    spot[longest] = (spot[longest] + 1) % extent[longest]
    return values.at[tuple(spot)].set(top_value)


def level_of(key, shape, shards, smallest, largest):
    def one(dim, shards_of):
        steps = jax.random.uniform(jax.random.fold_in(jax.random.fold_in(key, 6), dim), (shards_of,), jnp.float32, smallest / len(shards), largest / len(shards))
        return jnp.repeat(jnp.exp(steps), shape[dim] // shards_of).reshape((-1,) + (1,) * (len(shape) - dim - 1))

    loudness = one(*shards[0])
    for cut in shards[1:]:
        loudness = loudness * one(*cut)
    return loudness


def bell_draw(rng, extent, deviation, bound, cuts=(), kind=jnp.bfloat16):
    values = jax.random.normal(rng, extent, jnp.float32) * deviation
    if len(cuts) > 0:
        values = level_of(rng, extent, cuts, -0.22, 0.18) * values
    return jnp.clip(values, min=-bound, max=bound).astype(kind)


def setup_inputs(seed: int = 0) -> dict:
    key_of = jax.random.split(jax.random.key(seed), 15)
    return {
        "primal": bell_draw(key_of[0], (DOF, CELLS), 1.0, 6.0, ((1, 128),), jnp.float32),
        "dual": bell_draw(key_of[1], (DOF, CELLS), 1.0, 6.0, ((1, 128),), jnp.float32),
        "load": bell_draw(key_of[2], (DOF, CELLS), 1.0, 6.0, ((1, 128),), jnp.float32),
        "cell_size": draw_cell_size(jax.random.fold_in(key_of[14], 71), 0),
        "cell_count": draw_cell_count(jax.random.fold_in(key_of[14], 71), 0),
        "ghost_send": draw_ghost_send(jax.random.fold_in(key_of[14], 71), 0),
        "face_cell": draw_face_cell(jax.random.fold_in(key_of[14], 71), 0),
        "face_other": draw_face_other(jax.random.fold_in(key_of[14], 71), 0),
        "face_dir": set_ends(jax.random.randint(key_of[8], (FACES,), 0, DIRS), jax.random.fold_in(key_of[8], 1), 0, DIRS - 1).astype(jnp.int32),
        "hanging": set_ends((jax.random.randint(key_of[9], (FACES,), 0, 4) < 1).astype(jnp.int32), jax.random.fold_in(key_of[9], 1), 0, 1),
        "stiffness": bell_draw(key_of[10], (DOF, DOF), DOF ** -0.5, 0.625, (), jnp.float32),
        "recon": bell_draw(key_of[11], (FAM_DOF, FAM_DOF), FAM_DOF ** -0.5, 0.25, (), jnp.float32),
        "traction": bell_draw(key_of[12], (DIRS * FACE_DOF, DOF), (16 * DOF) ** -0.5, 0.15625, (), jnp.float32),
        "trace": bell_draw(key_of[13], (DIRS * FACE_DOF, DOF), DOF ** -0.5, 0.625, (), jnp.float32),
    }


precise = lax.Precision.HIGHEST


def list_offsets():
    list_index = jnp.arange(NEIGH, dtype=jnp.int32)
    return jnp.left_shift(jnp.int32(1), list_index // 2) * (1 - 2 * (list_index % 2))


def rebuild(columns, recon):
    node_rows = columns.shape[0]
    blocks = columns.shape[1] // CHILD
    family = columns.reshape(node_rows, blocks, CHILD).transpose(2, 0, 1).reshape(CHILD * node_rows, blocks)
    rebuilt = jnp.dot(recon, family, precision=precise, preferred_element_type=jnp.float32)
    return rebuilt.reshape(CHILD, node_rows, blocks).transpose(1, 2, 0).reshape(node_rows, blocks * CHILD)


def pick_direction(all_rows, direction):
    width_cols = all_rows.shape[1]
    dir_table = all_rows.reshape(DIRS, FACE_DOF, width_cols)
    onehot = (direction[None, :] == jnp.arange(DIRS, dtype=jnp.int32)[:, None]).astype(all_rows.dtype)
    return jnp.sum(dir_table * onehot[:, None, :], axis=0)


def reference(primal, dual, load, cell_size, cell_count, ghost_send, face_cell, face_other, face_dir, hanging, stiffness, recon, traction, trace):
    counts = cell_count.astype(jnp.int32)
    rank_ends = jnp.cumsum(counts).astype(jnp.int32)
    starts = rank_ends - counts
    live_total = rank_ends[RANKS - 1]
    slot_ids = jnp.arange(CELLS, dtype=jnp.int32)
    slot_rank = slot_ids // CELL_DEV
    slot_local = slot_ids % CELL_DEV
    live_mask = slot_local < counts[slot_rank]
    morton_pos = jnp.clip(starts[slot_rank] + slot_local, 0, CELLS - 1)
    order_owner = jnp.minimum(jnp.searchsorted(rank_ends, slot_ids, side="right").astype(jnp.int32), RANKS - 1)
    source = jnp.clip(order_owner * CELL_DEV + slot_ids - starts[order_owner], 0, CELLS - 1).astype(jnp.int32)
    weight_order = rebuild(dual[:, source], recon)
    weight = jnp.where(live_mask[None, :], weight_order[:, morton_pos], jnp.float32(0.0))
    residual = load - jnp.dot(stiffness, primal, precision=precise, preferred_element_type=jnp.float32)
    cell_term = cell_size * jnp.sum(residual * weight, axis=0)

    face_ids = jnp.arange(FACES, dtype=jnp.int32)
    face_rank = face_ids // FACE_DEV
    live_face = (face_ids % FACE_DEV) < 3 * counts[face_rank]
    slot_a = face_rank * CELL_DEV + face_cell
    remote = face_other >= CELL_DEV
    ghost_pos = jnp.where(remote, face_other - CELL_DEV, 0)
    list_index = jnp.clip(ghost_pos // GHOST, 0, NEIGH - 1)
    within = ghost_pos % GHOST
    sender = jnp.clip(face_rank - list_offsets()[list_index], 0, RANKS - 1)
    slot_b = jnp.where(remote, sender * CELL_DEV + ghost_send[sender, list_index, within], face_rank * CELL_DEV + face_other).astype(jnp.int32)
    dir_b = face_dir + 1 - 2 * (face_dir % 2)
    face_area = jnp.where(live_face, 1.0 - 0.75 * hanging.astype(jnp.float32), jnp.float32(0.0))

    def face_block(inputs):
        side_a, side_b, dir_a, dir_other, area_here = inputs
        trac_a = pick_direction(jnp.dot(traction, primal[:, side_a], precision=precise, preferred_element_type=jnp.float32), dir_a)
        trac_b = pick_direction(jnp.dot(traction, primal[:, side_b], precision=precise, preferred_element_type=jnp.float32), dir_other)
        trace_a = pick_direction(jnp.dot(trace, weight[:, side_a], precision=precise, preferred_element_type=jnp.float32), dir_a)
        trace_b = pick_direction(jnp.dot(trace, weight[:, side_b], precision=precise, preferred_element_type=jnp.float32), dir_other)
        face_jump = trac_a + trac_b
        return (0.5 * area_here * jnp.sum(face_jump * trace_a, axis=0), 0.5 * area_here * jnp.sum(face_jump * trace_b, axis=0))

    term_a, term_b = lax.map(face_block, (slot_a.reshape(RANKS, FACE_DEV), slot_b.reshape(RANKS, FACE_DEV), face_dir.reshape(RANKS, FACE_DEV), dir_b.reshape(RANKS, FACE_DEV), face_area.reshape(RANKS, FACE_DEV)))
    indicator = cell_term.at[slot_a].add(term_a.reshape(-1)).at[slot_b].add(term_b.reshape(-1))
    indicator = jnp.where(live_mask, indicator, jnp.float32(0.0))
    mean_abs = jnp.sum(jnp.abs(indicator)) / live_total.astype(jnp.float32)
    share = jnp.abs(indicator) / (mean_abs + 1e-6)
    return indicator, share
```

```python
import functools

import jax
import jax.numpy as jnp
from jax import lax
from jax.experimental import pallas as pl
from jax.experimental.pallas import tpu as pltpu
from jax.sharding import PartitionSpec as P

F32 = jnp.float32
BF16 = jnp.bfloat16
I32 = jnp.int32

DOF = 81
FACE_DOF = 27
CHILD = 8
CELLS = 2048
NEIGH = 8
GHOST = 256
GHOSTS = NEIGH * GHOST
SLOTS = CELLS + GHOSTS
FACES = 6144
LANES = 128
BATCH = 16
FAMILIES = 264
CHUNK = 256
CHUNKS = FACES // CHUNK
SPLIT = CHUNK // LANES


def split(x):
    high = x.astype(BF16)
    return high, (x - high.astype(F32)).astype(BF16)


def dot_nt(a, b):
    return lax.dot_general(a, b, (((1,), (1,)), ((), ())), preferred_element_type=F32)


def dot_nn(a, b):
    return lax.dot_general(a, b, (((1,), (0,)), ((), ())), preferred_element_type=F32)


def gather_rows(dst, dst_at, src, index_of, count):
    for base in range(0, count, BATCH):
        rows = [src[pl.ds(index_of(base + u), 1), :] for u in range(BATCH)]
        for u in range(BATCH):
            dst[pl.ds(dst_at + (base + u), 1), :] = rows[u]


def turned_block(src, at):
    return jnp.concatenate([src[:, pl.ds(at, 256)], jnp.zeros((LANES - DOF, 256), F32)], 0).T


def to_cell_major(dst, src, step):
    at = pl.multiple_of(step * 256, 256)
    dst[pl.ds(at, 256), :] = turned_block(src, at)


def fill_operator(operator, traction, trace):
    operator[...] = jnp.zeros(operator.shape, F32)
    for d in range(6):
        rows = slice(d * FACE_DOF, (d + 1) * FACE_DOF)
        operator[64 * d : 64 * d + FACE_DOF, 0:DOF] = traction[rows, :]
        operator[64 * d + 32 : 64 * d + 32 + FACE_DOF, LANES : LANES + DOF] = trace[rows, :]


def fill_table(table, slot, p_rows, w_rows, operator):
    o_hi, o_lo = split(operator[...])
    x_hi, x_lo = split(jnp.concatenate([p_rows[...], w_rows[...]], 1))
    out = dot_nt(x_hi, o_hi) + dot_nt(x_lo, o_hi) + dot_nt(x_hi, o_lo)
    for pair in range(3):
        table[pl.ds(pl.multiple_of(pair * SLOTS + slot, 256), 256), :] = out[:, pair * LANES : (pair + 1) * LANES]


def cell_terms(out, primal, load, w_t, cell_size, stiffness, step):
    at = pl.multiple_of(step * 256, 256)
    s_hi, s_lo = split(stiffness[...])
    p_hi, p_lo = split(primal[:, pl.ds(at, 256)])
    residual = load[:, pl.ds(at, 256)] - (dot_nn(s_hi, p_hi) + dot_nn(s_lo, p_hi) + dot_nn(s_hi, p_lo))
    weight = w_t[pl.ds(at, 256), :].T[:DOF, :]
    total = jnp.sum(residual * weight, axis=0, keepdims=True)
    for r in range(2):
        i = step * 2 + r
        out[pl.ds(i, 1), :] = cell_size[pl.ds(i, 1), :] * total[:, r * LANES : (r + 1) * LANES]


def lanes_of(ref, chunk):
    return jnp.concatenate([ref[pl.ds(chunk * SPLIT + i, 1), :] for i in range(SPLIT)], 1)


def scatter(index, value, high_count):
    width = index.shape[1]
    high = index >> 7
    low = index & 127
    chosen = lax.broadcasted_iota(I32, (high_count, width), 0) == high
    v_hi, v_lo = split(jnp.where(chosen, value, 0.0))
    onehot = jnp.where(lax.broadcasted_iota(I32, (LANES, width), 0) == low, 1.0, 0.0).astype(BF16)
    both = dot_nt(jnp.concatenate([v_hi, v_lo], 0), onehot)
    return both[:high_count] + both[high_count:]


MESH = pl.DeviceIdType.MESH
RANKS = 128
SHIFTS = [(1 << which // 2) * (1 - 2 * (which % 2)) for which in range(NEIGH)]
FIRST_LIST = 4
STAGES = ((1, 8), (8, 16))


def counts_of(counts, me):
    def body(i, carry):
        before, here = carry
        c = counts[i]
        return before + jnp.where(i < me, c, 0), here + jnp.where(i == me, c, 0)

    return lax.fori_loop(0, RANKS, body, (jnp.int32(0), jnp.int32(0)), unroll=8)


def behind(me, by):
    return lax.rem(me + (by + RANKS), RANKS)


def shift_of(k):
    e = k // 2
    power = 1 + e + e * (e - 1) // 2 + e * (e - 1) * (e - 2) // 6
    return power * (1 - 2 * (k % 2))


def in_stage(me, stride, size, step):
    place = lax.rem(me // stride, size)
    return me + (lax.rem(place + step, size) - place) * stride


def gather_list(ghosts, source, send, k):
    gather_rows(ghosts.at[k], 0, source, lambda i: send[k, i], GHOST)


def rebuild(head, live, d_t, before, after, recon_hi, recon_lo, w_t, padded, families, rebuilt, after2):
    after2[0:8, :] = after[...]
    after2[8:16, :] = after[...]
    turned = after2[pl.ds(8 - live % 8, 8), :]
    row = lax.broadcasted_iota(I32, (8, LANES), 0)
    padded[0:8, :] = before[...]

    def fill(i, carry):
        at = pl.multiple_of(i * 8, 8)
        own = d_t[pl.ds(at, 8), :]
        padded[pl.ds(at + 8, 8), :] = jnp.where(row + at < live, own, turned)
        return carry

    lax.fori_loop(0, CELLS // 8, fill, 0, unroll=8)
    padded[CELLS + 8 : CELLS + 16, :] = turned
    padded[CELLS + 16 :, :] = jnp.zeros((padded.shape[0] - CELLS - 16, LANES), F32)
    for m in range(CHILD):
        families[:, m * DOF : (m + 1) * DOF] = padded[pl.ds(head + m, FAMILIES, stride=CHILD), :][:, :DOF]
    f_hi, f_lo = split(families[:, : CHILD * DOF])
    r_hi = recon_hi[0 : CHILD * DOF, :]
    rebuilt[:, : CHILD * DOF] = dot_nt(f_hi, r_hi) + dot_nt(f_lo, r_hi) + dot_nt(f_hi, recon_lo[0 : CHILD * DOF, :])
    lane = lax.broadcasted_iota(I32, (FAMILIES, LANES), 1)
    for m in range(CHILD):
        part = rebuilt[:, m * DOF : m * DOF + LANES]
        padded[pl.ds(m, FAMILIES, stride=CHILD), :] = jnp.where(lane < DOF, part, 0.0)

    def cut(i, carry):
        at = pl.multiple_of(i * 8, 8)
        w_t[pl.ds(at, 8), :] = jnp.where(row + at < live, padded[pl.ds(at + 8 - head, 8), :], 0.0)
        return carry

    lax.fori_loop(0, CELLS // 8, cut, 0, unroll=8)


def kernel(counts, send, primal_in, dual_in, load_in, size_in, send_in, cell_in, other_in, dir_in, hanging_in,
           stiffness_in, recon_in, traction_in, trace_in,
           indicator, facts,
           primal, dual, load, cell_size, send_v, face_cell, face_other, face_dir, hanging, stiffness, recon, traction,
           trace, p_t, d_t, w_t, first, last, before, after, after2, p_out, p_in, w_out, w_in, padded, families, rebuilt,
           operator, table, side_a, side_b0, side_b1, recon_hi, recon_lo, index_a, index_b, smem_a, smem_b, term, partial, returned, part, parts,
           in_sem, index_sem, edge_send, edge_recv, p_send, p_recv, w_send, w_recv, b_send, b_recv, r_send, r_recv):
    me = lax.axis_index("dom")
    staged = [(dual_in, dual), (primal_in, primal), (recon_in, recon.at[pl.ds(0, CHILD * DOF), :]), (traction_in, traction), (trace_in, trace),
              (load_in, load), (size_in, cell_size), (stiffness_in, stiffness), (cell_in, face_cell),
              (other_in, face_other), (dir_in, face_dir), (hanging_in, hanging), (send_in, send_v)]
    loads = {}
    for i, (source, to) in enumerate(staged):
        loads[i] = pltpu.make_async_copy(source, to, in_sem.at[i])
        loads[i].start()

    barrier = pltpu.get_barrier_semaphore()
    partners = [behind(me, shift) for shift in SHIFTS]
    for stride, size in STAGES:
        partners += [in_stage(me, stride, size, step) for step in range(1, size)]
    for partner in partners:
        pl.semaphore_signal(barrier, inc=1, device_id=(partner,), device_id_type=MESH)

    start, live = counts_of(counts, me)
    head = lax.rem(CHILD - lax.rem(start, CHILD), CHILD)

    def remote(source, to, send_sem, recv_sem, target):
        return pltpu.make_async_remote_copy(src_ref=source, dst_ref=to, send_sem=send_sem, recv_sem=recv_sem,
                                            device_id=(target,), device_id_type=MESH)

    def list_copy(source, to, send_sem, recv_sem, k):
        return remote(source.at[k], to.at[k], send_sem.at[k], recv_sem.at[k], behind(me, shift_of(k)))

    loads[0].wait()

    def transpose_dual(step, carry):
        to_cell_major(d_t, dual, step)
        return carry

    lax.fori_loop(0, 8, transpose_dual, 0)
    first[...] = d_t[0:8, :]
    last[...] = d_t[pl.ds(jnp.maximum(live, 8) - 8, 8), :]
    pl.semaphore_wait(barrier, len(partners))
    edges = [remote(last, before, edge_send.at[0], edge_recv.at[0], behind(me, 1)),
             remote(first, after, edge_send.at[1], edge_recv.at[1], behind(me, -1))]
    for copy in edges:
        copy.start()

    def transpose_primal(step, carry):
        to_cell_major(p_t, primal, step)
        return carry

    loads[1].wait()
    lax.fori_loop(0, 8, transpose_primal, 0)

    def send_primal(step, carry):
        k = lax.rem(step + FIRST_LIST, NEIGH)
        gather_list(p_out, p_t, send, k)
        rows = pl.ds(pl.multiple_of(step * 96, 96), 96)
        recon_hi[rows, :], recon_lo[rows, :] = split(recon[rows, :])
        list_copy(p_out, p_in, p_send, p_recv, k).start()
        return carry

    loads[2].wait()
    lax.fori_loop(0, NEIGH, send_primal, 0)
    for copy in edges:
        copy.wait()
    rebuild(head, live, d_t, before, after, recon_hi, recon_lo, w_t, padded, families, rebuilt, after2)

    for i in range(3, len(staged)):
        loads[i].wait()
    fill_operator(operator, traction, trace)
    pair = (face_dir[...] // 2) * SLOTS
    index_a[...] = pair + face_cell[...]
    index_b[...] = pair + face_other[...]
    copy_a = pltpu.make_async_copy(index_a, smem_a, index_sem.at[0])
    copy_b = pltpu.make_async_copy(index_b, smem_b, index_sem.at[1])
    copy_a.start()
    copy_b.start()
    def send_weight(step, carry):
        k = lax.rem(step + FIRST_LIST, NEIGH)
        at = pl.multiple_of(step * 256, 256)
        gather_list(w_out, w_t, send, k)
        fill_table(table, at, p_t.at[pl.ds(at, 256), :], w_t.at[pl.ds(at, 256), :], operator)
        cell_terms(term, primal, load, w_t, cell_size, stiffness, step)
        list_copy(w_out, w_in, w_send, w_recv, k).start()
        return carry

    lax.fori_loop(0, NEIGH, send_weight, 0)
    copy_a.wait()
    copy_b.wait()

    def take_ghosts(step, carry):
        k = lax.rem(step + FIRST_LIST, NEIGH)
        list_copy(p_out, p_in, p_send, p_recv, k).wait()
        list_copy(w_out, w_in, w_send, w_recv, k).wait()
        row = step * 6
        gather_rows(side_a, row * LANES, table, lambda i: smem_a[row + i // LANES, i % LANES], 256)
        fill_table(table, CELLS + k * GHOST, p_in.at[k], w_in.at[k], operator)

        def rest(r, carry):
            gather_rows(side_a, r * LANES, table, lambda i: smem_a[r, i], LANES)
            return carry

        lax.fori_loop(row + 2, row + 6, rest, 0)
        return carry

    lax.fori_loop(0, NEIGH, take_ghosts, 0)

    lane = lax.broadcasted_iota(I32, (8, 2 * LANES), 1) % LANES
    sub = lax.broadcasted_iota(I32, (8, 2 * LANES), 0)
    pick = jnp.where(lane // 32 == sub, 1.0, 0.0).astype(BF16)
    upper = lax.broadcasted_iota(I32, (CHUNK, LANES), 1) % 64 >= 32

    def gather_b(to, c):
        gather_rows(to, 0, table, lambda i: smem_b[c * SPLIT + i // LANES, i % LANES], CHUNK)

    def raw_sums(side_b, c):
        a = side_a[pl.ds(pl.multiple_of(c * CHUNK, CHUNK), CHUNK), :]
        b = pltpu.roll(side_b[...], 64, 1)
        jump = pltpu.roll(a + b, 32, 1)
        hi, lo = split(jnp.where(upper, jump * a, pltpu.roll(jump * b, 96, 1)))
        return dot_nt(pick, jnp.concatenate([hi, lo], 1))

    def add_sums(raw, c, carry):
        sum_a, sum_b = carry
        face = c * CHUNK + lax.broadcasted_iota(I32, (1, CHUNK), 1)
        area = jnp.where(face < 3 * live, 0.5 * (1.0 - 0.75 * lanes_of(hanging, c).astype(F32)), 0.0)
        is_even = lanes_of(face_dir, c) % 2 == 0
        term_a = area * jnp.where(is_even, raw[1:2], raw[3:4])
        term_b = area * jnp.where(is_even, raw[0:1], raw[2:3])
        sum_a += scatter(lanes_of(face_cell, c), term_a, CELLS // LANES)
        sum_b += scatter(lanes_of(face_other, c), term_b, SLOTS // LANES)
        return sum_a, sum_b

    def body(i, carry):
        raw_before, sums = carry
        gather_b(side_b1, 2 * i + 1)
        raw = raw_sums(side_b0, 2 * i)
        sums = add_sums(raw_before, jnp.maximum(2 * i - 1, 0), sums)
        gather_b(side_b0, jnp.minimum(2 * i + 2, CHUNKS - 1))
        raw_after = raw_sums(side_b1, 2 * i + 1)
        sums = add_sums(raw, 2 * i, sums)
        return raw_after, sums

    gather_b(side_b0, 0)
    zero = (jnp.zeros((CELLS // LANES, LANES), F32), jnp.zeros((SLOTS // LANES, LANES), F32))
    raw, sums = lax.fori_loop(0, CHUNKS // 2, body, (jnp.zeros((8, CHUNK), F32), zero))
    sum_a, sum_b = add_sums(raw, CHUNKS - 1, sums)
    backs = []
    for k in range(NEIGH):
        at = CELLS // LANES + 2 * k
        partial[k, 0:2, :] = sum_b[at : at + 2]
        backs.append(remote(partial.at[k], returned.at[k], b_send.at[k], b_recv.at[k], behind(me, -SHIFTS[k])))
        backs[-1].start()
    for copy in backs:
        copy.wait()
    index = jnp.concatenate([send_v[k : k + 1, :] for k in range(NEIGH)], 1)
    value = jnp.concatenate([returned[k, r : r + 1, :] for k in range(NEIGH) for r in range(2)], 1)
    out = term[...] + sum_a + sum_b[: CELLS // LANES] + scatter(index, value, CELLS // LANES)
    slot = lax.broadcasted_iota(I32, out.shape, 0) * LANES + lax.broadcasted_iota(I32, out.shape, 1)
    indicator[...] = out

    size = jnp.where(slot < live, jnp.abs(out), 0.0)
    total = size[0:8] + size[8:16]
    place = 0
    for stage, (stride, count) in enumerate(STAGES):
        part[stage] = total
        copies = []
        for step in range(1, count):
            copies.append(remote(part.at[stage], parts.at[place + step - 1], r_send.at[place + step - 1],
                                 r_recv.at[place + step - 1], in_stage(me, stride, count, step)))
            copies[-1].start()
        for step in range(1, count):
            copies[step - 1].wait()
            total += parts[place + step - 1]
        place += count - 1

    def all_cells(i, carry):
        return carry + counts[i]

    cells = lax.fori_loop(0, RANKS, all_cells, jnp.int32(0), unroll=8)
    mean = jnp.sum(total) / cells.astype(F32)
    facts[...] = jnp.where(slot < live, mean, -1.0)


SMEM = pl.BlockSpec(memory_space=pltpu.SMEM)
VMEM = pl.BlockSpec(memory_space=pltpu.VMEM)
ANY = pl.BlockSpec(memory_space=pl.ANY)


def per_device(primal, dual, load, cell_size, cell_count, ghost_send, face_cell, face_other, face_dir, hanging,
               stiffness, recon, traction, trace):
    send = ghost_send[0]
    as_rows = lambda x: x.reshape(-1, LANES)
    f32 = lambda *shape: pltpu.VMEM(shape, F32)
    i32 = lambda *shape: pltpu.VMEM(shape, I32)
    dma = lambda n: pltpu.SemaphoreType.DMA((n,))
    rows = FACES // LANES
    cells = CELLS // LANES
    steps = sum(size - 1 for _, size in STAGES)
    scratch = [
        f32(DOF, CELLS), f32(DOF, CELLS), f32(DOF, CELLS), f32(cells, LANES), i32(NEIGH, GHOST),
        i32(rows, LANES), i32(rows, LANES), i32(rows, LANES), i32(rows, LANES),
        f32(DOF, DOF), f32(768, CHILD * DOF), f32(6 * FACE_DOF, DOF), f32(6 * FACE_DOF, DOF),
        f32(CELLS, LANES), f32(CELLS, LANES), f32(CELLS, LANES),
        f32(8, LANES), f32(8, LANES), f32(8, LANES), f32(8, LANES), f32(16, LANES),
        f32(NEIGH, GHOST, LANES), f32(NEIGH, GHOST, LANES), f32(NEIGH, GHOST, LANES), f32(NEIGH, GHOST, LANES),
        f32(FAMILIES * CHILD + 8, LANES), f32(FAMILIES, 768), f32(FAMILIES, 768),
        f32(384, 256), f32(3 * SLOTS, LANES), f32(FACES, LANES), f32(CHUNK, LANES), f32(CHUNK, LANES),
        pltpu.VMEM((768, CHILD * DOF), BF16), pltpu.VMEM((768, CHILD * DOF), BF16),
        i32(rows, LANES), i32(rows, LANES), pltpu.SMEM((rows, LANES), I32), pltpu.SMEM((rows, LANES), I32),
        f32(cells, LANES), f32(NEIGH, 8, LANES), f32(NEIGH, 8, LANES), f32(len(STAGES), 8, LANES), f32(steps, 8, LANES),
        dma(13), dma(2), dma(2), dma(2), dma(NEIGH), dma(NEIGH), dma(NEIGH), dma(NEIGH), dma(NEIGH), dma(NEIGH),
        dma(steps), dma(steps),
    ]
    indicator, facts = pl.pallas_call(
        kernel,
        out_shape=[jax.ShapeDtypeStruct((cells, LANES), F32)] * 2,
        in_specs=[SMEM] * 2 + [ANY] * 13, out_specs=[VMEM] * 2, scratch_shapes=scratch,
        compiler_params=pltpu.CompilerParams(collective_id=0, has_side_effects=True,
                                             vmem_limit_bytes=56 * 1024 * 1024),
        name="indicators",
    )(cell_count, send, primal, dual, load, as_rows(cell_size), send, as_rows(face_cell), as_rows(face_other),
      as_rows(face_dir), as_rows(hanging), stiffness, recon, traction, trace)
    facts = facts.reshape(-1)
    indicator = jnp.where(facts < 0.0, 0.0, indicator.reshape(-1))
    return indicator, jnp.abs(indicator) / (jnp.abs(facts) + 1e-06)

def solution(mesh):
    in_specs = (P(None, "dom"), P(None, "dom"), P(None, "dom"), P("dom"), P(), P("dom", None, None), P("dom"), P("dom"),
                P("dom"), P("dom"), P(), P(), P(), P())
    return jax.shard_map(per_device, mesh=mesh, in_specs=in_specs, out_specs=(P("dom"), P("dom")), check_vma=False)
```

```python
import functools

import jax
import jax.numpy as jnp
from jax import lax
from jax.experimental import pallas as pl
from jax.experimental.pallas import tpu as pltpu
from jax.sharding import PartitionSpec as P

F32 = jnp.float32
BF16 = jnp.bfloat16
I32 = jnp.int32

DOF = 81
FACE_DOF = 27
CHILD = 8
CELLS = 2048
NEIGH = 8
GHOST = 256
GHOSTS = NEIGH * GHOST
SLOTS = CELLS + GHOSTS
FACES = 6144
LANES = 128
BATCH = 16
FAMILIES = 264
CHUNK = 256
CHUNKS = FACES // CHUNK
SPLIT = CHUNK // LANES


def split(x):
    high = x.astype(BF16)
    return high, (x - high.astype(F32)).astype(BF16)


def dot_nt(a, b):
    return lax.dot_general(a, b, (((1,), (1,)), ((), ())), preferred_element_type=F32)


def dot_nn(a, b):
    return lax.dot_general(a, b, (((1,), (0,)), ((), ())), preferred_element_type=F32)


def gather_rows(dst, dst_at, src, index_of, count):
    src = src.reshape(src.shape[0], 1, LANES)
    for base in range(0, count, BATCH):
        rows = [src[index_of(base + u)] for u in range(BATCH)]
        for u in range(BATCH):
            dst[pl.ds(dst_at + (base + u), 1), :] = rows[u]


def turned_block(src, at):
    return jnp.concatenate([src[:, pl.ds(at, 256)], jnp.zeros((LANES - DOF, 256), F32)], 0).T


def to_cell_major(dst, src, step):
    at = pl.multiple_of(step * 256, 256)
    dst[pl.ds(at, 256), :] = turned_block(src, at)


def fill_operator(operator, traction, trace):
    operator[...] = jnp.zeros(operator.shape, F32)
    for d in range(6):
        rows = slice(d * FACE_DOF, (d + 1) * FACE_DOF)
        operator[64 * d : 64 * d + FACE_DOF, 0:DOF] = traction[rows, :]
        operator[64 * d + 32 : 64 * d + 32 + FACE_DOF, LANES : LANES + DOF] = trace[rows, :]


def fill_table(table, slot, p_rows, w_rows, operator):
    o_hi, o_lo = split(operator[...])
    x_hi, x_lo = split(jnp.concatenate([p_rows[...], w_rows[...]], 1))
    out = dot_nt(x_hi, o_hi) + dot_nt(x_lo, o_hi) + dot_nt(x_hi, o_lo)
    for pair in range(3):
        table[pl.ds(pl.multiple_of(pair * SLOTS + slot, 256), 256), :] = out[:, pair * LANES : (pair + 1) * LANES]


def cell_terms(out, primal, load, w_t, cell_size, stiffness, step):
    at = pl.multiple_of(step * 256, 256)
    s_hi, s_lo = split(stiffness[...])
    p_hi, p_lo = split(primal[:, pl.ds(at, 256)])
    residual = load[:, pl.ds(at, 256)] - (dot_nn(s_hi, p_hi) + dot_nn(s_lo, p_hi) + dot_nn(s_hi, p_lo))
    weight = w_t[pl.ds(at, 256), :].T[:DOF, :]
    total = jnp.sum(residual * weight, axis=0, keepdims=True)
    for r in range(2):
        i = step * 2 + r
        out[pl.ds(i, 1), :] = cell_size[pl.ds(i, 1), :] * total[:, r * LANES : (r + 1) * LANES]


def lanes_of(ref, chunk):
    return jnp.concatenate([ref[pl.ds(chunk * SPLIT + i, 1), :] for i in range(SPLIT)], 1)


def scatter(index, value, high_count):
    width = index.shape[1]
    high = index >> 7
    low = index & 127
    chosen = lax.broadcasted_iota(I32, (high_count, width), 0) == high
    v_hi, v_lo = split(jnp.where(chosen, value, 0.0))
    onehot = jnp.where(lax.broadcasted_iota(I32, (LANES, width), 0) == low, 1.0, 0.0).astype(BF16)
    both = dot_nt(jnp.concatenate([v_hi, v_lo], 0), onehot)
    return both[:high_count] + both[high_count:]


MESH = pl.DeviceIdType.MESH
RANKS = 128
SHIFTS = [(1 << which // 2) * (1 - 2 * (which % 2)) for which in range(NEIGH)]
FIRST_LIST = 4
STAGES = ((1, 8), (8, 16))


def counts_of(counts, me):
    def body(i, carry):
        before, here = carry
        c = counts[i]
        return before + jnp.where(i < me, c, 0), here + jnp.where(i == me, c, 0)

    return lax.fori_loop(0, RANKS, body, (jnp.int32(0), jnp.int32(0)), unroll=8)


def behind(me, by):
    return lax.rem(me + (by + RANKS), RANKS)


def shift_of(k):
    e = k // 2
    power = 1 + e + e * (e - 1) // 2 + e * (e - 1) * (e - 2) // 6
    return power * (1 - 2 * (k % 2))


def in_stage(me, stride, size, step):
    place = lax.rem(me // stride, size)
    return me + (lax.rem(place + step, size) - place) * stride


def gather_list(ghosts, source, send, k):
    gather_rows(ghosts.at[k], 0, source, lambda i: send[k, i], GHOST)


def rebuild(head, live, d_t, before, after, recon_hi, recon_lo, w_t, padded, families, rebuilt, after2):
    after2[0:8, :] = after[...]
    after2[8:16, :] = after[...]
    turned = after2[pl.ds(8 - live % 8, 8), :]
    row = lax.broadcasted_iota(I32, (8, LANES), 0)
    padded[0:8, :] = before[...]

    def fill(i, carry):
        at = pl.multiple_of(i * 8, 8)
        own = d_t[pl.ds(at, 8), :]
        padded[pl.ds(at + 8, 8), :] = jnp.where(row + at < live, own, turned)
        return carry

    lax.fori_loop(0, CELLS // 8, fill, 0, unroll=8)
    padded[CELLS + 8 : CELLS + 16, :] = turned
    padded[CELLS + 16 :, :] = jnp.zeros((padded.shape[0] - CELLS - 16, LANES), F32)
    for m in range(CHILD):
        families[:, m * DOF : (m + 1) * DOF] = padded[pl.ds(head + m, FAMILIES, stride=CHILD), :][:, :DOF]
    f_hi, f_lo = split(families[:, : CHILD * DOF])
    r_hi = recon_hi[0 : CHILD * DOF, :]
    rebuilt[:, : CHILD * DOF] = dot_nt(f_hi, r_hi) + dot_nt(f_lo, r_hi) + dot_nt(f_hi, recon_lo[0 : CHILD * DOF, :])
    lane = lax.broadcasted_iota(I32, (FAMILIES, LANES), 1)
    for m in range(CHILD):
        part = rebuilt[:, m * DOF : m * DOF + LANES]
        padded[pl.ds(m, FAMILIES, stride=CHILD), :] = jnp.where(lane < DOF, part, 0.0)

    def cut(i, carry):
        at = pl.multiple_of(i * 8, 8)
        w_t[pl.ds(at, 8), :] = jnp.where(row + at < live, padded[pl.ds(at + 8 - head, 8), :], 0.0)
        return carry

    lax.fori_loop(0, CELLS // 8, cut, 0, unroll=8)


def kernel(counts, send, primal_in, dual_in, load_in, size_in, send_in, cell_in, other_in, dir_in, hanging_in,
           stiffness_in, recon_in, traction_in, trace_in,
           indicator, facts,
           primal, dual, load, cell_size, send_v, face_cell, face_other, face_dir, hanging, stiffness, recon, traction,
           trace, p_t, d_t, w_t, first, last, before, after, after2, p_out, p_in, w_out, w_in, padded, families, rebuilt,
           operator, table, side_a, side_b0, side_b1, recon_hi, recon_lo, index_a, index_b, smem_a, smem_b, term, partial, returned, part, parts,
           in_sem, index_sem, edge_send, edge_recv, p_send, p_recv, w_send, w_recv, b_send, b_recv, r_send, r_recv):
    me = lax.axis_index("dom")
    staged = [(dual_in, dual), (primal_in, primal), (recon_in, recon.at[pl.ds(0, CHILD * DOF), :]), (traction_in, traction), (trace_in, trace),
              (load_in, load), (size_in, cell_size), (stiffness_in, stiffness), (cell_in, face_cell),
              (other_in, face_other), (dir_in, face_dir), (hanging_in, hanging), (send_in, send_v)]
    loads = {}
    for i, (source, to) in enumerate(staged):
        loads[i] = pltpu.make_async_copy(source, to, in_sem.at[i])
        loads[i].start()

    barrier = pltpu.get_barrier_semaphore()
    partners = [behind(me, shift) for shift in SHIFTS]
    for stride, size in STAGES:
        partners += [in_stage(me, stride, size, step) for step in range(1, size)]
    for partner in partners:
        pl.semaphore_signal(barrier, inc=1, device_id=(partner,), device_id_type=MESH)

    start, live = counts_of(counts, me)
    head = lax.rem(CHILD - lax.rem(start, CHILD), CHILD)

    def remote(source, to, send_sem, recv_sem, target):
        return pltpu.make_async_remote_copy(src_ref=source, dst_ref=to, send_sem=send_sem, recv_sem=recv_sem,
                                            device_id=(target,), device_id_type=MESH)

    def list_copy(source, to, send_sem, recv_sem, k):
        return remote(source.at[k], to.at[k], send_sem.at[k], recv_sem.at[k], behind(me, shift_of(k)))

    loads[0].wait()

    def transpose_dual(step, carry):
        to_cell_major(d_t, dual, step)
        return carry

    lax.fori_loop(0, 8, transpose_dual, 0)
    first[...] = d_t[0:8, :]
    last[...] = d_t[pl.ds(jnp.maximum(live, 8) - 8, 8), :]
    pl.semaphore_wait(barrier, len(partners))
    edges = [remote(last, before, edge_send.at[0], edge_recv.at[0], behind(me, 1)),
             remote(first, after, edge_send.at[1], edge_recv.at[1], behind(me, -1))]
    for copy in edges:
        copy.start()

    def transpose_primal(step, carry):
        to_cell_major(p_t, primal, step)
        return carry

    loads[1].wait()
    lax.fori_loop(0, 8, transpose_primal, 0)

    def send_primal(step, carry):
        k = lax.rem(step + FIRST_LIST, NEIGH)
        gather_list(p_out, p_t, send, k)
        rows = pl.ds(pl.multiple_of(step * 96, 96), 96)
        recon_hi[rows, :], recon_lo[rows, :] = split(recon[rows, :])
        list_copy(p_out, p_in, p_send, p_recv, k).start()
        return carry

    loads[2].wait()
    lax.fori_loop(0, NEIGH, send_primal, 0)
    for copy in edges:
        copy.wait()
    rebuild(head, live, d_t, before, after, recon_hi, recon_lo, w_t, padded, families, rebuilt, after2)

    for i in range(3, len(staged)):
        loads[i].wait()
    fill_operator(operator, traction, trace)
    pair = (face_dir[...] // 2) * SLOTS
    index_a[...] = pair + face_cell[...]
    index_b[...] = pair + face_other[...]
    copy_a = pltpu.make_async_copy(index_a, smem_a, index_sem.at[0])
    copy_b = pltpu.make_async_copy(index_b, smem_b, index_sem.at[1])
    copy_a.start()
    copy_b.start()

    def send_weight(step, carry):
        k = lax.rem(step + FIRST_LIST, NEIGH)
        at = pl.multiple_of(step * 256, 256)
        gather_list(w_out, w_t, send, k)
        fill_table(table, at, p_t.at[pl.ds(at, 256), :], w_t.at[pl.ds(at, 256), :], operator)
        cell_terms(term, primal, load, w_t, cell_size, stiffness, step)
        list_copy(w_out, w_in, w_send, w_recv, k).start()
        return carry

    lax.fori_loop(0, NEIGH, send_weight, 0)
    copy_a.wait()
    copy_b.wait()

    def take_ghosts(step, carry):
        k = lax.rem(step + FIRST_LIST, NEIGH)
        list_copy(p_out, p_in, p_send, p_recv, k).wait()
        list_copy(w_out, w_in, w_send, w_recv, k).wait()
        row = step * 6
        gather_rows(side_a, row * LANES, table, lambda i: smem_a[row + i // LANES, i % LANES], 256)
        fill_table(table, CELLS + k * GHOST, p_in.at[k], w_in.at[k], operator)

        def rest(r, carry):
            gather_rows(side_a, r * LANES, table, lambda i: smem_a[r, i], LANES)
            return carry

        lax.fori_loop(row + 2, row + 6, rest, 0)
        return carry

    lax.fori_loop(0, NEIGH, take_ghosts, 0)

    lane = lax.broadcasted_iota(I32, (8, 2 * LANES), 1) % LANES
    sub = lax.broadcasted_iota(I32, (8, 2 * LANES), 0)
    pick = jnp.where(lane // 32 == sub, 1.0, 0.0).astype(BF16)
    upper = lax.broadcasted_iota(I32, (CHUNK, LANES), 1) % 64 >= 32

    def gather_b(to, c):
        gather_rows(to, 0, table, lambda i: smem_b[c * SPLIT + i // LANES, i % LANES], CHUNK)

    def raw_sums(side_b, c):
        a = side_a[pl.ds(pl.multiple_of(c * CHUNK, CHUNK), CHUNK), :]
        b = pltpu.roll(side_b[...], 64, 1)
        jump = pltpu.roll(a + b, 32, 1)
        hi, lo = split(jnp.where(upper, jump * a, pltpu.roll(jump * b, 96, 1)))
        return dot_nt(pick, jnp.concatenate([hi, lo], 1))

    def add_sums(raw, c, carry):
        sum_a, sum_b = carry
        face = c * CHUNK + lax.broadcasted_iota(I32, (1, CHUNK), 1)
        area = jnp.where(face < 3 * live, 0.5 * (1.0 - 0.75 * lanes_of(hanging, c).astype(F32)), 0.0)
        is_even = lanes_of(face_dir, c) % 2 == 0
        term_a = area * jnp.where(is_even, raw[1:2], raw[3:4])
        term_b = area * jnp.where(is_even, raw[0:1], raw[2:3])
        sum_a += scatter(lanes_of(face_cell, c), term_a, CELLS // LANES)
        sum_b += scatter(lanes_of(face_other, c), term_b, SLOTS // LANES)
        return sum_a, sum_b

    def body(i, carry):
        raw_before, sums = carry
        gather_b(side_b1, 2 * i + 1)
        raw = raw_sums(side_b0, 2 * i)
        sums = add_sums(raw_before, jnp.maximum(2 * i - 1, 0), sums)
        gather_b(side_b0, jnp.minimum(2 * i + 2, CHUNKS - 1))
        raw_after = raw_sums(side_b1, 2 * i + 1)
        sums = add_sums(raw, 2 * i, sums)
        return raw_after, sums

    gather_b(side_b0, 0)
    zero = (jnp.zeros((CELLS // LANES, LANES), F32), jnp.zeros((SLOTS // LANES, LANES), F32))
    raw, sums = lax.fori_loop(0, CHUNKS // 2, body, (jnp.zeros((8, CHUNK), F32), zero))
    sum_a, sum_b = add_sums(raw, CHUNKS - 1, sums)
    backs = []
    for k in range(NEIGH):
        at = CELLS // LANES + 2 * k
        partial[k, 0:2, :] = sum_b[at : at + 2]
        backs.append(remote(partial.at[k], returned.at[k], b_send.at[k], b_recv.at[k], behind(me, -SHIFTS[k])))
        backs[-1].start()
    for copy in backs:
        copy.wait()
    index = jnp.concatenate([send_v[k : k + 1, :] for k in range(NEIGH)], 1)
    value = jnp.concatenate([returned[k, r : r + 1, :] for k in range(NEIGH) for r in range(2)], 1)
    out = term[...] + sum_a + sum_b[: CELLS // LANES] + scatter(index, value, CELLS // LANES)
    slot = lax.broadcasted_iota(I32, out.shape, 0) * LANES + lax.broadcasted_iota(I32, out.shape, 1)
    indicator[...] = out

    size = jnp.where(slot < live, jnp.abs(out), 0.0)
    total = size[0:8] + size[8:16]
    place = 0
    for stage, (stride, count) in enumerate(STAGES):
        part[stage] = total
        copies = []
        for step in range(1, count):
            copies.append(remote(part.at[stage], parts.at[place + step - 1], r_send.at[place + step - 1],
                                 r_recv.at[place + step - 1], in_stage(me, stride, count, step)))
            copies[-1].start()
        for step in range(1, count):
            copies[step - 1].wait()
            total += parts[place + step - 1]
        place += count - 1

    def all_cells(i, carry):
        return carry + counts[i]

    cells = lax.fori_loop(0, RANKS, all_cells, jnp.int32(0), unroll=8)
    mean = jnp.sum(total) / cells.astype(F32)
    facts[...] = jnp.where(slot < live, mean, -1.0)


SMEM = pl.BlockSpec(memory_space=pltpu.SMEM)
VMEM = pl.BlockSpec(memory_space=pltpu.VMEM)
ANY = pl.BlockSpec(memory_space=pl.ANY)


def per_device(primal, dual, load, cell_size, cell_count, ghost_send, face_cell, face_other, face_dir, hanging,
               stiffness, recon, traction, trace):
    send = ghost_send[0]
    as_rows = lambda x: x.reshape(-1, LANES)
    f32 = lambda *shape: pltpu.VMEM(shape, F32)
    i32 = lambda *shape: pltpu.VMEM(shape, I32)
    dma = lambda n: pltpu.SemaphoreType.DMA((n,))
    rows = FACES // LANES
    cells = CELLS // LANES
    steps = sum(size - 1 for _, size in STAGES)
    scratch = [
        f32(DOF, CELLS), f32(DOF, CELLS), f32(DOF, CELLS), f32(cells, LANES), i32(NEIGH, GHOST),
        i32(rows, LANES), i32(rows, LANES), i32(rows, LANES), i32(rows, LANES),
        f32(DOF, DOF), f32(768, CHILD * DOF), f32(6 * FACE_DOF, DOF), f32(6 * FACE_DOF, DOF),
        f32(CELLS, LANES), f32(CELLS, LANES), f32(CELLS, LANES),
        f32(8, LANES), f32(8, LANES), f32(8, LANES), f32(8, LANES), f32(16, LANES),
        f32(NEIGH, GHOST, LANES), f32(NEIGH, GHOST, LANES), f32(NEIGH, GHOST, LANES), f32(NEIGH, GHOST, LANES),
        f32(FAMILIES * CHILD + 8, LANES), f32(FAMILIES, 768), f32(FAMILIES, 768),
        f32(384, 256), f32(3 * SLOTS, LANES), f32(FACES, LANES), f32(CHUNK, LANES), f32(CHUNK, LANES),
        pltpu.VMEM((768, CHILD * DOF), BF16), pltpu.VMEM((768, CHILD * DOF), BF16),
        i32(rows, LANES), i32(rows, LANES), pltpu.SMEM((rows, LANES), I32), pltpu.SMEM((rows, LANES), I32),
        f32(cells, LANES), f32(NEIGH, 8, LANES), f32(NEIGH, 8, LANES), f32(len(STAGES), 8, LANES), f32(steps, 8, LANES),
        dma(13), dma(2), dma(2), dma(2), dma(NEIGH), dma(NEIGH), dma(NEIGH), dma(NEIGH), dma(NEIGH), dma(NEIGH),
        dma(steps), dma(steps),
    ]
    indicator, facts = pl.pallas_call(
        kernel,
        out_shape=[jax.ShapeDtypeStruct((cells, LANES), F32)] * 2,
        in_specs=[SMEM] * 2 + [ANY] * 13, out_specs=[VMEM] * 2, scratch_shapes=scratch,
        compiler_params=pltpu.CompilerParams(collective_id=0, has_side_effects=True,
                                             vmem_limit_bytes=56 * 1024 * 1024),
        name="indicators",
    )(cell_count, send, primal, dual, load, as_rows(cell_size), send, as_rows(face_cell), as_rows(face_other),
      as_rows(face_dir), as_rows(hanging), stiffness, recon, traction, trace)
    facts = facts.reshape(-1)
    indicator = jnp.where(facts < 0.0, 0.0, indicator.reshape(-1))
    return indicator, jnp.abs(indicator) / (jnp.abs(facts) + 1e-06)

def solution(mesh):
    in_specs = (P(None, "dom"), P(None, "dom"), P(None, "dom"), P("dom"), P(), P("dom", None, None), P("dom"), P("dom"),
                P("dom"), P("dom"), P(), P(), P(), P())
    return jax.shard_map(per_device, mesh=mesh, in_specs=in_specs, out_specs=(P("dom"), P("dom")), check_vma=False)
```

```python
import functools

import jax
import jax.numpy as jnp
from jax import lax
from jax.experimental import pallas as pl
from jax.experimental.pallas import tpu as pltpu
from jax.sharding import PartitionSpec as P

F32 = jnp.float32
BF16 = jnp.bfloat16
I32 = jnp.int32

DOF = 81
FACE_DOF = 27
CHILD = 8
CELLS = 2048
NEIGH = 8
GHOST = 256
GHOSTS = NEIGH * GHOST
SLOTS = CELLS + GHOSTS
FACES = 6144
LANES = 128
BATCH = 16
FAMILIES = 272
THIRD = 88
PACKED = 2 * THIRD
CHUNK = 256
CHUNKS = FACES // CHUNK
SPLIT = CHUNK // LANES


def split(x):
    high = x.astype(BF16)
    return high, (x - high.astype(F32)).astype(BF16)


def dot_nt(a, b):
    return lax.dot_general(a, b, (((1,), (1,)), ((), ())), preferred_element_type=F32)


def dot_nn(a, b):
    return lax.dot_general(a, b, (((1,), (0,)), ((), ())), preferred_element_type=F32)


def gather_rows(dst, dst_at, src, index_of, count):
    for base in range(0, count, BATCH):
        rows = [src[pl.ds(index_of(base + u), 1), :] for u in range(BATCH)]
        for u in range(BATCH):
            dst[pl.ds(dst_at + (base + u), 1), :] = rows[u]


def turned_block(src, at):
    return jnp.concatenate([src[:, pl.ds(at, 256)], jnp.zeros((LANES - DOF, 256), F32)], 0).T


def to_cell_major(dst, src, step):
    at = pl.multiple_of(step * 256, 256)
    dst[pl.ds(at, 256), :] = turned_block(src, at)


def pack(to, rows):
    lane = lax.broadcasted_iota(I32, (THIRD, LANES), 1)
    second = pltpu.roll(rows[THIRD : 2 * THIRD, :], DOF, 1)
    third = pltpu.roll(rows[2 * THIRD :, :], 2 * DOF - LANES, 1)
    upper = jnp.where(lane < DOF, rows[0:THIRD, :], second)
    to[...] = jnp.concatenate([upper, jnp.where(lane < 2 * DOF - LANES, second, third)], 0)


def unpack(rows):
    lane = lax.broadcasted_iota(I32, (THIRD, LANES), 1)
    upper, lower = rows[:THIRD], rows[THIRD:]
    second = pltpu.roll(jnp.where(lane < 2 * DOF - LANES, lower, upper), LANES - DOF, 1)
    third = pltpu.roll(lower, 2 * LANES - 2 * DOF, 1)
    return jnp.concatenate([upper, second, third[: GHOST - PACKED]], 0)


def fill_operator(operator, traction, trace):
    operator[...] = jnp.zeros(operator.shape, F32)
    for d in range(6):
        rows = slice(d * FACE_DOF, (d + 1) * FACE_DOF)
        operator[64 * d : 64 * d + FACE_DOF, 0:DOF] = traction[rows, :]
        operator[64 * d + 32 : 64 * d + 32 + FACE_DOF, LANES : LANES + DOF] = trace[rows, :]


def fill_table(table, slot, p_rows, w_rows, operator):
    o_hi, o_lo = split(operator[...])
    x_hi, x_lo = split(jnp.concatenate([p_rows, w_rows], 1))
    out = dot_nt(x_hi, o_hi) + dot_nt(x_lo, o_hi) + dot_nt(x_hi, o_lo)
    for pair in range(3):
        table[pl.ds(pl.multiple_of(pair * SLOTS + slot, 256), 256), :] = out[:, pair * LANES : (pair + 1) * LANES]


def take_residual(load, primal, stiffness, step):
    cells = pl.ds(pl.multiple_of(step * 256, 256), 256)
    s_hi, s_lo = split(stiffness[...])
    p_hi, p_lo = split(primal[:, cells])
    load[:, cells] = load[:, cells] - (dot_nn(s_hi, p_hi) + dot_nn(s_lo, p_hi) + dot_nn(s_hi, p_lo))


def cell_terms(out, residual, w_t, cell_size, step):
    cells = pl.ds(pl.multiple_of(step * 256, 256), 256)
    total = jnp.sum(residual[:, cells] * w_t[cells, :].T[:DOF, :], axis=0, keepdims=True)
    for r in range(2):
        i = step * 2 + r
        out[pl.ds(i, 1), :] = cell_size[pl.ds(i, 1), :] * total[:, r * LANES : (r + 1) * LANES]


def lanes_of(ref, chunk):
    return jnp.concatenate([ref[pl.ds(chunk * SPLIT + i, 1), :] for i in range(SPLIT)], 1)


def scatter(index, value, high_count):
    width = index.shape[1]
    high = index >> 7
    low = index & 127
    chosen = lax.broadcasted_iota(I32, (high_count, width), 0) == high
    v_hi, v_lo = split(jnp.where(chosen, value, 0.0))
    onehot = jnp.where(lax.broadcasted_iota(I32, (LANES, width), 0) == low, 1.0, 0.0).astype(BF16)
    both = dot_nt(jnp.concatenate([v_hi, v_lo], 0), onehot)
    return both[:high_count] + both[high_count:]


MESH = pl.DeviceIdType.MESH
RANKS = 128
SHIFTS = [(1 << which // 2) * (1 - 2 * (which % 2)) for which in range(NEIGH)]
FIRST_LIST = 4
STAGES = ((1, 8), (8, 16))


def counts_of(counts, me):
    def body(i, carry):
        before, here = carry
        c = counts[i]
        return before + jnp.where(i < me, c, 0), here + jnp.where(i == me, c, 0)

    return lax.fori_loop(0, RANKS, body, (jnp.int32(0), jnp.int32(0)), unroll=8)


def behind(me, by):
    return lax.rem(me + (by + RANKS), RANKS)


def shift_of(k):
    e = k // 2
    power = 1 + e + e * (e - 1) // 2 + e * (e - 1) * (e - 2) // 6
    return power * (1 - 2 * (k % 2))


def in_stage(me, stride, size, step):
    place = lax.rem(me // stride, size)
    return me + (lax.rem(place + step, size) - place) * stride


def gather_list(picked, source, send, k):
    gather_rows(picked, 0, source, lambda i: send[k, i], GHOST)


def rebuild(head, live, d_t, before, after, recon_hi, recon_lo, w_t, padded, families, rebuilt, after2):
    after2[0:8, :] = after[...]
    after2[8:16, :] = after[...]
    turned = after2[pl.ds(8 - live % 8, 8), :]
    row = lax.broadcasted_iota(I32, (8, LANES), 0)
    padded[0:8, :] = before[...]

    def fill(i, carry):
        at = pl.multiple_of(i * 8, 8)
        own = d_t[pl.ds(at, 8), :]
        padded[pl.ds(at + 8, 8), :] = jnp.where(row + at < live, own, turned)
        return carry

    lax.fori_loop(0, CELLS // 8, fill, 0, unroll=8)
    padded[CELLS + 8 : CELLS + 16, :] = turned
    padded[CELLS + 16 :, :] = jnp.zeros((padded.shape[0] - CELLS - 16, LANES), F32)
    for m in range(CHILD):
        families[:, m * DOF : (m + 1) * DOF] = padded[pl.ds(head + m, FAMILIES, stride=CHILD), :][:, :DOF]
    f_hi, f_lo = split(families[:, : CHILD * DOF])
    r_hi = recon_hi[0 : CHILD * DOF, :]
    both = dot_nt(jnp.concatenate([f_hi, f_lo], 0), r_hi)
    rebuilt[:, : CHILD * DOF] = both[:FAMILIES] + both[FAMILIES:] + dot_nt(f_hi, recon_lo[0 : CHILD * DOF, :])
    lane = lax.broadcasted_iota(I32, (FAMILIES, LANES), 1)
    for m in range(CHILD):
        part = rebuilt[:, m * DOF : m * DOF + LANES]
        padded[pl.ds(m, FAMILIES, stride=CHILD), :] = jnp.where(lane < DOF, part, 0.0)

    def cut(i, carry):
        at = pl.multiple_of(i * 8, 8)
        w_t[pl.ds(at, 8), :] = jnp.where(row + at < live, padded[pl.ds(at + 8 - head, 8), :], 0.0)
        return carry

    lax.fori_loop(0, CELLS // 8, cut, 0, unroll=8)


def kernel(counts, send, primal_in, dual_in, load_in, size_in, send_in, cell_in, other_in, dir_in, hanging_in,
           stiffness_in, recon_in, traction_in, trace_in,
           indicator, facts,
           primal, dual, load, cell_size, send_v, face_cell, face_other, face_dir, hanging, stiffness, recon, traction,
           trace, p_t, d_t, w_t, first, last, before, after, after2, p_out, p_in, w_out, w_in, picked, padded, families, rebuilt,
           operator, table, side_a, side_b0, side_b1, recon_hi, recon_lo, index_a, index_b, smem_a, smem_b, term, partial, returned, part, parts,
           in_sem, index_sem, edge_send, edge_recv, p_send, p_recv, w_send, w_recv, b_send, b_recv, r_send, r_recv):
    me = lax.axis_index("dom")
    staged = [(primal_in, primal), (recon_in, recon.at[pl.ds(0, CHILD * DOF), :]), (dual_in, dual), (traction_in, traction), (trace_in, trace),
              (load_in, load), (size_in, cell_size), (stiffness_in, stiffness), (cell_in, face_cell),
              (other_in, face_other), (dir_in, face_dir), (hanging_in, hanging), (send_in, send_v)]
    loads = {}
    for i, (source, to) in enumerate(staged):
        loads[i] = pltpu.make_async_copy(source, to, in_sem.at[i])
        loads[i].start()

    barrier = pltpu.get_barrier_semaphore()
    partners = [behind(me, shift) for shift in SHIFTS]
    for stride, size in STAGES:
        partners += [in_stage(me, stride, size, step) for step in range(1, size)]
    for partner in partners:
        pl.semaphore_signal(barrier, inc=1, device_id=(partner,), device_id_type=MESH)

    start, live = counts_of(counts, me)
    head = lax.rem(CHILD - lax.rem(start, CHILD), CHILD)

    def remote(source, to, send_sem, recv_sem, target):
        return pltpu.make_async_remote_copy(src_ref=source, dst_ref=to, send_sem=send_sem, recv_sem=recv_sem,
                                            device_id=(target,), device_id_type=MESH)

    def list_copy(source, to, send_sem, recv_sem, k):
        return remote(source.at[k], to.at[k], send_sem.at[k], recv_sem.at[k], behind(me, shift_of(k)))

    loads[0].wait()

    def transpose_primal(step, carry):
        to_cell_major(p_t, primal, step)
        rows = pl.ds(pl.multiple_of(step * 96, 96), 96)
        recon_hi[rows, :], recon_lo[rows, :] = split(recon[rows, :])
        return carry

    loads[1].wait()
    lax.fori_loop(0, 8, transpose_primal, 0)
    loads[2].wait()
    pl.semaphore_wait(barrier, len(partners))

    def send_primal(step, carry):
        k = lax.rem(step + FIRST_LIST, NEIGH)
        gather_list(picked, p_t, send, k)
        to_cell_major(d_t, dual, step)
        pack(p_out.at[k], picked)
        list_copy(p_out, p_in, p_send, p_recv, k).start()
        return carry

    lax.fori_loop(0, NEIGH, send_primal, 0)
    first[...] = d_t[0:8, :]
    last[...] = d_t[pl.ds(jnp.maximum(live, 8) - 8, 8), :]
    edges = [remote(last, before, edge_send.at[0], edge_recv.at[0], behind(me, 1)),
             remote(first, after, edge_send.at[1], edge_recv.at[1], behind(me, -1))]
    for copy in edges:
        copy.start()

    for i in range(3, len(staged)):
        loads[i].wait()
    fill_operator(operator, traction, trace)
    pair = (face_dir[...] // 2) * SLOTS
    index_a[...] = pair + face_cell[...]
    index_b[...] = pair + face_other[...]
    copy_a = pltpu.make_async_copy(index_a, smem_a, index_sem.at[0])
    copy_b = pltpu.make_async_copy(index_b, smem_b, index_sem.at[1])
    copy_a.start()
    copy_b.start()

    def residuals(step, carry):
        take_residual(load, primal, stiffness, step)
        return carry

    lax.fori_loop(0, 8, residuals, 0)
    for copy in edges:
        copy.wait()
    rebuild(head, live, d_t, before, after, recon_hi, recon_lo, w_t, padded, families, rebuilt, after2)

    def send_weight(step, carry):
        k = lax.rem(step + FIRST_LIST, NEIGH)
        at = pl.multiple_of(step * 256, 256)
        gather_list(picked, w_t, send, k)
        fill_table(table, at, p_t[pl.ds(at, 256), :], w_t[pl.ds(at, 256), :], operator)
        cell_terms(term, load, w_t, cell_size, step)
        pack(w_out.at[k], picked)
        list_copy(w_out, w_in, w_send, w_recv, k).start()
        return carry

    lax.fori_loop(0, NEIGH, send_weight, 0)
    copy_a.wait()
    copy_b.wait()

    def take_ghosts(step, carry):
        k = lax.rem(step + FIRST_LIST, NEIGH)
        list_copy(p_out, p_in, p_send, p_recv, k).wait()
        list_copy(w_out, w_in, w_send, w_recv, k).wait()
        row = step * 6
        gather_rows(side_a, row * LANES, table, lambda i: smem_a[row + i // LANES, i % LANES], 256)
        fill_table(table, CELLS + k * GHOST, unpack(p_in[k]), unpack(w_in[k]), operator)

        def rest(r, carry):
            gather_rows(side_a, r * LANES, table, lambda i: smem_a[r, i], LANES)
            return carry

        lax.fori_loop(row + 2, row + 6, rest, 0)
        return carry

    lax.fori_loop(0, NEIGH, take_ghosts, 0)

    lane = lax.broadcasted_iota(I32, (8, 2 * LANES), 1) % LANES
    sub = lax.broadcasted_iota(I32, (8, 2 * LANES), 0)
    pick = jnp.where(lane // 32 == sub, 1.0, 0.0).astype(BF16)
    upper = lax.broadcasted_iota(I32, (CHUNK, LANES), 1) % 64 >= 32

    def gather_b(to, c):
        gather_rows(to, 0, table, lambda i: smem_b[c * SPLIT + i // LANES, i % LANES], CHUNK)

    def raw_sums(side_b, c):
        a = side_a[pl.ds(pl.multiple_of(c * CHUNK, CHUNK), CHUNK), :]
        b = pltpu.roll(side_b[...], 64, 1)
        jump = pltpu.roll(a + b, 32, 1)
        hi, lo = split(jnp.where(upper, jump * a, pltpu.roll(jump * b, 96, 1)))
        return dot_nt(pick, jnp.concatenate([hi, lo], 1))

    def add_sums(raw, c, carry):
        sum_a, sum_b = carry
        face = c * CHUNK + lax.broadcasted_iota(I32, (1, CHUNK), 1)
        area = jnp.where(face < 3 * live, 0.5 * (1.0 - 0.75 * lanes_of(hanging, c).astype(F32)), 0.0)
        is_even = lanes_of(face_dir, c) % 2 == 0
        term_a = area * jnp.where(is_even, raw[1:2], raw[3:4])
        term_b = area * jnp.where(is_even, raw[0:1], raw[2:3])
        sum_a += scatter(lanes_of(face_cell, c), term_a, CELLS // LANES)
        sum_b += scatter(lanes_of(face_other, c), term_b, SLOTS // LANES)
        return sum_a, sum_b

    def body(i, carry):
        raw_before, sums = carry
        gather_b(side_b1, 2 * i + 1)
        raw = raw_sums(side_b0, 2 * i)
        sums = add_sums(raw_before, jnp.maximum(2 * i - 1, 0), sums)
        gather_b(side_b0, jnp.minimum(2 * i + 2, CHUNKS - 1))
        raw_after = raw_sums(side_b1, 2 * i + 1)
        sums = add_sums(raw, 2 * i, sums)
        return raw_after, sums

    gather_b(side_b0, 0)
    zero = (jnp.zeros((CELLS // LANES, LANES), F32), jnp.zeros((SLOTS // LANES, LANES), F32))
    raw, sums = lax.fori_loop(0, CHUNKS // 2, body, (jnp.zeros((8, CHUNK), F32), zero))
    sum_a, sum_b = add_sums(raw, CHUNKS - 1, sums)
    backs = []
    for k in range(NEIGH):
        at = CELLS // LANES + 2 * k
        partial[k, 0:2, :] = sum_b[at : at + 2]
        backs.append(remote(partial.at[k], returned.at[k], b_send.at[k], b_recv.at[k], behind(me, -SHIFTS[k])))
        backs[-1].start()
    for copy in backs:
        copy.wait()
    index = jnp.concatenate([send_v[k : k + 1, :] for k in range(NEIGH)], 1)
    value = jnp.concatenate([returned[k, r : r + 1, :] for k in range(NEIGH) for r in range(2)], 1)
    out = term[...] + sum_a + sum_b[: CELLS // LANES] + scatter(index, value, CELLS // LANES)
    slot = lax.broadcasted_iota(I32, out.shape, 0) * LANES + lax.broadcasted_iota(I32, out.shape, 1)
    indicator[...] = out

    size = jnp.where(slot < live, jnp.abs(out), 0.0)
    total = size[0:8] + size[8:16]
    place = 0
    for stage, (stride, count) in enumerate(STAGES):
        part[stage] = total
        copies = []
        for step in range(1, count):
            copies.append(remote(part.at[stage], parts.at[place + step - 1], r_send.at[place + step - 1],
                                 r_recv.at[place + step - 1], in_stage(me, stride, count, step)))
            copies[-1].start()
        for step in range(1, count):
            copies[step - 1].wait()
            total += parts[place + step - 1]
        place += count - 1

    def all_cells(i, carry):
        return carry + counts[i]

    cells = lax.fori_loop(0, RANKS, all_cells, jnp.int32(0), unroll=8)
    mean = jnp.sum(total) / cells.astype(F32)
    facts[...] = jnp.where(slot < live, mean, -1.0)


SMEM = pl.BlockSpec(memory_space=pltpu.SMEM)
VMEM = pl.BlockSpec(memory_space=pltpu.VMEM)
ANY = pl.BlockSpec(memory_space=pl.ANY)


def per_device(primal, dual, load, cell_size, cell_count, ghost_send, face_cell, face_other, face_dir, hanging,
               stiffness, recon, traction, trace):
    send = ghost_send[0]
    as_rows = lambda x: x.reshape(-1, LANES)
    f32 = lambda *shape: pltpu.VMEM(shape, F32)
    i32 = lambda *shape: pltpu.VMEM(shape, I32)
    dma = lambda n: pltpu.SemaphoreType.DMA((n,))
    rows = FACES // LANES
    cells = CELLS // LANES
    steps = sum(size - 1 for _, size in STAGES)
    scratch = [
        f32(DOF, CELLS), f32(DOF, CELLS), f32(DOF, CELLS), f32(cells, LANES), i32(NEIGH, GHOST),
        i32(rows, LANES), i32(rows, LANES), i32(rows, LANES), i32(rows, LANES),
        f32(DOF, DOF), f32(768, CHILD * DOF), f32(6 * FACE_DOF, DOF), f32(6 * FACE_DOF, DOF),
        f32(CELLS, LANES), f32(CELLS, LANES), f32(CELLS, LANES),
        f32(8, LANES), f32(8, LANES), f32(8, LANES), f32(8, LANES), f32(16, LANES),
        f32(NEIGH, PACKED, LANES), f32(NEIGH, PACKED, LANES), f32(NEIGH, PACKED, LANES), f32(NEIGH, PACKED, LANES),
        f32(3 * THIRD, LANES),
        f32(FAMILIES * CHILD + 8, LANES), f32(FAMILIES, 768), f32(FAMILIES, 768),
        f32(384, 256), f32(3 * SLOTS, LANES), f32(FACES, LANES), f32(CHUNK, LANES), f32(CHUNK, LANES),
        pltpu.VMEM((768, CHILD * DOF), BF16), pltpu.VMEM((768, CHILD * DOF), BF16),
        i32(rows, LANES), i32(rows, LANES), pltpu.SMEM((rows, LANES), I32), pltpu.SMEM((rows, LANES), I32),
        f32(cells, LANES), f32(NEIGH, 8, LANES), f32(NEIGH, 8, LANES), f32(len(STAGES), 8, LANES), f32(steps, 8, LANES),
        dma(13), dma(2), dma(2), dma(2), dma(NEIGH), dma(NEIGH), dma(NEIGH), dma(NEIGH), dma(NEIGH), dma(NEIGH),
        dma(steps), dma(steps),
    ]
    indicator, facts = pl.pallas_call(
        kernel,
        out_shape=[jax.ShapeDtypeStruct((cells, LANES), F32)] * 2,
        in_specs=[SMEM] * 2 + [ANY] * 13, out_specs=[VMEM] * 2, scratch_shapes=scratch,
        compiler_params=pltpu.CompilerParams(collective_id=0, has_side_effects=True,
                                             vmem_limit_bytes=56 * 1024 * 1024),
        name="indicators",
    )(cell_count, send, primal, dual, load, as_rows(cell_size), send, as_rows(face_cell), as_rows(face_other),
      as_rows(face_dir), as_rows(hanging), stiffness, recon, traction, trace)
    facts = facts.reshape(-1)
    indicator = jnp.where(facts < 0.0, 0.0, indicator.reshape(-1))
    return indicator, jnp.abs(indicator) / (jnp.abs(facts) + 1e-06)

def solution(mesh):
    in_specs = (P(None, "dom"), P(None, "dom"), P(None, "dom"), P("dom"), P(), P("dom", None, None), P("dom"), P("dom"),
                P("dom"), P("dom"), P(), P(), P(), P())
    return jax.shard_map(per_device, mesh=mesh, in_specs=in_specs, out_specs=(P("dom"), P("dom")), check_vma=False)
```

```python
import functools

import jax
import jax.numpy as jnp
from jax import lax
from jax.experimental import pallas as pl
from jax.experimental.pallas import tpu as pltpu
from jax.sharding import PartitionSpec as P

F32 = jnp.float32
BF16 = jnp.bfloat16
I32 = jnp.int32

DOF = 81
FACE_DOF = 27
CHILD = 8
CELLS = 2048
NEIGH = 8
GHOST = 256
GHOSTS = NEIGH * GHOST
SLOTS = CELLS + GHOSTS
FACES = 6144
LANES = 128
LAG = 16
FAMILIES = 272
THIRD = 88
PACKED = 2 * THIRD
CHUNK = 256
CHUNKS = FACES // CHUNK
SPLIT = CHUNK // LANES


def split(x):
    high = x.astype(BF16)
    return high, (x - high.astype(F32)).astype(BF16)


def dot_nt(a, b):
    return lax.dot_general(a, b, (((1,), (1,)), ((), ())), preferred_element_type=F32)


def dot_nn(a, b):
    return lax.dot_general(a, b, (((1,), (0,)), ((), ())), preferred_element_type=F32)


def gather_rows(dst, dst_at, src, index_of, count):
    held = []
    for i in range(count + LAG):
        if i < count:
            held.append(src[pl.ds(index_of(i), 1), :])
        if i >= LAG:
            dst[pl.ds(dst_at + (i - LAG), 1), :] = held[i - LAG]


def turned_block(src, at):
    return jnp.concatenate([src[:, pl.ds(at, 256)], jnp.zeros((LANES - DOF, 256), F32)], 0).T


def to_cell_major(dst, row, src, step):
    at = pl.multiple_of(step * 256, 256)
    dst[pl.ds(pl.multiple_of(row + at, CHILD), 256), :] = turned_block(src, at)


def pack(to, rows):
    lane = lax.broadcasted_iota(I32, (THIRD, LANES), 1)
    second = pltpu.roll(rows[THIRD : 2 * THIRD, :], DOF, 1)
    third = pltpu.roll(rows[2 * THIRD :, :], 2 * DOF - LANES, 1)
    upper = jnp.where(lane < DOF, rows[0:THIRD, :], second)
    to[...] = jnp.concatenate([upper, jnp.where(lane < 2 * DOF - LANES, second, third)], 0)


def unpack(rows):
    lane = lax.broadcasted_iota(I32, (THIRD, LANES), 1)
    upper, lower = rows[:THIRD], rows[THIRD:]
    second = pltpu.roll(jnp.where(lane < 2 * DOF - LANES, lower, upper), LANES - DOF, 1)
    third = pltpu.roll(lower, 2 * LANES - 2 * DOF, 1)
    return jnp.concatenate([upper, second, third[: GHOST - PACKED]], 0)


def fill_operator(operator, traction, trace):
    operator[...] = jnp.zeros(operator.shape, F32)
    for d in range(6):
        rows = slice(d * FACE_DOF, (d + 1) * FACE_DOF)
        operator[64 * d : 64 * d + FACE_DOF, 0:DOF] = traction[rows, :]
        operator[64 * d + 32 : 64 * d + 32 + FACE_DOF, LANES : LANES + DOF] = trace[rows, :]


def fill_table(table, slot, p_rows, w_rows, operator):
    hi, lo = split(jnp.concatenate([p_rows, w_rows], 1))
    out = dot_nn(jnp.concatenate([hi, lo, hi], 1), operator[...])
    for pair in range(3):
        table[pl.ds(pl.multiple_of(pair * SLOTS + slot, 256), 256), :] = out[:, pair * LANES : (pair + 1) * LANES]


def take_residual(load, primal, stiffness, step):
    cells = pl.ds(pl.multiple_of(step * 256, 256), 256)
    s_hi, s_lo = split(stiffness[...])
    p_hi, p_lo = split(primal[:, cells])
    load[:, cells] = load[:, cells] - (dot_nn(s_hi, p_hi) + dot_nn(s_lo, p_hi) + dot_nn(s_hi, p_lo))


def cell_terms(out, residual, woven, skip, cell_size, step):
    cells = pl.ds(pl.multiple_of(step * 256, 256), 256)
    total = jnp.sum(residual[:, cells] * woven[pl.ds(skip + step * 256, 256), :].T[:DOF, :], axis=0, keepdims=True)
    for r in range(2):
        i = step * 2 + r
        out[pl.ds(i, 1), :] = cell_size[pl.ds(i, 1), :] * total[:, r * LANES : (r + 1) * LANES]


def lanes_of(ref, chunk):
    return jnp.concatenate([ref[pl.ds(chunk * SPLIT + i, 1), :] for i in range(SPLIT)], 1)


def low_onehot(index):
    low = lax.broadcasted_iota(I32, (LANES, index.shape[1]), 0) == index % LANES
    return jnp.where(low, 1.0, 0.0).astype(BF16)


def scatter(index, value, high_count, onehot):
    high = lax.broadcasted_iota(I32, (high_count, index.shape[1]), 0) == index // LANES
    both = dot_nt(jnp.concatenate(split(jnp.where(high, value, 0.0)), 0), onehot)
    return both[:high_count] + both[high_count:]


MESH = pl.DeviceIdType.MESH
RANKS = 128
SHIFTS = [(1 << which // 2) * (1 - 2 * (which % 2)) for which in range(NEIGH)]
FIRST_LIST = 4
STAGES = ((1, 8), (8, 16))


def counts_of(counts, me):
    def body(i, carry):
        before, here, cells = carry
        c = counts[i]
        return before + jnp.where(i < me, c, 0), here + jnp.where(i == me, c, 0), cells + c

    return lax.fori_loop(0, RANKS, body, (jnp.int32(0), jnp.int32(0), jnp.int32(0)), unroll=32)


def behind(me, by):
    return lax.rem(me + (by + RANKS), RANKS)


def shift_of(k):
    e = k // 2
    power = 1 + e + e * (e - 1) // 2 + e * (e - 1) * (e - 2) // 6
    return power * (1 - 2 * (k % 2))


def in_stage(me, stride, size, step):
    place = lax.rem(me // stride, size)
    return me + (lax.rem(place + step, size) - place) * stride


def gather_list(picked, source, send, k):
    gather_rows(picked, 0, source, lambda i: send[k, i], GHOST)


def rebuild(head, live, padded, after, after2, recon3, families, rebuilt, woven):
    after2[0:8, :] = jnp.zeros((8, LANES), F32)
    after2[8:16, :] = after[...]
    own = lax.rem(live - head + CHILD, CHILD)
    split_family = 1 + (live - head) // CHILD
    row = lax.broadcasted_iota(I32, (FAMILIES, LANES), 0)
    families[:, 640:768] = jnp.zeros((FAMILIES, LANES), F32)
    for m in range(CHILD):
        cells = padded[pl.ds(head + m, FAMILIES, stride=CHILD), :]
        late = after2[pl.ds(CHILD + m - own, 1), :]
        cells = jnp.where((row == split_family) & (m >= own), late, cells)
        families[:, m * DOF : (m + 1) * DOF] = cells[:, :DOF]
    hi, lo = split(families[...])
    rebuilt[:, : CHILD * DOF] = dot_nt(jnp.concatenate([hi, lo, hi], 1), recon3[0 : CHILD * DOF, :])
    lane = lax.broadcasted_iota(I32, (FAMILIES, LANES), 1)
    for m in range(CHILD):
        part = rebuilt[:, m * DOF : m * DOF + LANES]
        woven[pl.ds(m, FAMILIES, stride=CHILD), :] = jnp.where(lane < DOF, part, 0.0)


def kernel(counts, send, primal_in, dual_in, load_in, size_in, send_in, cell_in, other_in, dir_in, hanging_in,
           stiffness_in, recon_in, traction_in, trace_in,
           indicator, facts,
           primal, dual, load, cell_size, send_v, face_cell, face_other, face_dir, hanging, stiffness, recon, traction,
           trace, p_t, first, last, before, after, after2, p_out, p_in, w_out, w_in, picked, padded, woven, families, rebuilt,
           operator, operator3, table, side_a, side_b0, side_b1, recon3, onehot, index_a, index_b, smem_a, smem_b, term, partial, returned, part, parts,
           in_sem, index_sem, edge_send, edge_recv, p_send, p_recv, w_send, w_recv, b_send, b_recv, r_send, r_recv):
    me = lax.axis_index("dom")
    staged = [(primal_in, primal), (recon_in, recon.at[pl.ds(0, CHILD * DOF), :]), (dual_in, dual), (traction_in, traction), (trace_in, trace),
              (load_in, load), (size_in, cell_size), (stiffness_in, stiffness), (cell_in, face_cell),
              (other_in, face_other), (dir_in, face_dir), (hanging_in, hanging), (send_in, send_v)]
    loads = {}
    for i, (source, to) in enumerate(staged):
        loads[i] = pltpu.make_async_copy(source, to, in_sem.at[i])
        loads[i].start()

    barrier = pltpu.get_barrier_semaphore()
    partners = [behind(me, shift) for shift in SHIFTS]
    for stride, size in STAGES:
        partners += [in_stage(me, stride, size, step) for step in range(1, size)]
    for partner in partners:
        pl.semaphore_signal(barrier, inc=1, device_id=(partner,), device_id_type=MESH)

    start, live, cells = counts_of(counts, me)
    head = lax.rem(CHILD - lax.rem(start, CHILD), CHILD)

    def remote(source, to, send_sem, recv_sem, target):
        return pltpu.make_async_remote_copy(src_ref=source, dst_ref=to, send_sem=send_sem, recv_sem=recv_sem,
                                            device_id=(target,), device_id_type=MESH)

    def list_copy(source, to, send_sem, recv_sem, k):
        return remote(source.at[k], to.at[k], send_sem.at[k], recv_sem.at[k], behind(me, shift_of(k)))

    loads[0].wait()

    def transpose_primal(step, carry):
        to_cell_major(p_t, 0, primal, step)
        rows = pl.ds(pl.multiple_of(step * 96, 96), 96)
        wide = jnp.concatenate([recon[rows, :], jnp.zeros((96, 768 - CHILD * DOF), F32)], 1)
        hi, lo = split(wide)
        recon3[rows, 0:768] = hi
        recon3[rows, 768:1536] = hi
        recon3[rows, 1536:2304] = lo
        return carry

    loads[1].wait()
    lax.fori_loop(0, 8, transpose_primal, 0)
    loads[2].wait()
    pl.semaphore_wait(barrier, len(partners))

    def send_primal(step, carry):
        k = lax.rem(step + FIRST_LIST, NEIGH)
        gather_list(picked, p_t, send, k)
        to_cell_major(padded, CHILD, dual, step)
        pack(p_out.at[k], picked)
        list_copy(p_out, p_in, p_send, p_recv, k).start()
        return carry

    lax.fori_loop(0, NEIGH, send_primal, 0)
    first[...] = padded[8:16, :]
    last[...] = padded[pl.ds(jnp.maximum(live, 8), 8), :]
    padded[CELLS + 8 :, :] = jnp.zeros((padded.shape[0] - CELLS - 8, LANES), F32)
    edges = [remote(last, before, edge_send.at[0], edge_recv.at[0], behind(me, 1)),
             remote(first, after, edge_send.at[1], edge_recv.at[1], behind(me, -1))]
    for copy in edges:
        copy.start()

    for i in range(3, len(staged)):
        loads[i].wait()
    fill_operator(operator, traction, trace)
    hi, lo = split(operator[...].T)
    operator3[0:256, :] = hi
    operator3[256:512, :] = hi
    operator3[512:768, :] = lo
    pair = (face_dir[...] // 2) * SLOTS
    index_a[...] = pair + face_cell[...]
    index_b[...] = pair + face_other[...]
    copy_a = pltpu.make_async_copy(index_a, smem_a, index_sem.at[0])
    copy_b = pltpu.make_async_copy(index_b, smem_b, index_sem.at[1])
    copy_a.start()
    copy_b.start()

    def residuals(step, carry):
        take_residual(load, primal, stiffness, step)
        return carry

    lax.fori_loop(0, 8, residuals, 0)
    for k in range(NEIGH):
        onehot[:, k * GHOST : (k + 1) * GHOST] = low_onehot(send_v[k : k + 1, :])
    for copy in edges:
        copy.wait()
    padded[0:8, :] = before[...]
    rebuild(head, live, padded, after, after2, recon3, families, rebuilt, woven)

    def send_weight(step, carry):
        k = lax.rem(step + FIRST_LIST, NEIGH)
        at = pl.multiple_of(step * 256, 256)
        gather_rows(picked, 0, woven, lambda i: send[k, i] + (CHILD - head), GHOST)
        fill_table(table, at, p_t[pl.ds(at, 256), :], woven[pl.ds(CHILD - head + at, 256), :], operator3)
        cell_terms(term, load, woven, CHILD - head, cell_size, step)
        pack(w_out.at[k], picked)
        list_copy(w_out, w_in, w_send, w_recv, k).start()
        return carry

    lax.fori_loop(0, NEIGH, send_weight, 0)
    copy_a.wait()
    copy_b.wait()

    def take_ghosts(step, carry):
        k = lax.rem(step + FIRST_LIST, NEIGH)
        list_copy(p_out, p_in, p_send, p_recv, k).wait()
        list_copy(w_out, w_in, w_send, w_recv, k).wait()
        row = step * 6
        gather_rows(side_a, row * LANES, table, lambda i: smem_a[row + i // LANES, i % LANES], 256)
        fill_table(table, CELLS + k * GHOST, unpack(p_in[k]), unpack(w_in[k]), operator3)

        def rest(r, carry):
            gather_rows(side_a, r * LANES, table, lambda i: smem_a[r, i], LANES)
            return carry

        lax.fori_loop(row + 2, row + 6, rest, 0)
        return carry

    lax.fori_loop(0, NEIGH, take_ghosts, 0)

    lane = lax.broadcasted_iota(I32, (8, 2 * LANES), 1) % LANES
    sub = lax.broadcasted_iota(I32, (8, 2 * LANES), 0)
    pick = jnp.where(lane // 32 == sub, 1.0, 0.0).astype(BF16)
    upper = lax.broadcasted_iota(I32, (CHUNK, LANES), 1) % 64 >= 32

    def gather_b(to, c):
        gather_rows(to, 0, table, lambda i: smem_b[c * SPLIT + i // LANES, i % LANES], CHUNK)

    def raw_sums(side_b, c):
        a = side_a[pl.ds(pl.multiple_of(c * CHUNK, CHUNK), CHUNK), :]
        b = pltpu.roll(side_b[...], 64, 1)
        jump = pltpu.roll(a + b, 32, 1)
        hi, lo = split(jnp.where(upper, jump * a, pltpu.roll(jump * b, 96, 1)))
        return dot_nt(pick, jnp.concatenate([hi, lo], 1))

    def add_sums(raw, c, carry):
        sum_a, sum_b = carry
        face = c * CHUNK + lax.broadcasted_iota(I32, (1, CHUNK), 1)
        area = jnp.where(face < 3 * live, 0.5 * (1.0 - 0.75 * lanes_of(hanging, c).astype(F32)), 0.0)
        is_even = lanes_of(face_dir, c) % 2 == 0
        term_a = area * jnp.where(is_even, raw[1:2], raw[3:4])
        term_b = area * jnp.where(is_even, raw[0:1], raw[2:3])
        cell, other = lanes_of(face_cell, c), lanes_of(face_other, c)
        sum_a += scatter(cell, term_a, CELLS // LANES, low_onehot(cell))
        sum_b += scatter(other, term_b, SLOTS // LANES, low_onehot(other))
        return sum_a, sum_b

    def body(i, carry):
        raw_before, sums = carry
        gather_b(side_b1, 2 * i + 1)
        raw = raw_sums(side_b0, 2 * i)
        sums = add_sums(raw_before, jnp.maximum(2 * i - 1, 0), sums)
        gather_b(side_b0, jnp.minimum(2 * i + 2, CHUNKS - 1))
        raw_after = raw_sums(side_b1, 2 * i + 1)
        sums = add_sums(raw, 2 * i, sums)
        return raw_after, sums

    gather_b(side_b0, 0)
    zero = (jnp.zeros((CELLS // LANES, LANES), F32), jnp.zeros((SLOTS // LANES, LANES), F32))
    raw, sums = lax.fori_loop(0, CHUNKS // 2, body, (jnp.zeros((8, CHUNK), F32), zero))
    sum_a, sum_b = add_sums(raw, CHUNKS - 1, sums)
    for k in range(NEIGH):
        at = CELLS // LANES + 2 * k
        partial[k] = sum_b[at : at + 2]
    backs = [remote(partial.at[k], returned.at[k], b_send, b_recv, behind(me, -SHIFTS[k])) for k in range(NEIGH)]
    for copy in backs:
        copy.start()
    index = jnp.concatenate([send_v[k : k + 1, :] for k in range(NEIGH)], 1)
    out = term[...] + sum_a + sum_b[: CELLS // LANES]
    remote(partial, returned, b_send, b_recv, behind(me, 1)).wait_recv()
    value = jnp.concatenate([returned[k, r : r + 1, :] for k in range(NEIGH) for r in range(2)], 1)
    out = out + scatter(index, value, CELLS // LANES, onehot[...])
    slot = lax.broadcasted_iota(I32, out.shape, 0) * LANES + lax.broadcasted_iota(I32, out.shape, 1)
    indicator[...] = out

    total = jnp.sum(jnp.where(slot < live, jnp.abs(out), 0.0), axis=0, keepdims=True)
    place = 0
    for stage, (stride, count) in enumerate(STAGES):
        part[stage] = total
        slots = pl.ds(place, count - 1)
        for step in range(1, count):
            remote(part.at[stage], parts.at[place + step - 1], r_send.at[stage], r_recv.at[stage],
                   in_stage(me, stride, count, step)).start()
        remote(parts.at[slots], parts.at[slots], r_send.at[stage], r_recv.at[stage], behind(me, 1)).wait_recv()
        total = total + jnp.sum(parts[place : place + count - 1], axis=0)
        place += count - 1

    mean = jnp.sum(total) / cells.astype(F32)
    facts[...] = jnp.where(slot < live, mean, -1.0)
    remote(partial, returned, b_send, b_recv, behind(me, 1)).wait_send()
    place = 0
    for stage, (stride, count) in enumerate(STAGES):
        slots = pl.ds(place, count - 1)
        remote(parts.at[slots], parts.at[slots], r_send.at[stage], r_recv.at[stage], behind(me, 1)).wait_send()
        place += count - 1


SMEM = pl.BlockSpec(memory_space=pltpu.SMEM)
VMEM = pl.BlockSpec(memory_space=pltpu.VMEM)
ANY = pl.BlockSpec(memory_space=pl.ANY)


def per_device(primal, dual, load, cell_size, cell_count, ghost_send, face_cell, face_other, face_dir, hanging,
               stiffness, recon, traction, trace):
    send = ghost_send[0]
    as_rows = lambda x: x.reshape(-1, LANES)
    f32 = lambda *shape: pltpu.VMEM(shape, F32)
    bf16 = lambda *shape: pltpu.VMEM(shape, BF16)
    i32 = lambda *shape: pltpu.VMEM(shape, I32)
    dma = lambda n: pltpu.SemaphoreType.DMA((n,))
    rows = FACES // LANES
    cells = CELLS // LANES
    steps = sum(size - 1 for _, size in STAGES)
    scratch = [
        f32(DOF, CELLS), f32(DOF, CELLS), f32(DOF, CELLS), f32(cells, LANES), i32(NEIGH, GHOST),
        i32(rows, LANES), i32(rows, LANES), i32(rows, LANES), i32(rows, LANES),
        f32(DOF, DOF), f32(768, CHILD * DOF), f32(6 * FACE_DOF, DOF), f32(6 * FACE_DOF, DOF),
        f32(CELLS, LANES),
        f32(8, LANES), f32(8, LANES), f32(8, LANES), f32(8, LANES), f32(16, LANES),
        f32(NEIGH, PACKED, LANES), f32(NEIGH, PACKED, LANES), f32(NEIGH, PACKED, LANES), f32(NEIGH, PACKED, LANES),
        f32(3 * THIRD, LANES),
        f32(FAMILIES * CHILD + 8, LANES), f32(FAMILIES * CHILD, LANES), f32(FAMILIES, 768), f32(FAMILIES, 768),
        f32(384, 256), bf16(768, 384), f32(3 * SLOTS, LANES), f32(FACES, LANES), f32(CHUNK, LANES), f32(CHUNK, LANES),
        bf16(768, 2304), bf16(LANES, GHOSTS),
        i32(rows, LANES), i32(rows, LANES), pltpu.SMEM((rows, LANES), I32), pltpu.SMEM((rows, LANES), I32),
        f32(cells, LANES), f32(NEIGH, 2, LANES), f32(NEIGH, 2, LANES), f32(len(STAGES), 1, LANES), f32(steps, 1, LANES),
        dma(13), dma(2), dma(2), dma(2), dma(NEIGH), dma(NEIGH), dma(NEIGH), dma(NEIGH),
        pltpu.SemaphoreType.DMA, pltpu.SemaphoreType.DMA, dma(len(STAGES)), dma(len(STAGES)),
    ]
    indicator, facts = pl.pallas_call(
        kernel,
        out_shape=[jax.ShapeDtypeStruct((cells, LANES), F32)] * 2,
        in_specs=[SMEM] * 2 + [ANY] * 13, out_specs=[VMEM] * 2, scratch_shapes=scratch,
        compiler_params=pltpu.CompilerParams(collective_id=0, has_side_effects=True,
                                             vmem_limit_bytes=56 * 1024 * 1024),
        name="indicators",
    )(cell_count, send, primal, dual, load, as_rows(cell_size), send, as_rows(face_cell), as_rows(face_other),
      as_rows(face_dir), as_rows(hanging), stiffness, recon, traction, trace)
    facts = facts.reshape(-1)
    indicator = jnp.where(facts < 0.0, 0.0, indicator.reshape(-1))
    return indicator, jnp.abs(indicator) / (jnp.abs(facts) + 1e-06)

def solution(mesh):
    in_specs = (P(None, "dom"), P(None, "dom"), P(None, "dom"), P("dom"), P(), P("dom", None, None), P("dom"), P("dom"),
                P("dom"), P("dom"), P(), P(), P(), P())
    return jax.shard_map(per_device, mesh=mesh, in_specs=in_specs, out_specs=(P("dom"), P("dom")), check_vma=False)
```

```python
import functools

import jax
import jax.numpy as jnp
from jax import lax
from jax.experimental import pallas as pl
from jax.experimental.pallas import tpu as pltpu
from jax.sharding import PartitionSpec as P

F32 = jnp.float32
BF16 = jnp.bfloat16
I32 = jnp.int32

DOF = 81
FACE_DOF = 27
CHILD = 8
CELLS = 2048
NEIGH = 8
GHOST = 256
GHOSTS = NEIGH * GHOST
SLOTS = CELLS + GHOSTS
FACES = 6144
LANES = 128
BATCH = 16
FAMILIES = 272
THIRD = 96
PACKED = 2 * THIRD
CHUNK = 256
CHUNKS = FACES // CHUNK
SPLIT = CHUNK // LANES


def split(x):
    high = x.astype(BF16)
    return high, (x - high.astype(F32)).astype(BF16)


def dot_nt(a, b):
    return lax.dot_general(a, b, (((1,), (1,)), ((), ())), preferred_element_type=F32)


def dot_nn(a, b):
    return lax.dot_general(a, b, (((1,), (0,)), ((), ())), preferred_element_type=F32)


def gathers(dst, dst_at, src, index_of, count):
    def step(base):
        rows = [src[pl.ds(index_of(base + u), 1), :] for u in range(BATCH)]
        for u in range(BATCH):
            dst[pl.ds(dst_at + (base + u), 1), :] = rows[u]

    return [functools.partial(step, base) for base in range(0, count, BATCH)]


def together(*lists):
    spread = [((i + 0.5) / len(steps), n, step) for n, steps in enumerate(lists) for i, step in enumerate(steps)]
    for _, _, step in sorted(spread, key=lambda entry: entry[:2]):
        step()


def turns(dst, row, src, step):
    def turn(half):
        at = pl.multiple_of(step * 256 + half * LANES, LANES)
        block = jnp.concatenate([src[:, pl.ds(at, LANES)], jnp.zeros((LANES - DOF, LANES), F32)], 0)
        dst[pl.ds(pl.multiple_of(row + at, CHILD), LANES), :] = block.T

    return [functools.partial(turn, half) for half in range(2)]


def packs(to, rows):
    lane = lax.broadcasted_iota(I32, (16, LANES), 1)

    def step(at):
        second = pltpu.roll(rows[THIRD + at : THIRD + at + 16, :], DOF, 1)
        third = pltpu.roll(rows[2 * THIRD + at : 2 * THIRD + at + 16, :], 2 * DOF - LANES, 1)
        to[at : at + 16, :] = jnp.where(lane < DOF, rows[at : at + 16, :], second)
        to[THIRD + at : THIRD + at + 16, :] = jnp.where(lane < 2 * DOF - LANES, second, third)

    return [functools.partial(step, at) for at in range(0, THIRD, 16)]


def put_terms(x3, rows, lanes, value):
    hi, lo = split(value)
    x3[rows, lanes : lanes + LANES] = hi
    x3[rows, 256 + lanes : 256 + lanes + LANES] = lo
    x3[rows, 512 + lanes : 512 + lanes + LANES] = hi


def unpacks(x3, lanes, rows):
    lane = lax.broadcasted_iota(I32, (16, LANES), 1)

    def step(at):
        upper, lower = rows[at : at + 16, :], rows[THIRD + at : THIRD + at + 16, :]
        second = pltpu.roll(jnp.where(lane < 2 * DOF - LANES, lower, upper), LANES - DOF, 1)
        put_terms(x3, slice(at, at + 16), lanes, upper)
        put_terms(x3, slice(THIRD + at, THIRD + at + 16), lanes, second)
        if 2 * THIRD + at < GHOST:
            put_terms(x3, slice(2 * THIRD + at, 2 * THIRD + at + 16), lanes, pltpu.roll(lower, 2 * LANES - 2 * DOF, 1))

    return [functools.partial(step, at) for at in range(0, THIRD, 16)]


def term_steps(x3, lanes, src, at):
    def step(row):
        put_terms(x3, slice(row, row + 32), lanes, src[pl.ds(at + row, 32), :])

    return [functools.partial(step, row) for row in range(0, 256, 32)]


def fill_operator(operator, traction, trace):
    operator[...] = jnp.zeros(operator.shape, F32)
    for d in range(6):
        rows = slice(d * FACE_DOF, (d + 1) * FACE_DOF)
        operator[64 * d : 64 * d + FACE_DOF, 0:DOF] = traction[rows, :]
        operator[64 * d + 32 : 64 * d + 32 + FACE_DOF, LANES : LANES + DOF] = trace[rows, :]


def fill_table(table, slot, x3, operator):
    out = dot_nn(x3[...], operator[...])
    for pair in range(3):
        table[pl.ds(pl.multiple_of(pair * SLOTS + slot, 256), 256), :] = out[:, pair * LANES : (pair + 1) * LANES]


def take_residual(load, primal, stiffness, step):
    cells = pl.ds(pl.multiple_of(step * 256, 256), 256)
    s_hi, s_lo = split(stiffness[...])
    p_hi, p_lo = split(primal[:, cells])
    load[:, cells] = load[:, cells] - (dot_nn(s_hi, p_hi) + dot_nn(s_lo, p_hi) + dot_nn(s_hi, p_lo))


def cell_terms(out, residual, woven, skip, cell_size, step):
    def half_step(half):
        i = step * 2 + half
        at = pl.multiple_of(i * LANES, LANES)
        weight = woven[pl.ds(skip + at, LANES), :].T[:DOF, :]
        total = jnp.sum(residual[:, pl.ds(at, LANES)] * weight, axis=0, keepdims=True)
        out[pl.ds(i, 1), :] = cell_size[pl.ds(i, 1), :] * total

    return [functools.partial(half_step, half) for half in range(2)]


def lanes_of(ref, chunk):
    return jnp.concatenate([ref[pl.ds(chunk * SPLIT + i, 1), :] for i in range(SPLIT)], 1)


def low_onehot(index):
    low = lax.broadcasted_iota(I32, (LANES, index.shape[1]), 0) == index % LANES
    return jnp.where(low, 1.0, 0.0).astype(BF16)


def scatter(index, value, high_count, onehot):
    high = lax.broadcasted_iota(I32, (high_count, index.shape[1]), 0) == index // LANES
    both = dot_nt(jnp.concatenate(split(jnp.where(high, value, 0.0)), 0), onehot)
    return both[:high_count] + both[high_count:]


MESH = pl.DeviceIdType.MESH
RANKS = 128
SHIFTS = [(1 << which // 2) * (1 - 2 * (which % 2)) for which in range(NEIGH)]
FIRST_LIST = 4
STAGES = ((1, 8), (8, 16))


def counts_of(counts, me):
    def body(i, carry):
        before, here, cells = carry
        c = counts[i]
        return before + jnp.where(i < me, c, 0), here + jnp.where(i == me, c, 0), cells + c

    return lax.fori_loop(0, RANKS, body, (jnp.int32(0), jnp.int32(0), jnp.int32(0)), unroll=32)


def behind(me, by):
    return lax.rem(me + (by + RANKS), RANKS)


def shift_of(k):
    e = k // 2
    power = 1 + e + e * (e - 1) // 2 + e * (e - 1) * (e - 2) // 6
    return power * (1 - 2 * (k % 2))


def in_stage(me, stride, size, step):
    place = lax.rem(me // stride, size)
    return me + (lax.rem(place + step, size) - place) * stride


def rebuild(head, live, padded, after, after2, recon3, families, f3, rebuilt, woven):
    after2[0:8, :] = jnp.zeros((8, LANES), F32)
    after2[8:16, :] = after[...]
    own = lax.rem(live - head + CHILD, CHILD)
    split_family = 1 + (live - head) // CHILD
    for part in range(0, FAMILIES, 16):
        row = part + lax.broadcasted_iota(I32, (16, LANES), 0)
        rows = slice(part, part + 16)
        families[rows, 640:768] = jnp.zeros((16, LANES), F32)
        for m in range(CHILD):
            cells = padded[pl.ds(head + m + part * CHILD, 16, stride=CHILD), :]
            late = after2[pl.ds(CHILD + m - own, 1), :]
            cells = jnp.where((row == split_family) & (m >= own), late, cells)
            families[rows, m * DOF : (m + 1) * DOF] = cells[:, :DOF]
        hi, lo = split(families[rows, :])
        f3[rows, 0:768] = hi
        f3[rows, 768:1536] = lo
        f3[rows, 1536:2304] = hi
    for part in range(0, CHILD * DOF, 256):
        cols = slice(part, min(part + 256, CHILD * DOF))
        rebuilt[:, cols] = dot_nt(f3[...], recon3[cols, :])
    lane = lax.broadcasted_iota(I32, (16, LANES), 1)
    for part in range(0, FAMILIES, 16):
        for m in range(CHILD):
            value = rebuilt[part : part + 16, m * DOF : m * DOF + LANES]
            woven[pl.ds(m + part * CHILD, 16, stride=CHILD), :] = jnp.where(lane < DOF, value, 0.0)


def kernel(counts, send, primal_in, dual_in, load_in, size_in, send_in, cell_in, other_in, dir_in, hanging_in,
           stiffness_in, recon_in, traction_in, trace_in,
           indicator, facts,
           primal, dual, load, cell_size, send_v, face_cell, face_other, face_dir, hanging, stiffness, recon, traction,
           trace, p_t, first, last, before, after, after2, p_out, p_in, w_out, w_in, picked, packed, p_packed, padded, woven, families, f3, rebuilt, x3, mixed,
           operator, operator3, table, side_a, side_b0, side_b1, recon3, onehot, index_a, index_b, smem_a, smem_b, term, partial, returned, part, parts,
           in_sem, index_sem, edge_send, edge_recv, p_send, p_recv, w_send, w_recv, b_send, b_recv, r_send, r_recv):
    me = lax.axis_index("dom")
    staged = [(primal_in, primal), (recon_in, recon.at[pl.ds(0, CHILD * DOF), :]), (dual_in, dual), (traction_in, traction), (trace_in, trace),
              (load_in, load), (size_in, cell_size), (stiffness_in, stiffness), (cell_in, face_cell),
              (other_in, face_other), (dir_in, face_dir), (hanging_in, hanging), (send_in, send_v)]
    loads = {}
    for i, (source, to) in enumerate(staged):
        loads[i] = pltpu.make_async_copy(source, to, in_sem.at[i])
        loads[i].start()

    barrier = pltpu.get_barrier_semaphore()
    partners = [behind(me, shift) for shift in SHIFTS]
    for stride, size in STAGES:
        partners += [in_stage(me, stride, size, step) for step in range(1, size)]
    for partner in partners:
        pl.semaphore_signal(barrier, inc=1, device_id=(partner,), device_id_type=MESH)

    start, live, cells = counts_of(counts, me)
    head = lax.rem(CHILD - lax.rem(start, CHILD), CHILD)

    def remote(source, to, send_sem, recv_sem, target):
        return pltpu.make_async_remote_copy(src_ref=source, dst_ref=to, send_sem=send_sem, recv_sem=recv_sem,
                                            device_id=(target,), device_id_type=MESH)

    def list_copy(source, to, send_sem, recv_sem, k):
        return remote(source.at[k], to.at[k], send_sem.at[k], recv_sem.at[k], behind(me, shift_of(k)))

    loads[0].wait()

    def transpose_primal(step, carry):
        def recon_step(part):
            rows = pl.ds(pl.multiple_of(step * 96 + part * 16, 16), 16)
            hi, lo = split(jnp.concatenate([recon[rows, :], jnp.zeros((16, 768 - CHILD * DOF), F32)], 1))
            recon3[rows, 0:768] = hi
            recon3[rows, 768:1536] = hi
            recon3[rows, 1536:2304] = lo

        together(turns(p_t, 0, primal, step), [functools.partial(recon_step, part) for part in range(6)])
        return carry

    loads[1].wait()
    lax.fori_loop(0, 8, transpose_primal, 0)
    loads[2].wait()
    pl.semaphore_wait(barrier, len(partners))

    def send_primal(step, carry):
        k = lax.rem(step + FIRST_LIST, NEIGH)
        together(gathers(picked, 0, p_t, lambda i: send[k, i], GHOST), turns(padded, CHILD, dual, step))
        together(packs(packed, picked))
        p_out[k] = packed[...]
        list_copy(p_out, p_in, p_send, p_recv, k).start()
        return carry

    lax.fori_loop(0, NEIGH, send_primal, 0)
    first[...] = padded[8:16, :]
    last[...] = padded[pl.ds(jnp.maximum(live, 8), 8), :]
    padded[CELLS + 8 :, :] = jnp.zeros((padded.shape[0] - CELLS - 8, LANES), F32)
    edges = [remote(last, before, edge_send.at[0], edge_recv.at[0], behind(me, 1)),
             remote(first, after, edge_send.at[1], edge_recv.at[1], behind(me, -1))]
    for copy in edges:
        copy.start()

    for i in range(3, len(staged)):
        loads[i].wait()
    fill_operator(operator, traction, trace)
    hi, lo = split(operator[...].T)
    operator3[0:256, :] = hi
    operator3[256:512, :] = hi
    operator3[512:768, :] = lo
    pair = (face_dir[...] // 2) * SLOTS
    index_a[...] = pair + face_cell[...]
    index_b[...] = pair + face_other[...]
    copy_a = pltpu.make_async_copy(index_a, smem_a, index_sem.at[0])
    copy_b = pltpu.make_async_copy(index_b, smem_b, index_sem.at[1])
    copy_a.start()
    copy_b.start()

    def residuals(step, carry):
        take_residual(load, primal, stiffness, step)
        return carry

    lax.fori_loop(0, 8, residuals, 0)
    for k in range(NEIGH):
        onehot[:, k * GHOST : (k + 1) * GHOST] = low_onehot(send_v[k : k + 1, :])
    for copy in edges:
        copy.wait()
    padded[0:8, :] = before[...]
    rebuild(head, live, padded, after, after2, recon3, families, f3, rebuilt, woven)

    def send_weight(step, carry):
        k = lax.rem(step + FIRST_LIST, NEIGH)
        at = pl.multiple_of(step * 256, 256)
        skip = CHILD - head
        terms = term_steps(x3, 0, p_t, at) + term_steps(x3, LANES, woven, skip + at)
        table_step = functools.partial(fill_table, table, at, x3, operator3)
        together(gathers(picked, 0, woven, lambda i: send[k, i] + skip, GHOST),
                 terms + [table_step] + cell_terms(term, load, woven, skip, cell_size, step))
        together(packs(packed, picked))
        w_out[k] = packed[...]
        list_copy(w_out, w_in, w_send, w_recv, k).start()
        return carry

    lax.fori_loop(0, NEIGH, send_weight, 0)
    copy_a.wait()
    copy_b.wait()

    def take_ghosts(step, carry):
        k = lax.rem(step + FIRST_LIST, NEIGH)
        list_copy(p_out, p_in, p_send, p_recv, k).wait()
        list_copy(w_out, w_in, w_send, w_recv, k).wait()
        row = step * 6
        p_packed[...] = p_in[k]
        packed[...] = w_in[k]
        table_step = functools.partial(fill_table, table, CELLS + k * GHOST, x3, operator3)
        together(gathers(side_a, row * LANES, table, lambda i: smem_a[row + i // LANES, i % LANES], 256),
                 unpacks(x3, 0, p_packed) + unpacks(x3, LANES, packed))
        together(gathers(side_a, row * LANES + 256, table, lambda i: smem_a[row + 2 + i // LANES, i % LANES], 256))
        table_step()

        def rest(r, carry):
            together(gathers(side_a, r * LANES, table, lambda i: smem_a[r, i], LANES))
            return carry

        lax.fori_loop(row + 4, row + 6, rest, 0)
        return carry

    lax.fori_loop(0, NEIGH, take_ghosts, 0)

    lane = lax.broadcasted_iota(I32, (8, 2 * LANES), 1) % LANES
    sub = lax.broadcasted_iota(I32, (8, 2 * LANES), 0)
    pick = jnp.where(lane // 32 == sub, 1.0, 0.0).astype(BF16)
    upper = lax.broadcasted_iota(I32, (16, LANES), 1) % 64 >= 32

    def gather_b(to, c):
        return gathers(to, 0, table, lambda i: smem_b[c * SPLIT + i // LANES, i % LANES], CHUNK)

    def mix_steps(side_b, c):
        def step(row):
            a = side_a[pl.ds(pl.multiple_of(c * CHUNK + row, 16), 16), :]
            b = pltpu.roll(side_b[row : row + 16, :], 64, 1)
            jump = pltpu.roll(a + b, 32, 1)
            hi, lo = split(jnp.where(upper, jump * a, pltpu.roll(jump * b, 96, 1)))
            mixed[row : row + 16, :] = jnp.concatenate([hi, lo], 1)

        return [functools.partial(step, row) for row in range(0, CHUNK, 16)]

    def raw_sums():
        return dot_nt(pick, mixed[...])

    def add_sums(raw, c, carry):
        sum_a, sum_b = carry
        face = c * CHUNK + lax.broadcasted_iota(I32, (1, CHUNK), 1)
        area = jnp.where(face < 3 * live, 0.5 * (1.0 - 0.75 * lanes_of(hanging, c).astype(F32)), 0.0)
        is_even = lanes_of(face_dir, c) % 2 == 0
        term_a = area * jnp.where(is_even, raw[1:2], raw[3:4])
        term_b = area * jnp.where(is_even, raw[0:1], raw[2:3])
        cell, other = lanes_of(face_cell, c), lanes_of(face_other, c)
        sum_a += scatter(cell, term_a, CELLS // LANES, low_onehot(cell))
        sum_b += scatter(other, term_b, SLOTS // LANES, low_onehot(other))
        return sum_a, sum_b

    def body(i, carry):
        raw_before, sums = carry
        together(gather_b(side_b1, 2 * i + 1), mix_steps(side_b0, 2 * i))
        raw = raw_sums()
        sums = add_sums(raw_before, jnp.maximum(2 * i - 1, 0), sums)
        together(gather_b(side_b0, jnp.minimum(2 * i + 2, CHUNKS - 1)), mix_steps(side_b1, 2 * i + 1))
        raw_after = raw_sums()
        sums = add_sums(raw, 2 * i, sums)
        return raw_after, sums

    together(gather_b(side_b0, 0))
    zero = (jnp.zeros((CELLS // LANES, LANES), F32), jnp.zeros((SLOTS // LANES, LANES), F32))
    raw, sums = lax.fori_loop(0, CHUNKS // 2, body, (jnp.zeros((8, CHUNK), F32), zero))
    sum_a, sum_b = add_sums(raw, CHUNKS - 1, sums)
    for k in range(NEIGH):
        at = CELLS // LANES + 2 * k
        partial[k] = sum_b[at : at + 2]
    backs = [remote(partial.at[k], returned.at[k], b_send, b_recv, behind(me, -SHIFTS[k])) for k in range(NEIGH)]
    for copy in backs:
        copy.start()
    index = jnp.concatenate([send_v[k : k + 1, :] for k in range(NEIGH)], 1)
    out = term[...] + sum_a + sum_b[: CELLS // LANES]
    remote(partial, returned, b_send, b_recv, behind(me, 1)).wait_recv()
    value = jnp.concatenate([returned[k, r : r + 1, :] for k in range(NEIGH) for r in range(2)], 1)
    out = out + scatter(index, value, CELLS // LANES, onehot[...])
    slot = lax.broadcasted_iota(I32, out.shape, 0) * LANES + lax.broadcasted_iota(I32, out.shape, 1)
    indicator[...] = out

    total = jnp.sum(jnp.where(slot < live, jnp.abs(out), 0.0), axis=0, keepdims=True)
    place = 0
    for stage, (stride, count) in enumerate(STAGES):
        part[stage] = total
        slots = pl.ds(place, count - 1)
        for step in range(1, count):
            remote(part.at[stage], parts.at[place + step - 1], r_send.at[stage], r_recv.at[stage],
                   in_stage(me, stride, count, step)).start()
        remote(parts.at[slots], parts.at[slots], r_send.at[stage], r_recv.at[stage], behind(me, 1)).wait_recv()
        total = total + jnp.sum(parts[place : place + count - 1], axis=0)
        place += count - 1

    mean = jnp.sum(total) / cells.astype(F32)
    facts[...] = jnp.where(slot < live, mean, -1.0)
    remote(partial, returned, b_send, b_recv, behind(me, 1)).wait_send()
    place = 0
    for stage, (stride, count) in enumerate(STAGES):
        slots = pl.ds(place, count - 1)
        remote(parts.at[slots], parts.at[slots], r_send.at[stage], r_recv.at[stage], behind(me, 1)).wait_send()
        place += count - 1


SMEM = pl.BlockSpec(memory_space=pltpu.SMEM)
VMEM = pl.BlockSpec(memory_space=pltpu.VMEM)
ANY = pl.BlockSpec(memory_space=pl.ANY)


def per_device(primal, dual, load, cell_size, cell_count, ghost_send, face_cell, face_other, face_dir, hanging,
               stiffness, recon, traction, trace):
    send = ghost_send[0]
    as_rows = lambda x: x.reshape(-1, LANES)
    f32 = lambda *shape: pltpu.VMEM(shape, F32)
    bf16 = lambda *shape: pltpu.VMEM(shape, BF16)
    i32 = lambda *shape: pltpu.VMEM(shape, I32)
    dma = lambda n: pltpu.SemaphoreType.DMA((n,))
    rows = FACES // LANES
    cells = CELLS // LANES
    steps = sum(size - 1 for _, size in STAGES)
    scratch = [
        f32(DOF, CELLS), f32(DOF, CELLS), f32(DOF, CELLS), f32(cells, LANES), i32(NEIGH, GHOST),
        i32(rows, LANES), i32(rows, LANES), i32(rows, LANES), i32(rows, LANES),
        f32(DOF, DOF), f32(768, CHILD * DOF), f32(6 * FACE_DOF, DOF), f32(6 * FACE_DOF, DOF),
        f32(CELLS, LANES),
        f32(8, LANES), f32(8, LANES), f32(8, LANES), f32(8, LANES), f32(16, LANES),
        f32(NEIGH, PACKED, LANES), f32(NEIGH, PACKED, LANES), f32(NEIGH, PACKED, LANES), f32(NEIGH, PACKED, LANES),
        f32(3 * THIRD, LANES), f32(PACKED, LANES), f32(PACKED, LANES),
        f32(FAMILIES * CHILD + 8, LANES), f32(FAMILIES * CHILD, LANES), f32(FAMILIES, 768), bf16(FAMILIES, 2304), f32(FAMILIES, 768),
        bf16(256, 768), bf16(CHUNK, 2 * LANES),
        f32(384, 256), bf16(768, 384), f32(3 * SLOTS, LANES), f32(FACES, LANES), f32(CHUNK, LANES), f32(CHUNK, LANES),
        bf16(768, 2304), bf16(LANES, GHOSTS),
        i32(rows, LANES), i32(rows, LANES), pltpu.SMEM((rows, LANES), I32), pltpu.SMEM((rows, LANES), I32),
        f32(cells, LANES), f32(NEIGH, 2, LANES), f32(NEIGH, 2, LANES), f32(len(STAGES), 1, LANES), f32(steps, 1, LANES),
        dma(13), dma(2), dma(2), dma(2), dma(NEIGH), dma(NEIGH), dma(NEIGH), dma(NEIGH),
        pltpu.SemaphoreType.DMA, pltpu.SemaphoreType.DMA, dma(len(STAGES)), dma(len(STAGES)),
    ]
    indicator, facts = pl.pallas_call(
        kernel,
        out_shape=[jax.ShapeDtypeStruct((cells, LANES), F32)] * 2,
        in_specs=[SMEM] * 2 + [ANY] * 13, out_specs=[VMEM] * 2, scratch_shapes=scratch,
        compiler_params=pltpu.CompilerParams(collective_id=0, has_side_effects=True,
                                             vmem_limit_bytes=56 * 1024 * 1024),
        name="indicators",
    )(cell_count, send, primal, dual, load, as_rows(cell_size), send, as_rows(face_cell), as_rows(face_other),
      as_rows(face_dir), as_rows(hanging), stiffness, recon, traction, trace)
    facts = facts.reshape(-1)
    indicator = jnp.where(facts < 0.0, 0.0, indicator.reshape(-1))
    return indicator, jnp.abs(indicator) / (jnp.abs(facts) + 1e-06)

def solution(mesh):
    in_specs = (P(None, "dom"), P(None, "dom"), P(None, "dom"), P("dom"), P(), P("dom", None, None), P("dom"), P("dom"),
                P("dom"), P("dom"), P(), P(), P(), P())
    return jax.shard_map(per_device, mesh=mesh, in_specs=in_specs, out_specs=(P("dom"), P("dom")), check_vma=False)
```

```python
import functools

import jax
import jax.numpy as jnp
from jax import lax
from jax.experimental import pallas as pl
from jax.experimental.pallas import tpu as pltpu
from jax.sharding import PartitionSpec as P

F32 = jnp.float32
BF16 = jnp.bfloat16
I32 = jnp.int32

DOF = 81
FACE_DOF = 27
CHILD = 8
CELLS = 2048
NEIGH = 8
GHOST = 256
GHOSTS = NEIGH * GHOST
SLOTS = CELLS + GHOSTS
FACES = 6144
LANES = 128
FAMILIES = 272
THIRD = 88
PACKED = 2 * THIRD
CHUNK = 256
CHUNKS = FACES // CHUNK
SPLIT = CHUNK // LANES


def split(x):
    high = x.astype(BF16)
    return high, (x - high.astype(F32)).astype(BF16)


def dot_nt(a, b):
    return lax.dot_general(a, b, (((1,), (1,)), ((), ())), preferred_element_type=F32)


def dot_nn(a, b):
    return lax.dot_general(a, b, (((1,), (0,)), ((), ())), preferred_element_type=F32)


def gather_rows(dst, dst_at, src, index_of, count):
    sub = lax.broadcasted_iota(I32, (8, LANES), 0)
    for base in range(0, count, 8):
        rows = [src[pl.ds(index_of(base + u), 1), :] for u in range(8)]
        tile = jnp.broadcast_to(rows[0], (8, LANES))
        for u in range(1, 8):
            tile = jnp.where(sub == u, jnp.broadcast_to(rows[u], (8, LANES)), tile)
        dst[pl.ds(pl.multiple_of(dst_at + base, 8), 8), :] = tile


def turned_block(src, at):
    return jnp.concatenate([src[:, pl.ds(at, 256)], jnp.zeros((LANES - DOF, 256), F32)], 0).T


def to_cell_major(dst, row, src, step):
    at = pl.multiple_of(step * 256, 256)
    dst[pl.ds(pl.multiple_of(row + at, CHILD), 256), :] = turned_block(src, at)


def pack(to, rows):
    lane = lax.broadcasted_iota(I32, (THIRD, LANES), 1)
    second = pltpu.roll(rows[THIRD : 2 * THIRD, :], DOF, 1)
    third = pltpu.roll(rows[2 * THIRD :, :], 2 * DOF - LANES, 1)
    upper = jnp.where(lane < DOF, rows[0:THIRD, :], second)
    to[...] = jnp.concatenate([upper, jnp.where(lane < 2 * DOF - LANES, second, third)], 0)


def unpack(rows):
    lane = lax.broadcasted_iota(I32, (THIRD, LANES), 1)
    upper, lower = rows[:THIRD], rows[THIRD:]
    second = pltpu.roll(jnp.where(lane < 2 * DOF - LANES, lower, upper), LANES - DOF, 1)
    third = pltpu.roll(lower, 2 * LANES - 2 * DOF, 1)
    return jnp.concatenate([upper, second, third[: GHOST - PACKED]], 0)


def fill_operator(operator, traction, trace):
    operator[...] = jnp.zeros(operator.shape, F32)
    for d in range(6):
        rows = slice(d * FACE_DOF, (d + 1) * FACE_DOF)
        operator[64 * d : 64 * d + FACE_DOF, 0:DOF] = traction[rows, :]
        operator[64 * d + 32 : 64 * d + 32 + FACE_DOF, LANES : LANES + DOF] = trace[rows, :]


def fill_table(table, slot, p_rows, w_rows, operator):
    hi, lo = split(jnp.concatenate([p_rows, w_rows], 1))
    out = dot_nn(jnp.concatenate([hi, lo, hi], 1), operator[...])
    for pair in range(3):
        table[pl.ds(pl.multiple_of(pair * SLOTS + slot, 256), 256), :] = out[:, pair * LANES : (pair + 1) * LANES]


def take_residual(load, primal, stiffness, step):
    cells = pl.ds(pl.multiple_of(step * 256, 256), 256)
    s_hi, s_lo = split(stiffness[...])
    p_hi, p_lo = split(primal[:, cells])
    load[:, cells] = load[:, cells] - (dot_nn(s_hi, p_hi) + dot_nn(s_lo, p_hi) + dot_nn(s_hi, p_lo))


def cell_terms(out, residual, woven, skip, cell_size, step):
    cells = pl.ds(pl.multiple_of(step * 256, 256), 256)
    total = jnp.sum(residual[:, cells] * woven[pl.ds(skip + step * 256, 256), :].T[:DOF, :], axis=0, keepdims=True)
    for r in range(2):
        i = step * 2 + r
        out[pl.ds(i, 1), :] = cell_size[pl.ds(i, 1), :] * total[:, r * LANES : (r + 1) * LANES]


def lanes_of(ref, chunk):
    return jnp.concatenate([ref[pl.ds(chunk * SPLIT + i, 1), :] for i in range(SPLIT)], 1)


def low_onehot(index):
    low = lax.broadcasted_iota(I32, (LANES, index.shape[1]), 0) == index % LANES
    return jnp.where(low, 1.0, 0.0).astype(BF16)


def scatter(index, value, high_count, onehot):
    high = lax.broadcasted_iota(I32, (high_count, index.shape[1]), 0) == index // LANES
    both = dot_nt(jnp.concatenate(split(jnp.where(high, value, 0.0)), 0), onehot)
    return both[:high_count] + both[high_count:]


MESH = pl.DeviceIdType.MESH
RANKS = 128
SHIFTS = [(1 << which // 2) * (1 - 2 * (which % 2)) for which in range(NEIGH)]
FIRST_LIST = 4
STAGES = ((1, 8), (8, 16))


def counts_of(counts, me):
    def body(i, carry):
        before, here, cells = carry
        c = counts[i]
        return before + jnp.where(i < me, c, 0), here + jnp.where(i == me, c, 0), cells + c

    return lax.fori_loop(0, RANKS, body, (jnp.int32(0), jnp.int32(0), jnp.int32(0)), unroll=32)


def behind(me, by):
    return lax.rem(me + (by + RANKS), RANKS)


def shift_of(k):
    e = k // 2
    power = 1 + e + e * (e - 1) // 2 + e * (e - 1) * (e - 2) // 6
    return power * (1 - 2 * (k % 2))


def in_stage(me, stride, size, step):
    place = lax.rem(me // stride, size)
    return me + (lax.rem(place + step, size) - place) * stride


def gather_list(picked, source, send, k):
    gather_rows(picked, 0, source, lambda i: send[k, i], GHOST)


def rebuild(head, live, padded, after, after2, recon3, families, rebuilt, woven):
    after2[0:8, :] = jnp.zeros((8, LANES), F32)
    after2[8:16, :] = after[...]
    own = lax.rem(live - head + CHILD, CHILD)
    split_family = 1 + (live - head) // CHILD
    row = lax.broadcasted_iota(I32, (FAMILIES, LANES), 0)
    families[:, 640:768] = jnp.zeros((FAMILIES, LANES), F32)
    for m in range(CHILD):
        cells = padded[pl.ds(head + m, FAMILIES, stride=CHILD), :]
        late = after2[pl.ds(CHILD + m - own, 1), :]
        cells = jnp.where((row == split_family) & (m >= own), late, cells)
        families[:, m * DOF : (m + 1) * DOF] = cells[:, :DOF]
    hi, lo = split(families[...])
    rebuilt[:, : CHILD * DOF] = dot_nt(jnp.concatenate([hi, lo, hi], 1), recon3[0 : CHILD * DOF, :])
    lane = lax.broadcasted_iota(I32, (FAMILIES, LANES), 1)
    for m in range(CHILD):
        part = rebuilt[:, m * DOF : m * DOF + LANES]
        woven[pl.ds(m, FAMILIES, stride=CHILD), :] = jnp.where(lane < DOF, part, 0.0)


def kernel(counts, send, primal_in, dual_in, load_in, size_in, send_in, cell_in, other_in, dir_in, hanging_in,
           stiffness_in, recon_in, traction_in, trace_in,
           indicator, facts,
           primal, dual, load, cell_size, send_v, face_cell, face_other, face_dir, hanging, stiffness, recon, traction,
           trace, p_t, first, last, before, after, after2, p_out, p_in, w_out, w_in, picked, padded, woven, families, rebuilt,
           operator, operator3, table, side_a, side_b0, side_b1, recon3, onehot, index_a, index_b, smem_a, smem_b, term, partial, returned, part, parts,
           in_sem, index_sem, edge_send, edge_recv, p_send, p_recv, w_send, w_recv, b_send, b_recv, r_send, r_recv):
    me = lax.axis_index("dom")
    staged = [(primal_in, primal), (recon_in, recon.at[pl.ds(0, CHILD * DOF), :]), (dual_in, dual), (traction_in, traction), (trace_in, trace),
              (load_in, load), (size_in, cell_size), (stiffness_in, stiffness), (cell_in, face_cell),
              (other_in, face_other), (dir_in, face_dir), (hanging_in, hanging), (send_in, send_v)]
    loads = {}
    for i, (source, to) in enumerate(staged):
        loads[i] = pltpu.make_async_copy(source, to, in_sem.at[i])
        loads[i].start()

    barrier = pltpu.get_barrier_semaphore()
    partners = [behind(me, shift) for shift in SHIFTS]
    for stride, size in STAGES:
        partners += [in_stage(me, stride, size, step) for step in range(1, size)]
    for partner in partners:
        pl.semaphore_signal(barrier, inc=1, device_id=(partner,), device_id_type=MESH)

    start, live, cells = counts_of(counts, me)
    head = lax.rem(CHILD - lax.rem(start, CHILD), CHILD)

    def remote(source, to, send_sem, recv_sem, target):
        return pltpu.make_async_remote_copy(src_ref=source, dst_ref=to, send_sem=send_sem, recv_sem=recv_sem,
                                            device_id=(target,), device_id_type=MESH)

    def list_copy(source, to, send_sem, recv_sem, k):
        return remote(source.at[k], to.at[k], send_sem.at[k], recv_sem.at[k], behind(me, shift_of(k)))

    loads[0].wait()

    def transpose_primal(step, carry):
        to_cell_major(p_t, 0, primal, step)
        rows = pl.ds(pl.multiple_of(step * 96, 96), 96)
        wide = jnp.concatenate([recon[rows, :], jnp.zeros((96, 768 - CHILD * DOF), F32)], 1)
        hi, lo = split(wide)
        recon3[rows, 0:768] = hi
        recon3[rows, 768:1536] = hi
        recon3[rows, 1536:2304] = lo
        return carry

    loads[1].wait()
    lax.fori_loop(0, 8, transpose_primal, 0)
    loads[2].wait()
    pl.semaphore_wait(barrier, len(partners))

    def send_primal(step, carry):
        k = lax.rem(step + FIRST_LIST, NEIGH)
        gather_list(picked, p_t, send, k)
        to_cell_major(padded, CHILD, dual, step)
        pack(p_out.at[k], picked)
        list_copy(p_out, p_in, p_send, p_recv, k).start()
        return carry

    lax.fori_loop(0, NEIGH, send_primal, 0)
    first[...] = padded[8:16, :]
    last[...] = padded[pl.ds(jnp.maximum(live, 8), 8), :]
    padded[CELLS + 8 :, :] = jnp.zeros((padded.shape[0] - CELLS - 8, LANES), F32)
    edges = [remote(last, before, edge_send.at[0], edge_recv.at[0], behind(me, 1)),
             remote(first, after, edge_send.at[1], edge_recv.at[1], behind(me, -1))]
    for copy in edges:
        copy.start()

    for i in range(3, len(staged)):
        loads[i].wait()
    fill_operator(operator, traction, trace)
    hi, lo = split(operator[...].T)
    operator3[0:256, :] = hi
    operator3[256:512, :] = hi
    operator3[512:768, :] = lo
    pair = (face_dir[...] // 2) * SLOTS
    index_a[...] = pair + face_cell[...]
    index_b[...] = pair + face_other[...]
    copy_a = pltpu.make_async_copy(index_a, smem_a, index_sem.at[0])
    copy_b = pltpu.make_async_copy(index_b, smem_b, index_sem.at[1])
    copy_a.start()
    copy_b.start()

    def residuals(step, carry):
        take_residual(load, primal, stiffness, step)
        return carry

    lax.fori_loop(0, 8, residuals, 0)
    for k in range(NEIGH):
        onehot[:, k * GHOST : (k + 1) * GHOST] = low_onehot(send_v[k : k + 1, :])
    for copy in edges:
        copy.wait()
    padded[0:8, :] = before[...]
    rebuild(head, live, padded, after, after2, recon3, families, rebuilt, woven)

    def send_weight(step, carry):
        k = lax.rem(step + FIRST_LIST, NEIGH)
        at = pl.multiple_of(step * 256, 256)
        gather_rows(picked, 0, woven, lambda i: send[k, i] + (CHILD - head), GHOST)
        fill_table(table, at, p_t[pl.ds(at, 256), :], woven[pl.ds(CHILD - head + at, 256), :], operator3)
        cell_terms(term, load, woven, CHILD - head, cell_size, step)
        pack(w_out.at[k], picked)
        list_copy(w_out, w_in, w_send, w_recv, k).start()
        return carry

    lax.fori_loop(0, NEIGH, send_weight, 0)
    copy_a.wait()
    copy_b.wait()

    def take_ghosts(step, carry):
        k = lax.rem(step + FIRST_LIST, NEIGH)
        list_copy(p_out, p_in, p_send, p_recv, k).wait()
        list_copy(w_out, w_in, w_send, w_recv, k).wait()
        row = step * 6
        gather_rows(side_a, row * LANES, table, lambda i: smem_a[row + i // LANES, i % LANES], 256)
        fill_table(table, CELLS + k * GHOST, unpack(p_in[k]), unpack(w_in[k]), operator3)

        def rest(r, carry):
            gather_rows(side_a, r * LANES, table, lambda i: smem_a[r, i], LANES)
            return carry

        lax.fori_loop(row + 2, row + 6, rest, 0)
        return carry

    lax.fori_loop(0, NEIGH, take_ghosts, 0)

    lane = lax.broadcasted_iota(I32, (8, 2 * LANES), 1) % LANES
    sub = lax.broadcasted_iota(I32, (8, 2 * LANES), 0)
    pick = jnp.where(lane // 32 == sub, 1.0, 0.0).astype(BF16)
    upper = lax.broadcasted_iota(I32, (CHUNK, LANES), 1) % 64 >= 32

    def gather_b(to, c):
        gather_rows(to, 0, table, lambda i: smem_b[c * SPLIT + i // LANES, i % LANES], CHUNK)

    def raw_sums(side_b, c):
        a = side_a[pl.ds(pl.multiple_of(c * CHUNK, CHUNK), CHUNK), :]
        b = pltpu.roll(side_b[...], 64, 1)
        jump = pltpu.roll(a + b, 32, 1)
        hi, lo = split(jnp.where(upper, jump * a, pltpu.roll(jump * b, 96, 1)))
        return dot_nt(pick, jnp.concatenate([hi, lo], 1))

    def add_sums(raw, c, carry):
        sum_a, sum_b = carry
        face = c * CHUNK + lax.broadcasted_iota(I32, (1, CHUNK), 1)
        area = jnp.where(face < 3 * live, 0.5 * (1.0 - 0.75 * lanes_of(hanging, c).astype(F32)), 0.0)
        is_even = lanes_of(face_dir, c) % 2 == 0
        term_a = area * jnp.where(is_even, raw[1:2], raw[3:4])
        term_b = area * jnp.where(is_even, raw[0:1], raw[2:3])
        cell, other = lanes_of(face_cell, c), lanes_of(face_other, c)
        sum_a += scatter(cell, term_a, CELLS // LANES, low_onehot(cell))
        sum_b += scatter(other, term_b, SLOTS // LANES, low_onehot(other))
        return sum_a, sum_b

    def body(i, carry):
        raw_before, sums = carry
        gather_b(side_b1, 2 * i + 1)
        raw = raw_sums(side_b0, 2 * i)
        sums = add_sums(raw_before, jnp.maximum(2 * i - 1, 0), sums)
        gather_b(side_b0, jnp.minimum(2 * i + 2, CHUNKS - 1))
        raw_after = raw_sums(side_b1, 2 * i + 1)
        sums = add_sums(raw, 2 * i, sums)
        return raw_after, sums

    gather_b(side_b0, 0)
    zero = (jnp.zeros((CELLS // LANES, LANES), F32), jnp.zeros((SLOTS // LANES, LANES), F32))
    raw, sums = lax.fori_loop(0, CHUNKS // 2, body, (jnp.zeros((8, CHUNK), F32), zero))
    sum_a, sum_b = add_sums(raw, CHUNKS - 1, sums)
    for k in range(NEIGH):
        at = CELLS // LANES + 2 * k
        partial[k] = sum_b[at : at + 2]
    backs = [remote(partial.at[k], returned.at[k], b_send, b_recv, behind(me, -SHIFTS[k])) for k in range(NEIGH)]
    for copy in backs:
        copy.start()
    index = jnp.concatenate([send_v[k : k + 1, :] for k in range(NEIGH)], 1)
    out = term[...] + sum_a + sum_b[: CELLS // LANES]
    remote(partial, returned, b_send, b_recv, behind(me, 1)).wait_recv()
    value = jnp.concatenate([returned[k, r : r + 1, :] for k in range(NEIGH) for r in range(2)], 1)
    out = out + scatter(index, value, CELLS // LANES, onehot[...])
    slot = lax.broadcasted_iota(I32, out.shape, 0) * LANES + lax.broadcasted_iota(I32, out.shape, 1)
    indicator[...] = out

    total = jnp.sum(jnp.where(slot < live, jnp.abs(out), 0.0), axis=0, keepdims=True)
    place = 0
    for stage, (stride, count) in enumerate(STAGES):
        part[stage] = total
        slots = pl.ds(place, count - 1)
        for step in range(1, count):
            remote(part.at[stage], parts.at[place + step - 1], r_send.at[stage], r_recv.at[stage],
                   in_stage(me, stride, count, step)).start()
        remote(parts.at[slots], parts.at[slots], r_send.at[stage], r_recv.at[stage], behind(me, 1)).wait_recv()
        total = total + jnp.sum(parts[place : place + count - 1], axis=0)
        place += count - 1

    mean = jnp.sum(total) / cells.astype(F32)
    facts[...] = jnp.where(slot < live, mean, -1.0)
    remote(partial, returned, b_send, b_recv, behind(me, 1)).wait_send()
    place = 0
    for stage, (stride, count) in enumerate(STAGES):
        slots = pl.ds(place, count - 1)
        remote(parts.at[slots], parts.at[slots], r_send.at[stage], r_recv.at[stage], behind(me, 1)).wait_send()
        place += count - 1


SMEM = pl.BlockSpec(memory_space=pltpu.SMEM)
VMEM = pl.BlockSpec(memory_space=pltpu.VMEM)
ANY = pl.BlockSpec(memory_space=pl.ANY)


def per_device(primal, dual, load, cell_size, cell_count, ghost_send, face_cell, face_other, face_dir, hanging,
               stiffness, recon, traction, trace):
    send = ghost_send[0]
    as_rows = lambda x: x.reshape(-1, LANES)
    f32 = lambda *shape: pltpu.VMEM(shape, F32)
    bf16 = lambda *shape: pltpu.VMEM(shape, BF16)
    i32 = lambda *shape: pltpu.VMEM(shape, I32)
    dma = lambda n: pltpu.SemaphoreType.DMA((n,))
    rows = FACES // LANES
    cells = CELLS // LANES
    steps = sum(size - 1 for _, size in STAGES)
    scratch = [
        f32(DOF, CELLS), f32(DOF, CELLS), f32(DOF, CELLS), f32(cells, LANES), i32(NEIGH, GHOST),
        i32(rows, LANES), i32(rows, LANES), i32(rows, LANES), i32(rows, LANES),
        f32(DOF, DOF), f32(768, CHILD * DOF), f32(6 * FACE_DOF, DOF), f32(6 * FACE_DOF, DOF),
        f32(CELLS, LANES),
        f32(8, LANES), f32(8, LANES), f32(8, LANES), f32(8, LANES), f32(16, LANES),
        f32(NEIGH, PACKED, LANES), f32(NEIGH, PACKED, LANES), f32(NEIGH, PACKED, LANES), f32(NEIGH, PACKED, LANES),
        f32(3 * THIRD, LANES),
        f32(FAMILIES * CHILD + 8, LANES), f32(FAMILIES * CHILD, LANES), f32(FAMILIES, 768), f32(FAMILIES, 768),
        f32(384, 256), bf16(768, 384), f32(3 * SLOTS, LANES), f32(FACES, LANES), f32(CHUNK, LANES), f32(CHUNK, LANES),
        bf16(768, 2304), bf16(LANES, GHOSTS),
        i32(rows, LANES), i32(rows, LANES), pltpu.SMEM((rows, LANES), I32), pltpu.SMEM((rows, LANES), I32),
        f32(cells, LANES), f32(NEIGH, 2, LANES), f32(NEIGH, 2, LANES), f32(len(STAGES), 1, LANES), f32(steps, 1, LANES),
        dma(13), dma(2), dma(2), dma(2), dma(NEIGH), dma(NEIGH), dma(NEIGH), dma(NEIGH),
        pltpu.SemaphoreType.DMA, pltpu.SemaphoreType.DMA, dma(len(STAGES)), dma(len(STAGES)),
    ]
    indicator, facts = pl.pallas_call(
        kernel,
        out_shape=[jax.ShapeDtypeStruct((cells, LANES), F32)] * 2,
        in_specs=[SMEM] * 2 + [ANY] * 13, out_specs=[VMEM] * 2, scratch_shapes=scratch,
        compiler_params=pltpu.CompilerParams(collective_id=0, has_side_effects=True,
                                             vmem_limit_bytes=56 * 1024 * 1024),
        name="indicators",
    )(cell_count, send, primal, dual, load, as_rows(cell_size), send, as_rows(face_cell), as_rows(face_other),
      as_rows(face_dir), as_rows(hanging), stiffness, recon, traction, trace)
    facts = facts.reshape(-1)
    indicator = jnp.where(facts < 0.0, 0.0, indicator.reshape(-1))
    return indicator, jnp.abs(indicator) / (jnp.abs(facts) + 1e-06)

def solution(mesh):
    in_specs = (P(None, "dom"), P(None, "dom"), P(None, "dom"), P("dom"), P(), P("dom", None, None), P("dom"), P("dom"),
                P("dom"), P("dom"), P(), P(), P(), P())
    return jax.shard_map(per_device, mesh=mesh, in_specs=in_specs, out_specs=(P("dom"), P("dom")), check_vma=False)
```

```python
import functools

import jax
import jax.numpy as jnp
from jax import lax
from jax.experimental import pallas as pl
from jax.experimental.pallas import tpu as pltpu
from jax.sharding import PartitionSpec as P

F32 = jnp.float32
BF16 = jnp.bfloat16
I32 = jnp.int32

DOF = 81
FACE_DOF = 27
CHILD = 8
CELLS = 2048
NEIGH = 8
GHOST = 256
GHOSTS = NEIGH * GHOST
SLOTS = CELLS + GHOSTS
FACES = 6144
LANES = 128
FAMILIES = 272
THIRD = 88
PACKED = 2 * THIRD
CHUNK = 256
CHUNKS = FACES // CHUNK
SPLIT = CHUNK // LANES


def split(x):
    high = x.astype(BF16)
    return high, (x - high.astype(F32)).astype(BF16)


def dot_nt(a, b):
    return lax.dot_general(a, b, (((1,), (1,)), ((), ())), preferred_element_type=F32)


def dot_nn(a, b):
    return lax.dot_general(a, b, (((1,), (0,)), ((), ())), preferred_element_type=F32)


def gather_rows(dst, dst_at, src, index_of, count):
    sub = lax.broadcasted_iota(I32, (8, LANES), 0)
    for base in range(0, count, 8):
        rows = [src[pl.ds(index_of(base + u), 1), :] for u in range(8)]
        tile = jnp.broadcast_to(rows[0], (8, LANES))
        for u in range(1, 8):
            tile = jnp.where(sub == u, jnp.broadcast_to(rows[u], (8, LANES)), tile)
        dst[pl.ds(pl.multiple_of(dst_at + base, 8), 8), :] = tile


def turned_block(src, at):
    return jnp.concatenate([src[:, pl.ds(at, 256)], jnp.zeros((LANES - DOF, 256), F32)], 0).T


def to_cell_major(dst, row, src, step):
    at = pl.multiple_of(step * 256, 256)
    dst[pl.ds(pl.multiple_of(row + at, CHILD), 256), :] = turned_block(src, at)


def pack(to, rows):
    lane = lax.broadcasted_iota(I32, (THIRD, LANES), 1)
    second = pltpu.roll(rows[THIRD : 2 * THIRD, :], DOF, 1)
    third = pltpu.roll(rows[2 * THIRD :, :], 2 * DOF - LANES, 1)
    upper = jnp.where(lane < DOF, rows[0:THIRD, :], second)
    to[...] = jnp.concatenate([upper, jnp.where(lane < 2 * DOF - LANES, second, third)], 0)


def unpack(rows):
    lane = lax.broadcasted_iota(I32, (THIRD, LANES), 1)
    upper, lower = rows[:THIRD], rows[THIRD:]
    second = pltpu.roll(jnp.where(lane < 2 * DOF - LANES, lower, upper), LANES - DOF, 1)
    third = pltpu.roll(lower, 2 * LANES - 2 * DOF, 1)
    return jnp.concatenate([upper, second, third[: GHOST - PACKED]], 0)


def fill_operator(operator, traction, trace):
    operator[...] = jnp.zeros(operator.shape, F32)
    for d in range(6):
        rows = slice(d * FACE_DOF, (d + 1) * FACE_DOF)
        operator[64 * d : 64 * d + FACE_DOF, 0:DOF] = traction[rows, :]
        operator[64 * d + 32 : 64 * d + 32 + FACE_DOF, LANES : LANES + DOF] = trace[rows, :]


def fill_table(table, slot, p_rows, w_rows, operator):
    hi, lo = split(jnp.concatenate([p_rows, w_rows], 1))
    out = dot_nn(jnp.concatenate([hi, lo, hi], 1), operator[...])
    for pair in range(3):
        table[pl.ds(pl.multiple_of(pair * SLOTS + slot, 256), 256), :] = out[:, pair * LANES : (pair + 1) * LANES]


def take_residual(load, primal, stiffness, step):
    cells = pl.ds(pl.multiple_of(step * 256, 256), 256)
    s_hi, s_lo = split(stiffness[...])
    p_hi, p_lo = split(primal[:, cells])
    load[:, cells] = load[:, cells] - (dot_nn(s_hi, p_hi) + dot_nn(s_lo, p_hi) + dot_nn(s_hi, p_lo))


def cell_terms(out, residual, woven, skip, cell_size, step):
    cells = pl.ds(pl.multiple_of(step * 256, 256), 256)
    total = jnp.sum(residual[:, cells] * woven[pl.ds(skip + step * 256, 256), :].T[:DOF, :], axis=0, keepdims=True)
    for r in range(2):
        i = step * 2 + r
        out[pl.ds(i, 1), :] = cell_size[pl.ds(i, 1), :] * total[:, r * LANES : (r + 1) * LANES]


def lanes_of(ref, chunk):
    return jnp.concatenate([ref[pl.ds(chunk * SPLIT + i, 1), :] for i in range(SPLIT)], 1)


def low_onehot(index):
    low = lax.broadcasted_iota(I32, (LANES, index.shape[1]), 0) == index % LANES
    return jnp.where(low, 1.0, 0.0).astype(BF16)


def scatter(index, value, high_count, onehot):
    high = lax.broadcasted_iota(I32, (high_count, index.shape[1]), 0) == index // LANES
    both = dot_nt(jnp.concatenate(split(jnp.where(high, value, 0.0)), 0), onehot)
    return both[:high_count] + both[high_count:]


MESH = pl.DeviceIdType.MESH
RANKS = 128
SHIFTS = [(1 << which // 2) * (1 - 2 * (which % 2)) for which in range(NEIGH)]
FIRST_LIST = 4
STAGES = ((1, 8), (8, 16))


def counts_of(counts, me):
    def body(i, carry):
        before, here, cells = carry
        c = counts[i]
        return before + jnp.where(i < me, c, 0), here + jnp.where(i == me, c, 0), cells + c

    return lax.fori_loop(0, RANKS, body, (jnp.int32(0), jnp.int32(0), jnp.int32(0)), unroll=32)


def behind(me, by):
    return lax.rem(me + (by + RANKS), RANKS)


def shift_of(k):
    e = k // 2
    power = 1 + e + e * (e - 1) // 2 + e * (e - 1) * (e - 2) // 6
    return power * (1 - 2 * (k % 2))


def in_stage(me, stride, size, step):
    place = lax.rem(me // stride, size)
    return me + (lax.rem(place + step, size) - place) * stride


def gather_list(picked, source, send, k):
    gather_rows(picked, 0, source, lambda i: send[k, i], GHOST)


def rebuild(head, live, padded, after, after2, recon3, families, rebuilt, woven):
    after2[0:8, :] = jnp.zeros((8, LANES), F32)
    after2[8:16, :] = after[...]
    own = lax.rem(live - head + CHILD, CHILD)
    split_family = 1 + (live - head) // CHILD
    row = lax.broadcasted_iota(I32, (FAMILIES, LANES), 0)
    families[:, 640:768] = jnp.zeros((FAMILIES, LANES), F32)
    for m in range(CHILD):
        cells = padded[pl.ds(head + m, FAMILIES, stride=CHILD), :]
        late = after2[pl.ds(CHILD + m - own, 1), :]
        cells = jnp.where((row == split_family) & (m >= own), late, cells)
        families[:, m * DOF : (m + 1) * DOF] = cells[:, :DOF]
    hi, lo = split(families[...])
    rebuilt[:, : CHILD * DOF] = dot_nt(jnp.concatenate([hi, lo, hi], 1), recon3[0 : CHILD * DOF, :])
    lane = lax.broadcasted_iota(I32, (FAMILIES, LANES), 1)
    for m in range(CHILD):
        part = rebuilt[:, m * DOF : m * DOF + LANES]
        woven[pl.ds(m, FAMILIES, stride=CHILD), :] = jnp.where(lane < DOF, part, 0.0)


def kernel(counts, send, primal_in, dual_in, load_in, size_in, send_in, cell_in, other_in, dir_in, hanging_in,
           stiffness_in, recon_in, traction_in, trace_in,
           indicator, facts,
           primal, dual, load, cell_size, send_v, face_cell, face_other, face_dir, hanging, stiffness, recon, traction,
           trace, p_t, first, last, before, after, after2, p_out, p_in, w_out, w_in, picked, padded, woven, families, rebuilt,
           operator, operator3, table, side_a, side_b0, side_b1, recon3, onehot, index_a, index_b, smem_a, smem_b, term, partial, returned, part, parts,
           in_sem, index_sem, edge_send, edge_recv, p_send, p_recv, w_send, w_recv, b_send, b_recv, r_send, r_recv):
    me = lax.axis_index("dom")
    staged = [(dual_in, dual), (primal_in, primal), (recon_in, recon.at[pl.ds(0, CHILD * DOF), :]), (traction_in, traction), (trace_in, trace),
              (load_in, load), (size_in, cell_size), (stiffness_in, stiffness), (cell_in, face_cell),
              (other_in, face_other), (dir_in, face_dir), (hanging_in, hanging), (send_in, send_v)]
    loads = {}
    for i, (source, to) in enumerate(staged):
        loads[i] = pltpu.make_async_copy(source, to, in_sem.at[i])
        loads[i].start()

    barrier = pltpu.get_barrier_semaphore()
    partners = [behind(me, shift) for shift in SHIFTS]
    for stride, size in STAGES:
        partners += [in_stage(me, stride, size, step) for step in range(1, size)]
    for partner in partners:
        pl.semaphore_signal(barrier, inc=1, device_id=(partner,), device_id_type=MESH)

    start, live, cells = counts_of(counts, me)
    head = lax.rem(CHILD - lax.rem(start, CHILD), CHILD)

    def remote(source, to, send_sem, recv_sem, target):
        return pltpu.make_async_remote_copy(src_ref=source, dst_ref=to, send_sem=send_sem, recv_sem=recv_sem,
                                            device_id=(target,), device_id_type=MESH)

    def list_copy(source, to, send_sem, recv_sem, k):
        return remote(source.at[k], to.at[k], send_sem.at[k], recv_sem.at[k], behind(me, shift_of(k)))

    loads[0].wait()
    cell = lax.broadcasted_iota(I32, (16, CELLS), 1)
    row = lax.broadcasted_iota(I32, (16, CELLS), 0)
    picked_cell = jnp.where(row < CHILD, row, live - 2 * CHILD + row)
    chosen = jnp.where(cell == picked_cell, 1.0, 0.0).astype(BF16)
    hi, lo = split(dual[...])
    ends = dot_nt(chosen, hi) + dot_nt(chosen, lo)
    first[...] = jnp.zeros((8, LANES), F32)
    last[...] = jnp.zeros((8, LANES), F32)
    first[:, :DOF] = ends[:CHILD]
    last[:, :DOF] = ends[CHILD:]
    pl.semaphore_wait(barrier, len(partners))
    edges = [remote(last, before, edge_send.at[0], edge_recv.at[0], behind(me, 1)),
             remote(first, after, edge_send.at[1], edge_recv.at[1], behind(me, -1))]
    for copy in edges:
        copy.start()

    loads[1].wait()

    def transpose_primal(step, carry):
        to_cell_major(p_t, 0, primal, step)
        rows = pl.ds(pl.multiple_of(step * 96, 96), 96)
        wide = jnp.concatenate([recon[rows, :], jnp.zeros((96, 768 - CHILD * DOF), F32)], 1)
        hi, lo = split(wide)
        recon3[rows, 0:768] = hi
        recon3[rows, 768:1536] = hi
        recon3[rows, 1536:2304] = lo
        return carry

    loads[2].wait()
    lax.fori_loop(0, 8, transpose_primal, 0)

    def send_primal(step, carry):
        k = lax.rem(step + FIRST_LIST, NEIGH)
        gather_list(picked, p_t, send, k)
        to_cell_major(padded, CHILD, dual, step)
        pack(p_out.at[k], picked)
        list_copy(p_out, p_in, p_send, p_recv, k).start()
        return carry

    lax.fori_loop(0, NEIGH, send_primal, 0)
    padded[CELLS + 8 :, :] = jnp.zeros((padded.shape[0] - CELLS - 8, LANES), F32)
    for i in range(3, len(staged)):
        loads[i].wait()
    fill_operator(operator, traction, trace)
    hi, lo = split(operator[...].T)
    operator3[0:256, :] = hi
    operator3[256:512, :] = hi
    operator3[512:768, :] = lo
    pair = (face_dir[...] // 2) * SLOTS
    index_a[...] = pair + face_cell[...]
    index_b[...] = pair + face_other[...]
    copy_a = pltpu.make_async_copy(index_a, smem_a, index_sem.at[0])
    copy_b = pltpu.make_async_copy(index_b, smem_b, index_sem.at[1])
    copy_a.start()
    copy_b.start()

    def residuals(step, carry):
        take_residual(load, primal, stiffness, step)
        return carry

    lax.fori_loop(0, 8, residuals, 0)
    for k in range(NEIGH):
        onehot[:, k * GHOST : (k + 1) * GHOST] = low_onehot(send_v[k : k + 1, :])
    for copy in edges:
        copy.wait()
    padded[0:8, :] = before[...]
    rebuild(head, live, padded, after, after2, recon3, families, rebuilt, woven)

    def send_weight(step, carry):
        k = lax.rem(step + FIRST_LIST, NEIGH)
        at = pl.multiple_of(step * 256, 256)
        gather_rows(picked, 0, woven, lambda i: send[k, i] + (CHILD - head), GHOST)
        fill_table(table, at, p_t[pl.ds(at, 256), :], woven[pl.ds(CHILD - head + at, 256), :], operator3)
        cell_terms(term, load, woven, CHILD - head, cell_size, step)
        pack(w_out.at[k], picked)
        list_copy(w_out, w_in, w_send, w_recv, k).start()
        return carry

    lax.fori_loop(0, NEIGH, send_weight, 0)
    copy_a.wait()
    copy_b.wait()

    def take_ghosts(step, carry):
        k = lax.rem(step + FIRST_LIST, NEIGH)
        list_copy(p_out, p_in, p_send, p_recv, k).wait()
        list_copy(w_out, w_in, w_send, w_recv, k).wait()
        row = step * 6
        gather_rows(side_a, row * LANES, table, lambda i: smem_a[row + i // LANES, i % LANES], 256)
        fill_table(table, CELLS + k * GHOST, unpack(p_in[k]), unpack(w_in[k]), operator3)

        def rest(r, carry):
            gather_rows(side_a, r * LANES, table, lambda i: smem_a[r, i], LANES)
            return carry

        lax.fori_loop(row + 2, row + 6, rest, 0)
        return carry

    lax.fori_loop(0, NEIGH, take_ghosts, 0)

    lane = lax.broadcasted_iota(I32, (8, 2 * LANES), 1) % LANES
    sub = lax.broadcasted_iota(I32, (8, 2 * LANES), 0)
    pick = jnp.where(lane // 32 == sub, 1.0, 0.0).astype(BF16)
    upper = lax.broadcasted_iota(I32, (CHUNK, LANES), 1) % 64 >= 32

    def gather_b(to, c):
        gather_rows(to, 0, table, lambda i: smem_b[c * SPLIT + i // LANES, i % LANES], CHUNK)

    def raw_sums(side_b, c):
        a = side_a[pl.ds(pl.multiple_of(c * CHUNK, CHUNK), CHUNK), :]
        b = pltpu.roll(side_b[...], 64, 1)
        jump = pltpu.roll(a + b, 32, 1)
        hi, lo = split(jnp.where(upper, jump * a, pltpu.roll(jump * b, 96, 1)))
        return dot_nt(pick, jnp.concatenate([hi, lo], 1))

    def add_sums(raw, c, carry):
        sum_a, sum_b = carry
        face = c * CHUNK + lax.broadcasted_iota(I32, (1, CHUNK), 1)
        area = jnp.where(face < 3 * live, 0.5 * (1.0 - 0.75 * lanes_of(hanging, c).astype(F32)), 0.0)
        is_even = lanes_of(face_dir, c) % 2 == 0
        term_a = area * jnp.where(is_even, raw[1:2], raw[3:4])
        term_b = area * jnp.where(is_even, raw[0:1], raw[2:3])
        cell, other = lanes_of(face_cell, c), lanes_of(face_other, c)
        sum_a += scatter(cell, term_a, CELLS // LANES, low_onehot(cell))
        sum_b += scatter(other, term_b, SLOTS // LANES, low_onehot(other))
        return sum_a, sum_b

    def body(i, carry):
        raw_before, sums = carry
        gather_b(side_b1, 2 * i + 1)
        raw = raw_sums(side_b0, 2 * i)
        sums = add_sums(raw_before, jnp.maximum(2 * i - 1, 0), sums)
        gather_b(side_b0, jnp.minimum(2 * i + 2, CHUNKS - 1))
        raw_after = raw_sums(side_b1, 2 * i + 1)
        sums = add_sums(raw, 2 * i, sums)
        return raw_after, sums

    gather_b(side_b0, 0)
    zero = (jnp.zeros((CELLS // LANES, LANES), F32), jnp.zeros((SLOTS // LANES, LANES), F32))
    raw, sums = lax.fori_loop(0, CHUNKS // 2, body, (jnp.zeros((8, CHUNK), F32), zero))
    sum_a, sum_b = add_sums(raw, CHUNKS - 1, sums)
    for k in range(NEIGH):
        at = CELLS // LANES + 2 * k
        partial[k] = sum_b[at : at + 2]
    backs = [remote(partial.at[k], returned.at[k], b_send, b_recv, behind(me, -SHIFTS[k])) for k in range(NEIGH)]
    for copy in backs:
        copy.start()
    index = jnp.concatenate([send_v[k : k + 1, :] for k in range(NEIGH)], 1)
    out = term[...] + sum_a + sum_b[: CELLS // LANES]
    remote(partial, returned, b_send, b_recv, behind(me, 1)).wait_recv()
    value = jnp.concatenate([returned[k, r : r + 1, :] for k in range(NEIGH) for r in range(2)], 1)
    out = out + scatter(index, value, CELLS // LANES, onehot[...])
    slot = lax.broadcasted_iota(I32, out.shape, 0) * LANES + lax.broadcasted_iota(I32, out.shape, 1)
    indicator[...] = out

    total = jnp.sum(jnp.where(slot < live, jnp.abs(out), 0.0), axis=0, keepdims=True)
    place = 0
    for stage, (stride, count) in enumerate(STAGES):
        part[stage] = total
        slots = pl.ds(place, count - 1)
        for step in range(1, count):
            remote(part.at[stage], parts.at[place + step - 1], r_send.at[stage], r_recv.at[stage],
                   in_stage(me, stride, count, step)).start()
        remote(parts.at[slots], parts.at[slots], r_send.at[stage], r_recv.at[stage], behind(me, 1)).wait_recv()
        total = total + jnp.sum(parts[place : place + count - 1], axis=0)
        place += count - 1

    mean = jnp.sum(total) / cells.astype(F32)
    facts[...] = jnp.where(slot < live, mean, -1.0)
    remote(partial, returned, b_send, b_recv, behind(me, 1)).wait_send()
    place = 0
    for stage, (stride, count) in enumerate(STAGES):
        slots = pl.ds(place, count - 1)
        remote(parts.at[slots], parts.at[slots], r_send.at[stage], r_recv.at[stage], behind(me, 1)).wait_send()
        place += count - 1


SMEM = pl.BlockSpec(memory_space=pltpu.SMEM)
VMEM = pl.BlockSpec(memory_space=pltpu.VMEM)
ANY = pl.BlockSpec(memory_space=pl.ANY)


def per_device(primal, dual, load, cell_size, cell_count, ghost_send, face_cell, face_other, face_dir, hanging,
               stiffness, recon, traction, trace):
    send = ghost_send[0]
    as_rows = lambda x: x.reshape(-1, LANES)
    f32 = lambda *shape: pltpu.VMEM(shape, F32)
    bf16 = lambda *shape: pltpu.VMEM(shape, BF16)
    i32 = lambda *shape: pltpu.VMEM(shape, I32)
    dma = lambda n: pltpu.SemaphoreType.DMA((n,))
    rows = FACES // LANES
    cells = CELLS // LANES
    steps = sum(size - 1 for _, size in STAGES)
    scratch = [
        f32(DOF, CELLS), f32(DOF, CELLS), f32(DOF, CELLS), f32(cells, LANES), i32(NEIGH, GHOST),
        i32(rows, LANES), i32(rows, LANES), i32(rows, LANES), i32(rows, LANES),
        f32(DOF, DOF), f32(768, CHILD * DOF), f32(6 * FACE_DOF, DOF), f32(6 * FACE_DOF, DOF),
        f32(CELLS, LANES),
        f32(8, LANES), f32(8, LANES), f32(8, LANES), f32(8, LANES), f32(16, LANES),
        f32(NEIGH, PACKED, LANES), f32(NEIGH, PACKED, LANES), f32(NEIGH, PACKED, LANES), f32(NEIGH, PACKED, LANES),
        f32(3 * THIRD, LANES),
        f32(FAMILIES * CHILD + 8, LANES), f32(FAMILIES * CHILD, LANES), f32(FAMILIES, 768), f32(FAMILIES, 768),
        f32(384, 256), bf16(768, 384), f32(3 * SLOTS, LANES), f32(FACES, LANES), f32(CHUNK, LANES), f32(CHUNK, LANES),
        bf16(768, 2304), bf16(LANES, GHOSTS),
        i32(rows, LANES), i32(rows, LANES), pltpu.SMEM((rows, LANES), I32), pltpu.SMEM((rows, LANES), I32),
        f32(cells, LANES), f32(NEIGH, 2, LANES), f32(NEIGH, 2, LANES), f32(len(STAGES), 1, LANES), f32(steps, 1, LANES),
        dma(13), dma(2), dma(2), dma(2), dma(NEIGH), dma(NEIGH), dma(NEIGH), dma(NEIGH),
        pltpu.SemaphoreType.DMA, pltpu.SemaphoreType.DMA, dma(len(STAGES)), dma(len(STAGES)),
    ]
    indicator, facts = pl.pallas_call(
        kernel,
        out_shape=[jax.ShapeDtypeStruct((cells, LANES), F32)] * 2,
        in_specs=[SMEM] * 2 + [ANY] * 13, out_specs=[VMEM] * 2, scratch_shapes=scratch,
        compiler_params=pltpu.CompilerParams(collective_id=0, has_side_effects=True,
                                             vmem_limit_bytes=56 * 1024 * 1024),
        name="indicators",
    )(cell_count, send, primal, dual, load, as_rows(cell_size), send, as_rows(face_cell), as_rows(face_other),
      as_rows(face_dir), as_rows(hanging), stiffness, recon, traction, trace)
    facts = facts.reshape(-1)
    indicator = jnp.where(facts < 0.0, 0.0, indicator.reshape(-1))
    return indicator, jnp.abs(indicator) / (jnp.abs(facts) + 1e-06)

def solution(mesh):
    in_specs = (P(None, "dom"), P(None, "dom"), P(None, "dom"), P("dom"), P(), P("dom", None, None), P("dom"), P("dom"),
                P("dom"), P("dom"), P(), P(), P(), P())
    return jax.shard_map(per_device, mesh=mesh, in_specs=in_specs, out_specs=(P("dom"), P("dom")), check_vma=False)
```

```python
import functools

import jax
import jax.numpy as jnp
from jax import lax
from jax.experimental import pallas as pl
from jax.experimental.pallas import tpu as pltpu
from jax.sharding import PartitionSpec as P

F32 = jnp.float32
BF16 = jnp.bfloat16
I32 = jnp.int32

DOF = 81
FACE_DOF = 27
CHILD = 8
CELLS = 2048
NEIGH = 8
GHOST = 256
GHOSTS = NEIGH * GHOST
SLOTS = CELLS + GHOSTS
FACES = 6144
LANES = 128
FAMILIES = 272
THIRD = 88
PACKED = 2 * THIRD
CHUNK = 256
CHUNKS = FACES // CHUNK
SPLIT = CHUNK // LANES


def split(x):
    high = x.astype(BF16)
    return high, (x - high.astype(F32)).astype(BF16)


def dot_nt(a, b):
    return lax.dot_general(a, b, (((1,), (1,)), ((), ())), preferred_element_type=F32)


def dot_nn(a, b):
    return lax.dot_general(a, b, (((1,), (0,)), ((), ())), preferred_element_type=F32)


def gather_rows(dst, dst_at, src, index_of, count):
    sub = lax.broadcasted_iota(I32, (8, LANES), 0)
    for base in range(0, count, 8):
        rows = [src[pl.ds(index_of(base + u), 1), :] for u in range(8)]
        tile = jnp.broadcast_to(rows[0], (8, LANES))
        for u in range(1, 8):
            tile = jnp.where(sub == u, jnp.broadcast_to(rows[u], (8, LANES)), tile)
        dst[pl.ds(pl.multiple_of(dst_at + base, 8), 8), :] = tile


def turned_block(src, at):
    return jnp.concatenate([src[:, pl.ds(at, 256)], jnp.zeros((LANES - DOF, 256), F32)], 0).T


def to_cell_major(dst, row, src, step):
    at = pl.multiple_of(step * 256, 256)
    dst[pl.ds(pl.multiple_of(row + at, CHILD), 256), :] = turned_block(src, at)


def pack(to, rows):
    lane = lax.broadcasted_iota(I32, (THIRD, LANES), 1)
    second = pltpu.roll(rows[THIRD : 2 * THIRD, :], DOF, 1)
    third = pltpu.roll(rows[2 * THIRD :, :], 2 * DOF - LANES, 1)
    upper = jnp.where(lane < DOF, rows[0:THIRD, :], second)
    to[...] = jnp.concatenate([upper, jnp.where(lane < 2 * DOF - LANES, second, third)], 0)


def unpack(rows):
    lane = lax.broadcasted_iota(I32, (THIRD, LANES), 1)
    upper, lower = rows[:THIRD], rows[THIRD:]
    second = pltpu.roll(jnp.where(lane < 2 * DOF - LANES, lower, upper), LANES - DOF, 1)
    third = pltpu.roll(lower, 2 * LANES - 2 * DOF, 1)
    return jnp.concatenate([upper, second, third[: GHOST - PACKED]], 0)


def fill_operator(operator, traction, trace):
    operator[...] = jnp.zeros(operator.shape, F32)
    for d in range(6):
        rows = slice(d * FACE_DOF, (d + 1) * FACE_DOF)
        operator[64 * d : 64 * d + FACE_DOF, 0:DOF] = traction[rows, :]
        operator[64 * d + 32 : 64 * d + 32 + FACE_DOF, LANES : LANES + DOF] = trace[rows, :]


def fill_table(table, slot, p_rows, w_rows, operator):
    hi, lo = split(jnp.concatenate([p_rows, w_rows], 1))
    out = dot_nn(jnp.concatenate([hi, lo, hi], 1), operator[...])
    for pair in range(3):
        table[pl.ds(pl.multiple_of(pair * SLOTS + slot, 256), 256), :] = out[:, pair * LANES : (pair + 1) * LANES]


def take_residual(load, primal, stiffness, step):
    cells = pl.ds(pl.multiple_of(step * 256, 256), 256)
    s_hi, s_lo = split(stiffness[...])
    p_hi, p_lo = split(primal[:, cells])
    load[:, cells] = load[:, cells] - (dot_nn(s_hi, p_hi) + dot_nn(s_lo, p_hi) + dot_nn(s_hi, p_lo))


def cell_terms(out, residual, woven, skip, cell_size, step):
    cells = pl.ds(pl.multiple_of(step * 256, 256), 256)
    total = jnp.sum(residual[:, cells] * woven[pl.ds(skip + step * 256, 256), :].T[:DOF, :], axis=0, keepdims=True)
    for r in range(2):
        i = step * 2 + r
        out[pl.ds(i, 1), :] = cell_size[pl.ds(i, 1), :] * total[:, r * LANES : (r + 1) * LANES]


def lanes_of(ref, chunk):
    return jnp.concatenate([ref[pl.ds(chunk * SPLIT + i, 1), :] for i in range(SPLIT)], 1)


def low_onehot(index):
    low = lax.broadcasted_iota(I32, (LANES, index.shape[1]), 0) == index % LANES
    return jnp.where(low, 1.0, 0.0).astype(BF16)


def scatter(index, value, high_count, onehot):
    high = lax.broadcasted_iota(I32, (high_count, index.shape[1]), 0) == index // LANES
    both = dot_nt(jnp.concatenate(split(jnp.where(high, value, 0.0)), 0), onehot)
    return both[:high_count] + both[high_count:]


MESH = pl.DeviceIdType.MESH
RANKS = 128
SHIFTS = [(1 << which // 2) * (1 - 2 * (which % 2)) for which in range(NEIGH)]
FIRST_LIST = 4
SEND_ORDER = [4, 5, 6, 7, 2, 3, 0, 1]
STAGES = ((1, 8), (8, 16))


def counts_of(counts, me):
    def body(i, carry):
        before, here, cells = carry
        c = counts[i]
        return before + jnp.where(i < me, c, 0), here + jnp.where(i == me, c, 0), cells + c

    return lax.fori_loop(0, RANKS, body, (jnp.int32(0), jnp.int32(0), jnp.int32(0)), unroll=32)


def behind(me, by):
    return lax.rem(me + (by + RANKS), RANKS)


def shift_of(k):
    e = k // 2
    power = 1 + e + e * (e - 1) // 2 + e * (e - 1) * (e - 2) // 6
    return power * (1 - 2 * (k % 2))


def in_stage(me, stride, size, step):
    place = lax.rem(me // stride, size)
    return me + (lax.rem(place + step, size) - place) * stride


def gather_list(picked, source, send, k):
    gather_rows(picked, 0, source, lambda i: send[k, i], GHOST)


def rebuild(head, live, padded, after, after2, recon3, families, rebuilt, woven):
    after2[0:8, :] = jnp.zeros((8, LANES), F32)
    after2[8:16, :] = after[...]
    own = lax.rem(live - head + CHILD, CHILD)
    split_family = 1 + (live - head) // CHILD
    row = lax.broadcasted_iota(I32, (FAMILIES, LANES), 0)
    families[:, 640:768] = jnp.zeros((FAMILIES, LANES), F32)
    for m in range(CHILD):
        cells = padded[pl.ds(head + m, FAMILIES, stride=CHILD), :]
        late = after2[pl.ds(CHILD + m - own, 1), :]
        cells = jnp.where((row == split_family) & (m >= own), late, cells)
        families[:, m * DOF : (m + 1) * DOF] = cells[:, :DOF]
    hi, lo = split(families[...])
    rebuilt[:, : CHILD * DOF] = dot_nt(jnp.concatenate([hi, lo, hi], 1), recon3[0 : CHILD * DOF, :])
    lane = lax.broadcasted_iota(I32, (FAMILIES, LANES), 1)
    for m in range(CHILD):
        part = rebuilt[:, m * DOF : m * DOF + LANES]
        woven[pl.ds(m, FAMILIES, stride=CHILD), :] = jnp.where(lane < DOF, part, 0.0)


def kernel(counts, send, primal_in, dual_in, load_in, size_in, send_in, cell_in, other_in, dir_in, hanging_in,
           stiffness_in, recon_in, traction_in, trace_in,
           indicator, facts,
           primal, dual, load, cell_size, send_v, face_cell, face_other, face_dir, hanging, stiffness, recon, traction,
           trace, p_t, first, last, before, after, after2, p_out, p_in, w_out, w_in, picked, padded, woven, families, rebuilt,
           operator, operator3, table, side_a, side_b0, side_b1, recon3, onehot, index_a, index_b, smem_a, smem_b, term, partial, returned, part, parts,
           in_sem, index_sem, edge_send, edge_recv, p_send, p_recv, w_send, w_recv, b_send, b_recv, r_send, r_recv):
    me = lax.axis_index("dom")
    staged = [(dual_in, dual), (primal_in, primal), (recon_in, recon.at[pl.ds(0, CHILD * DOF), :]), (traction_in, traction), (trace_in, trace),
              (load_in, load), (size_in, cell_size), (stiffness_in, stiffness), (cell_in, face_cell),
              (other_in, face_other), (dir_in, face_dir), (hanging_in, hanging), (send_in, send_v)]
    loads = {}
    for i, (source, to) in enumerate(staged):
        loads[i] = pltpu.make_async_copy(source, to, in_sem.at[i])
        loads[i].start()

    barrier = pltpu.get_barrier_semaphore()
    partners = [behind(me, shift) for shift in SHIFTS]
    for stride, size in STAGES:
        partners += [in_stage(me, stride, size, step) for step in range(1, size)]
    for partner in partners:
        pl.semaphore_signal(barrier, inc=1, device_id=(partner,), device_id_type=MESH)

    start, live, cells = counts_of(counts, me)
    head = lax.rem(CHILD - lax.rem(start, CHILD), CHILD)

    def remote(source, to, send_sem, recv_sem, target):
        return pltpu.make_async_remote_copy(src_ref=source, dst_ref=to, send_sem=send_sem, recv_sem=recv_sem,
                                            device_id=(target,), device_id_type=MESH)

    def list_copy(source, to, send_sem, recv_sem, k):
        return remote(source.at[k], to.at[k], send_sem.at[k], recv_sem.at[k], behind(me, shift_of(k)))

    loads[0].wait()
    cell = lax.broadcasted_iota(I32, (16, CELLS), 1)
    row = lax.broadcasted_iota(I32, (16, CELLS), 0)
    picked_cell = jnp.where(row < CHILD, row, live - 2 * CHILD + row)
    chosen = jnp.where(cell == picked_cell, 1.0, 0.0).astype(BF16)
    hi, lo = split(dual[...])
    ends = dot_nt(chosen, hi) + dot_nt(chosen, lo)
    first[...] = jnp.zeros((8, LANES), F32)
    last[...] = jnp.zeros((8, LANES), F32)
    first[:, :DOF] = ends[:CHILD]
    last[:, :DOF] = ends[CHILD:]
    pl.semaphore_wait(barrier, len(partners))
    edges = [remote(last, before, edge_send.at[0], edge_recv.at[0], behind(me, 1)),
             remote(first, after, edge_send.at[1], edge_recv.at[1], behind(me, -1))]
    for copy in edges:
        copy.start()

    loads[1].wait()

    def transpose_primal(step, carry):
        to_cell_major(p_t, 0, primal, step)
        rows = pl.ds(pl.multiple_of(step * 96, 96), 96)
        wide = jnp.concatenate([recon[rows, :], jnp.zeros((96, 768 - CHILD * DOF), F32)], 1)
        hi, lo = split(wide)
        recon3[rows, 0:768] = hi
        recon3[rows, 768:1536] = hi
        recon3[rows, 1536:2304] = lo
        return carry

    loads[2].wait()
    lax.fori_loop(0, 8, transpose_primal, 0)

    for i in range(3, len(staged)):
        loads[i].wait()
    fill_operator(operator, traction, trace)
    hi, lo = split(operator[...].T)
    operator3[0:256, :] = hi
    operator3[256:512, :] = hi
    operator3[512:768, :] = lo
    pair = (face_dir[...] // 2) * SLOTS
    index_a[...] = pair + face_cell[...]
    index_b[...] = pair + face_other[...]
    copy_a = pltpu.make_async_copy(index_a, smem_a, index_sem.at[0])
    copy_b = pltpu.make_async_copy(index_b, smem_b, index_sem.at[1])
    copy_a.start()
    copy_b.start()

    def send_primal(step, carry):
        k = lax.rem(step + FIRST_LIST, NEIGH)
        gather_list(picked, p_t, send, k)
        to_cell_major(padded, CHILD, dual, step)
        take_residual(load, primal, stiffness, step)
        onehot[:, pl.ds(pl.multiple_of(step * GHOST, GHOST), GHOST)] = low_onehot(send_v[pl.ds(step, 1), :])
        pack(p_out.at[k], picked)
        list_copy(p_out, p_in, p_send, p_recv, k).start()
        return carry

    lax.fori_loop(0, NEIGH, send_primal, 0)
    padded[CELLS + 8 :, :] = jnp.zeros((padded.shape[0] - CELLS - 8, LANES), F32)
    for copy in edges:
        copy.wait()
    padded[0:8, :] = before[...]
    rebuild(head, live, padded, after, after2, recon3, families, rebuilt, woven)

    def send_weight(step, carry):
        k = lax.rem(step + FIRST_LIST, NEIGH)
        at = pl.multiple_of(step * 256, 256)
        gather_rows(picked, 0, woven, lambda i: send[k, i] + (CHILD - head), GHOST)
        fill_table(table, at, p_t[pl.ds(at, 256), :], woven[pl.ds(CHILD - head + at, 256), :], operator3)
        cell_terms(term, load, woven, CHILD - head, cell_size, step)
        pack(w_out.at[k], picked)
        list_copy(w_out, w_in, w_send, w_recv, k).start()
        return carry

    lax.fori_loop(0, NEIGH, send_weight, 0)
    copy_a.wait()
    copy_b.wait()

    def take_ghosts(step, carry):
        k = lax.rem(step + FIRST_LIST, NEIGH)
        list_copy(p_out, p_in, p_send, p_recv, k).wait()
        list_copy(w_out, w_in, w_send, w_recv, k).wait()
        row = step * 6
        gather_rows(side_a, row * LANES, table, lambda i: smem_a[row + i // LANES, i % LANES], 512)
        fill_table(table, CELLS + k * GHOST, unpack(p_in[k]), unpack(w_in[k]), operator3)

        def rest(r, carry):
            gather_rows(side_a, r * LANES, table, lambda i: smem_a[r, i], LANES)
            return carry

        lax.fori_loop(row + 4, row + 6, rest, 0)
        return carry

    lax.fori_loop(0, NEIGH, take_ghosts, 0)

    lane = lax.broadcasted_iota(I32, (8, 2 * LANES), 1) % LANES
    sub = lax.broadcasted_iota(I32, (8, 2 * LANES), 0)
    pick = jnp.where(lane // 32 == sub, 1.0, 0.0).astype(BF16)
    upper = lax.broadcasted_iota(I32, (CHUNK, LANES), 1) % 64 >= 32

    def gather_b(to, c):
        gather_rows(to, 0, table, lambda i: smem_b[c * SPLIT + i // LANES, i % LANES], CHUNK)

    def raw_sums(side_b, c):
        a = side_a[pl.ds(pl.multiple_of(c * CHUNK, CHUNK), CHUNK), :]
        b = pltpu.roll(side_b[...], 64, 1)
        jump = pltpu.roll(a + b, 32, 1)
        hi, lo = split(jnp.where(upper, jump * a, pltpu.roll(jump * b, 96, 1)))
        return dot_nt(pick, jnp.concatenate([hi, lo], 1))

    def add_sums(raw, c, carry):
        sum_a, sum_b = carry
        face = c * CHUNK + lax.broadcasted_iota(I32, (1, CHUNK), 1)
        area = jnp.where(face < 3 * live, 0.5 * (1.0 - 0.75 * lanes_of(hanging, c).astype(F32)), 0.0)
        is_even = lanes_of(face_dir, c) % 2 == 0
        term_a = area * jnp.where(is_even, raw[1:2], raw[3:4])
        term_b = area * jnp.where(is_even, raw[0:1], raw[2:3])
        cell, other = lanes_of(face_cell, c), lanes_of(face_other, c)
        sum_a += scatter(cell, term_a, CELLS // LANES, low_onehot(cell))
        sum_b += scatter(other, term_b, SLOTS // LANES, low_onehot(other))
        return sum_a, sum_b

    def body(i, carry):
        raw_before, sums = carry
        gather_b(side_b1, 2 * i + 1)
        raw = raw_sums(side_b0, 2 * i)
        sums = add_sums(raw_before, jnp.maximum(2 * i - 1, 0), sums)
        gather_b(side_b0, jnp.minimum(2 * i + 2, CHUNKS - 1))
        raw_after = raw_sums(side_b1, 2 * i + 1)
        sums = add_sums(raw, 2 * i, sums)
        return raw_after, sums

    gather_b(side_b0, 0)
    zero = (jnp.zeros((CELLS // LANES, LANES), F32), jnp.zeros((SLOTS // LANES, LANES), F32))
    raw, sums = lax.fori_loop(0, CHUNKS // 2, body, (jnp.zeros((8, CHUNK), F32), zero))
    sum_a, sum_b = add_sums(raw, CHUNKS - 1, sums)
    for k in SEND_ORDER:
        at = CELLS // LANES + 2 * k
        partial[k] = sum_b[at : at + 2]
    backs = [remote(partial.at[k], returned.at[k], b_send, b_recv, behind(me, -SHIFTS[k])) for k in SEND_ORDER]
    for copy in backs:
        copy.start()
    index = jnp.concatenate([send_v[k : k + 1, :] for k in range(NEIGH)], 1)
    out = term[...] + sum_a + sum_b[: CELLS // LANES]
    remote(partial, returned, b_send, b_recv, behind(me, 1)).wait_recv()
    value = jnp.concatenate([returned[k, r : r + 1, :] for k in range(NEIGH) for r in range(2)], 1)
    out = out + scatter(index, value, CELLS // LANES, onehot[...])
    slot = lax.broadcasted_iota(I32, out.shape, 0) * LANES + lax.broadcasted_iota(I32, out.shape, 1)
    indicator[...] = out

    total = jnp.sum(jnp.where(slot < live, jnp.abs(out), 0.0), axis=0, keepdims=True)
    place = 0
    for stage, (stride, count) in enumerate(STAGES):
        part[stage] = total
        slots = pl.ds(place, count - 1)
        for step in range(1, count):
            remote(part.at[stage], parts.at[place + step - 1], r_send.at[stage], r_recv.at[stage],
                   in_stage(me, stride, count, step)).start()
        remote(parts.at[slots], parts.at[slots], r_send.at[stage], r_recv.at[stage], behind(me, 1)).wait_recv()
        total = total + jnp.sum(parts[place : place + count - 1], axis=0)
        place += count - 1

    mean = jnp.sum(total) / cells.astype(F32)
    facts[...] = jnp.where(slot < live, mean, -1.0)
    remote(partial, returned, b_send, b_recv, behind(me, 1)).wait_send()
    place = 0
    for stage, (stride, count) in enumerate(STAGES):
        slots = pl.ds(place, count - 1)
        remote(parts.at[slots], parts.at[slots], r_send.at[stage], r_recv.at[stage], behind(me, 1)).wait_send()
        place += count - 1


SMEM = pl.BlockSpec(memory_space=pltpu.SMEM)
VMEM = pl.BlockSpec(memory_space=pltpu.VMEM)
ANY = pl.BlockSpec(memory_space=pl.ANY)


def per_device(primal, dual, load, cell_size, cell_count, ghost_send, face_cell, face_other, face_dir, hanging,
               stiffness, recon, traction, trace):
    send = ghost_send[0]
    as_rows = lambda x: x.reshape(-1, LANES)
    f32 = lambda *shape: pltpu.VMEM(shape, F32)
    bf16 = lambda *shape: pltpu.VMEM(shape, BF16)
    i32 = lambda *shape: pltpu.VMEM(shape, I32)
    dma = lambda n: pltpu.SemaphoreType.DMA((n,))
    rows = FACES // LANES
    cells = CELLS // LANES
    steps = sum(size - 1 for _, size in STAGES)
    scratch = [
        f32(DOF, CELLS), f32(DOF, CELLS), f32(DOF, CELLS), f32(cells, LANES), i32(NEIGH, GHOST),
        i32(rows, LANES), i32(rows, LANES), i32(rows, LANES), i32(rows, LANES),
        f32(DOF, DOF), f32(768, CHILD * DOF), f32(6 * FACE_DOF, DOF), f32(6 * FACE_DOF, DOF),
        f32(CELLS, LANES),
        f32(8, LANES), f32(8, LANES), f32(8, LANES), f32(8, LANES), f32(16, LANES),
        f32(NEIGH, PACKED, LANES), f32(NEIGH, PACKED, LANES), f32(NEIGH, PACKED, LANES), f32(NEIGH, PACKED, LANES),
        f32(3 * THIRD, LANES),
        f32(FAMILIES * CHILD + 8, LANES), f32(FAMILIES * CHILD, LANES), f32(FAMILIES, 768), f32(FAMILIES, 768),
        f32(384, 256), bf16(768, 384), f32(3 * SLOTS, LANES), f32(FACES, LANES), f32(CHUNK, LANES), f32(CHUNK, LANES),
        bf16(768, 2304), bf16(LANES, GHOSTS),
        i32(rows, LANES), i32(rows, LANES), pltpu.SMEM((rows, LANES), I32), pltpu.SMEM((rows, LANES), I32),
        f32(cells, LANES), f32(NEIGH, 2, LANES), f32(NEIGH, 2, LANES), f32(len(STAGES), 1, LANES), f32(steps, 1, LANES),
        dma(13), dma(2), dma(2), dma(2), dma(NEIGH), dma(NEIGH), dma(NEIGH), dma(NEIGH),
        pltpu.SemaphoreType.DMA, pltpu.SemaphoreType.DMA, dma(len(STAGES)), dma(len(STAGES)),
    ]
    indicator, facts = pl.pallas_call(
        kernel,
        out_shape=[jax.ShapeDtypeStruct((cells, LANES), F32)] * 2,
        in_specs=[SMEM] * 2 + [ANY] * 13, out_specs=[VMEM] * 2, scratch_shapes=scratch,
        compiler_params=pltpu.CompilerParams(collective_id=0, has_side_effects=True,
                                             vmem_limit_bytes=56 * 1024 * 1024),
        name="indicators",
    )(cell_count, send, primal, dual, load, as_rows(cell_size), send, as_rows(face_cell), as_rows(face_other),
      as_rows(face_dir), as_rows(hanging), stiffness, recon, traction, trace)
    facts = facts.reshape(-1)
    indicator = jnp.where(facts < 0.0, 0.0, indicator.reshape(-1))
    return indicator, jnp.abs(indicator) / (jnp.abs(facts) + 1e-06)

def solution(mesh):
    in_specs = (P(None, "dom"), P(None, "dom"), P(None, "dom"), P("dom"), P(), P("dom", None, None), P("dom"), P("dom"),
                P("dom"), P("dom"), P(), P(), P(), P())
    return jax.shard_map(per_device, mesh=mesh, in_specs=in_specs, out_specs=(P("dom"), P("dom")), check_vma=False)
```

```python
import functools

import jax
import jax.numpy as jnp
from jax import lax
from jax.experimental import pallas as pl
from jax.experimental.pallas import tpu as pltpu
from jax.sharding import PartitionSpec as P

F32 = jnp.float32
BF16 = jnp.bfloat16
I32 = jnp.int32

DOF = 81
FACE_DOF = 27
CHILD = 8
CELLS = 2048
NEIGH = 8
GHOST = 256
GHOSTS = NEIGH * GHOST
SLOTS = CELLS + GHOSTS
FACES = 6144
LANES = 128
FAMILIES = 272
THIRD = 88
PACKED = 2 * THIRD
CHUNK = 256
CHUNKS = FACES // CHUNK
SPLIT = CHUNK // LANES


def split(x):
    high = x.astype(BF16)
    return high, (x - high.astype(F32)).astype(BF16)


def dot_nt(a, b):
    return lax.dot_general(a, b, (((1,), (1,)), ((), ())), preferred_element_type=F32)


def dot_nn(a, b):
    return lax.dot_general(a, b, (((1,), (0,)), ((), ())), preferred_element_type=F32)


def gather_rows(dst, dst_at, src, index_of, count):
    sub = lax.broadcasted_iota(I32, (8, LANES), 0)
    for base in range(0, count, 8):
        rows = [src[pl.ds(index_of(base + u), 1), :] for u in range(8)]
        tile = jnp.broadcast_to(rows[0], (8, LANES))
        for u in range(1, 8):
            tile = jnp.where(sub == u, jnp.broadcast_to(rows[u], (8, LANES)), tile)
        dst[pl.ds(pl.multiple_of(dst_at + base, 8), 8), :] = tile


def turned_block(src, at):
    return jnp.concatenate([src[:, pl.ds(at, 256)], jnp.zeros((LANES - DOF, 256), F32)], 0).T


def to_cell_major(dst, row, src, step):
    at = pl.multiple_of(step * 256, 256)
    dst[pl.ds(pl.multiple_of(row + at, CHILD), 256), :] = turned_block(src, at)


def pack(to, rows):
    lane = lax.broadcasted_iota(I32, (THIRD, LANES), 1)
    second = pltpu.roll(rows[THIRD : 2 * THIRD, :], DOF, 1)
    third = pltpu.roll(rows[2 * THIRD :, :], 2 * DOF - LANES, 1)
    upper = jnp.where(lane < DOF, rows[0:THIRD, :], second)
    to[...] = jnp.concatenate([upper, jnp.where(lane < 2 * DOF - LANES, second, third)], 0)


def unpack(rows):
    lane = lax.broadcasted_iota(I32, (THIRD, LANES), 1)
    upper, lower = rows[:THIRD], rows[THIRD:]
    second = pltpu.roll(jnp.where(lane < 2 * DOF - LANES, lower, upper), LANES - DOF, 1)
    third = pltpu.roll(lower, 2 * LANES - 2 * DOF, 1)
    return jnp.concatenate([upper, second, third[: GHOST - PACKED]], 0)


def fill_operator(operator, traction, trace):
    operator[...] = jnp.zeros(operator.shape, F32)
    for d in range(6):
        rows = slice(d * FACE_DOF, (d + 1) * FACE_DOF)
        operator[64 * d : 64 * d + FACE_DOF, 0:DOF] = traction[rows, :]
        operator[64 * d + 32 : 64 * d + 32 + FACE_DOF, LANES : LANES + DOF] = trace[rows, :]


def fill_table(table, slot, p_rows, w_rows, operator):
    hi, lo = split(jnp.concatenate([p_rows, w_rows], 1))
    out = dot_nn(jnp.concatenate([hi, lo, hi], 1), operator[...])
    for pair in range(3):
        table[pl.ds(pl.multiple_of(pair * SLOTS + slot, 256), 256), :] = out[:, pair * LANES : (pair + 1) * LANES]


def take_residual(load, primal, stiffness, step):
    cells = pl.ds(pl.multiple_of(step * 256, 256), 256)
    s_hi, s_lo = split(stiffness[...])
    p_hi, p_lo = split(primal[:, cells])
    load[:, cells] = load[:, cells] - (dot_nn(s_hi, p_hi) + dot_nn(s_lo, p_hi) + dot_nn(s_hi, p_lo))


def cell_terms(out, residual, woven, skip, cell_size, step):
    cells = pl.ds(pl.multiple_of(step * 256, 256), 256)
    total = jnp.sum(residual[:, cells] * woven[pl.ds(skip + step * 256, 256), :].T[:DOF, :], axis=0, keepdims=True)
    for r in range(2):
        i = step * 2 + r
        out[pl.ds(i, 1), :] = cell_size[pl.ds(i, 1), :] * total[:, r * LANES : (r + 1) * LANES]


def lanes_of(ref, chunk):
    return jnp.concatenate([ref[pl.ds(chunk * SPLIT + i, 1), :] for i in range(SPLIT)], 1)


def low_onehot(index):
    low = lax.broadcasted_iota(I32, (LANES, index.shape[1]), 0) == index % LANES
    return jnp.where(low, 1.0, 0.0).astype(BF16)


def scatter(index, value, high_count, onehot):
    high = lax.broadcasted_iota(I32, (high_count, index.shape[1]), 0) == index // LANES
    both = dot_nt(jnp.concatenate(split(jnp.where(high, value, 0.0)), 0), onehot)
    return both[:high_count] + both[high_count:]


MESH = pl.DeviceIdType.MESH
RANKS = 128
SHIFTS = [(1 << which // 2) * (1 - 2 * (which % 2)) for which in range(NEIGH)]
FIRST_LIST = 4
SEND_ORDER = [4, 5, 6, 7, 2, 3, 0, 1]
STAGES = ((1, 8), (8, 16))


def counts_of(counts, me):
    def body(i, carry):
        before, here, cells = carry
        c = counts[i]
        return before + jnp.where(i < me, c, 0), here + jnp.where(i == me, c, 0), cells + c

    return lax.fori_loop(0, RANKS, body, (jnp.int32(0), jnp.int32(0), jnp.int32(0)), unroll=32)


def behind(me, by):
    return lax.rem(me + (by + RANKS), RANKS)


def shift_of(k):
    e = k // 2
    power = 1 + e + e * (e - 1) // 2 + e * (e - 1) * (e - 2) // 6
    return power * (1 - 2 * (k % 2))


def in_stage(me, stride, size, step):
    place = lax.rem(me // stride, size)
    return me + (lax.rem(place + step, size) - place) * stride


def gather_list(picked, source, send, k):
    gather_rows(picked, 0, source, lambda i: send[k, i], GHOST)


def rebuild(head, live, padded, after, after2, recon3, families, rebuilt, woven):
    after2[0:8, :] = jnp.zeros((8, LANES), F32)
    after2[8:16, :] = after[...]
    own = lax.rem(live - head + CHILD, CHILD)
    split_family = 1 + (live - head) // CHILD
    row = lax.broadcasted_iota(I32, (FAMILIES, LANES), 0)
    families[:, 640:768] = jnp.zeros((FAMILIES, LANES), F32)
    for m in range(CHILD):
        cells = padded[pl.ds(head + m, FAMILIES, stride=CHILD), :]
        late = after2[pl.ds(CHILD + m - own, 1), :]
        cells = jnp.where((row == split_family) & (m >= own), late, cells)
        families[:, m * DOF : (m + 1) * DOF] = cells[:, :DOF]
    hi, lo = split(families[...])
    rebuilt[:, : CHILD * DOF] = dot_nt(jnp.concatenate([hi, lo, hi], 1), recon3[0 : CHILD * DOF, :])
    lane = lax.broadcasted_iota(I32, (FAMILIES, LANES), 1)
    for m in range(CHILD):
        part = rebuilt[:, m * DOF : m * DOF + LANES]
        woven[pl.ds(m, FAMILIES, stride=CHILD), :] = jnp.where(lane < DOF, part, 0.0)


def kernel(counts, send, primal_in, dual_in, load_in, size_in, send_in, cell_in, other_in, dir_in, hanging_in,
           stiffness_in, recon_in, traction_in, trace_in,
           indicator, facts,
           primal, dual, load, cell_size, send_v, face_cell, face_other, face_dir, hanging, stiffness, recon, traction,
           trace, p_t, first, last, before, after, after2, p_out, p_in, w_out, w_in, picked, padded, woven, families, rebuilt,
           operator, operator3, table, side_a, side_b0, side_b1, recon3, onehot, index_a, index_b, smem_a, smem_b, term, partial, returned, part, parts,
           in_sem, index_sem, edge_send, edge_recv, p_send, p_recv, w_send, w_recv, b_send, b_recv, r_send, r_recv):
    me = lax.axis_index("dom")
    staged = [(primal_in, primal), (dual_in, dual), (recon_in, recon.at[pl.ds(0, CHILD * DOF), :]), (traction_in, traction), (trace_in, trace),
              (load_in, load), (size_in, cell_size), (stiffness_in, stiffness), (cell_in, face_cell),
              (other_in, face_other), (dir_in, face_dir), (hanging_in, hanging), (send_in, send_v)]
    loads = {}
    for i, (source, to) in enumerate(staged):
        loads[i] = pltpu.make_async_copy(source, to, in_sem.at[i])
        loads[i].start()

    barrier = pltpu.get_barrier_semaphore()
    partners = [behind(me, shift) for shift in SHIFTS]
    for stride, size in STAGES:
        partners += [in_stage(me, stride, size, step) for step in range(1, size)]
    for partner in partners:
        pl.semaphore_signal(barrier, inc=1, device_id=(partner,), device_id_type=MESH)

    start, live, cells = counts_of(counts, me)
    head = lax.rem(CHILD - lax.rem(start, CHILD), CHILD)

    def remote(source, to, send_sem, recv_sem, target):
        return pltpu.make_async_remote_copy(src_ref=source, dst_ref=to, send_sem=send_sem, recv_sem=recv_sem,
                                            device_id=(target,), device_id_type=MESH)

    def list_copy(source, to, send_sem, recv_sem, k):
        return remote(source.at[k], to.at[k], send_sem.at[k], recv_sem.at[k], behind(me, shift_of(k)))

    def transpose_primal(step, carry):
        to_cell_major(p_t, 0, primal, step)
        return carry

    loads[0].wait()
    lax.fori_loop(0, 8, transpose_primal, 0)
    loads[1].wait()
    cell = lax.broadcasted_iota(I32, (16, CELLS), 1)
    row = lax.broadcasted_iota(I32, (16, CELLS), 0)
    picked_cell = jnp.where(row < CHILD, row, live - 2 * CHILD + row)
    chosen = jnp.where(cell == picked_cell, 1.0, 0.0).astype(BF16)
    hi, lo = split(dual[...])
    ends = dot_nt(chosen, hi) + dot_nt(chosen, lo)
    first[...] = jnp.zeros((8, LANES), F32)
    last[...] = jnp.zeros((8, LANES), F32)
    first[:, :DOF] = ends[:CHILD]
    last[:, :DOF] = ends[CHILD:]
    pl.semaphore_wait(barrier, len(partners))
    edges = [remote(last, before, edge_send.at[0], edge_recv.at[0], behind(me, 1)),
             remote(first, after, edge_send.at[1], edge_recv.at[1], behind(me, -1))]
    for copy in edges:
        copy.start()

    def send_primal(step, carry):
        k = lax.rem(step + FIRST_LIST, NEIGH)
        gather_list(picked, p_t, send, k)
        to_cell_major(padded, CHILD, dual, step)
        pack(p_out.at[k], picked)
        list_copy(p_out, p_in, p_send, p_recv, k).start()
        return carry

    lax.fori_loop(0, NEIGH, send_primal, 0)
    padded[CELLS + 8 :, :] = jnp.zeros((padded.shape[0] - CELLS - 8, LANES), F32)

    def split_recon(step, carry):
        rows = pl.ds(pl.multiple_of(step * 96, 96), 96)
        wide = jnp.concatenate([recon[rows, :], jnp.zeros((96, 768 - CHILD * DOF), F32)], 1)
        hi, lo = split(wide)
        recon3[rows, 0:768] = hi
        recon3[rows, 768:1536] = hi
        recon3[rows, 1536:2304] = lo
        return carry

    loads[2].wait()
    lax.fori_loop(0, 7, split_recon, 0)
    for i in range(3, len(staged)):
        loads[i].wait()
    fill_operator(operator, traction, trace)
    hi, lo = split(operator[...].T)
    operator3[0:256, :] = hi
    operator3[256:512, :] = hi
    operator3[512:768, :] = lo
    pair = (face_dir[...] // 2) * SLOTS
    index_a[...] = pair + face_cell[...]
    index_b[...] = pair + face_other[...]
    copy_a = pltpu.make_async_copy(index_a, smem_a, index_sem.at[0])
    copy_b = pltpu.make_async_copy(index_b, smem_b, index_sem.at[1])
    copy_a.start()
    copy_b.start()

    def residuals(step, carry):
        take_residual(load, primal, stiffness, step)
        return carry

    lax.fori_loop(0, 8, residuals, 0)
    for k in range(NEIGH):
        onehot[:, k * GHOST : (k + 1) * GHOST] = low_onehot(send_v[k : k + 1, :])
    for copy in edges:
        copy.wait()
    padded[0:8, :] = before[...]
    rebuild(head, live, padded, after, after2, recon3, families, rebuilt, woven)

    def send_weight(step, carry):
        k = lax.rem(step + FIRST_LIST, NEIGH)
        at = pl.multiple_of(step * 256, 256)
        gather_rows(picked, 0, woven, lambda i: send[k, i] + (CHILD - head), GHOST)
        fill_table(table, at, p_t[pl.ds(at, 256), :], woven[pl.ds(CHILD - head + at, 256), :], operator3)
        cell_terms(term, load, woven, CHILD - head, cell_size, step)
        pack(w_out.at[k], picked)
        list_copy(w_out, w_in, w_send, w_recv, k).start()
        return carry

    lax.fori_loop(0, NEIGH, send_weight, 0)
    copy_a.wait()
    copy_b.wait()

    def take_ghosts(step, carry):
        k = lax.rem(step + FIRST_LIST, NEIGH)
        list_copy(p_out, p_in, p_send, p_recv, k).wait()
        list_copy(w_out, w_in, w_send, w_recv, k).wait()
        row = step * 6
        gather_rows(side_a, row * LANES, table, lambda i: smem_a[row + i // LANES, i % LANES], 256)
        fill_table(table, CELLS + k * GHOST, unpack(p_in[k]), unpack(w_in[k]), operator3)

        def rest(r, carry):
            gather_rows(side_a, r * LANES, table, lambda i: smem_a[r, i], LANES)
            return carry

        lax.fori_loop(row + 2, row + 6, rest, 0)
        return carry

    lax.fori_loop(0, NEIGH, take_ghosts, 0)

    lane = lax.broadcasted_iota(I32, (8, 2 * LANES), 1) % LANES
    sub = lax.broadcasted_iota(I32, (8, 2 * LANES), 0)
    pick = jnp.where(lane // 32 == sub, 1.0, 0.0).astype(BF16)
    upper = lax.broadcasted_iota(I32, (CHUNK, LANES), 1) % 64 >= 32

    def gather_b(to, c):
        gather_rows(to, 0, table, lambda i: smem_b[c * SPLIT + i // LANES, i % LANES], CHUNK)

    def raw_sums(side_b, c):
        a = side_a[pl.ds(pl.multiple_of(c * CHUNK, CHUNK), CHUNK), :]
        b = pltpu.roll(side_b[...], 64, 1)
        jump = pltpu.roll(a + b, 32, 1)
        hi, lo = split(jnp.where(upper, jump * a, pltpu.roll(jump * b, 96, 1)))
        return dot_nt(pick, jnp.concatenate([hi, lo], 1))

    def add_sums(raw, c, carry):
        sum_a, sum_b = carry
        face = c * CHUNK + lax.broadcasted_iota(I32, (1, CHUNK), 1)
        area = jnp.where(face < 3 * live, 0.5 * (1.0 - 0.75 * lanes_of(hanging, c).astype(F32)), 0.0)
        is_even = lanes_of(face_dir, c) % 2 == 0
        term_a = area * jnp.where(is_even, raw[1:2], raw[3:4])
        term_b = area * jnp.where(is_even, raw[0:1], raw[2:3])
        cell, other = lanes_of(face_cell, c), lanes_of(face_other, c)
        sum_a += scatter(cell, term_a, CELLS // LANES, low_onehot(cell))
        sum_b += scatter(other, term_b, SLOTS // LANES, low_onehot(other))
        return sum_a, sum_b

    def body(i, carry):
        raw_before, sums = carry
        gather_b(side_b1, 2 * i + 1)
        raw = raw_sums(side_b0, 2 * i)
        sums = add_sums(raw_before, jnp.maximum(2 * i - 1, 0), sums)
        gather_b(side_b0, jnp.minimum(2 * i + 2, CHUNKS - 1))
        raw_after = raw_sums(side_b1, 2 * i + 1)
        sums = add_sums(raw, 2 * i, sums)
        return raw_after, sums

    gather_b(side_b0, 0)
    zero = (jnp.zeros((CELLS // LANES, LANES), F32), jnp.zeros((SLOTS // LANES, LANES), F32))
    raw, sums = lax.fori_loop(0, CHUNKS // 2, body, (jnp.zeros((8, CHUNK), F32), zero))
    sum_a, sum_b = add_sums(raw, CHUNKS - 1, sums)
    for k in SEND_ORDER:
        at = CELLS // LANES + 2 * k
        partial[k] = sum_b[at : at + 2]
    backs = [remote(partial.at[k], returned.at[k], b_send, b_recv, behind(me, -SHIFTS[k])) for k in SEND_ORDER]
    for copy in backs:
        copy.start()
    index = jnp.concatenate([send_v[k : k + 1, :] for k in range(NEIGH)], 1)
    out = term[...] + sum_a + sum_b[: CELLS // LANES]
    remote(partial, returned, b_send, b_recv, behind(me, 1)).wait_recv()
    value = jnp.concatenate([returned[k, r : r + 1, :] for k in range(NEIGH) for r in range(2)], 1)
    out = out + scatter(index, value, CELLS // LANES, onehot[...])
    slot = lax.broadcasted_iota(I32, out.shape, 0) * LANES + lax.broadcasted_iota(I32, out.shape, 1)
    indicator[...] = out

    total = jnp.sum(jnp.where(slot < live, jnp.abs(out), 0.0), axis=0, keepdims=True)
    place = 0
    for stage, (stride, count) in enumerate(STAGES):
        part[stage] = total
        slots = pl.ds(place, count - 1)
        for step in range(1, count):
            remote(part.at[stage], parts.at[place + step - 1], r_send.at[stage], r_recv.at[stage],
                   in_stage(me, stride, count, step)).start()
        remote(parts.at[slots], parts.at[slots], r_send.at[stage], r_recv.at[stage], behind(me, 1)).wait_recv()
        total = total + jnp.sum(parts[place : place + count - 1], axis=0)
        place += count - 1

    mean = jnp.sum(total) / cells.astype(F32)
    facts[...] = jnp.where(slot < live, mean, -1.0)
    remote(partial, returned, b_send, b_recv, behind(me, 1)).wait_send()
    place = 0
    for stage, (stride, count) in enumerate(STAGES):
        slots = pl.ds(place, count - 1)
        remote(parts.at[slots], parts.at[slots], r_send.at[stage], r_recv.at[stage], behind(me, 1)).wait_send()
        place += count - 1


SMEM = pl.BlockSpec(memory_space=pltpu.SMEM)
VMEM = pl.BlockSpec(memory_space=pltpu.VMEM)
ANY = pl.BlockSpec(memory_space=pl.ANY)


def per_device(primal, dual, load, cell_size, cell_count, ghost_send, face_cell, face_other, face_dir, hanging,
               stiffness, recon, traction, trace):
    send = ghost_send[0]
    as_rows = lambda x: x.reshape(-1, LANES)
    f32 = lambda *shape: pltpu.VMEM(shape, F32)
    bf16 = lambda *shape: pltpu.VMEM(shape, BF16)
    i32 = lambda *shape: pltpu.VMEM(shape, I32)
    dma = lambda n: pltpu.SemaphoreType.DMA((n,))
    rows = FACES // LANES
    cells = CELLS // LANES
    steps = sum(size - 1 for _, size in STAGES)
    scratch = [
        f32(DOF, CELLS), f32(DOF, CELLS), f32(DOF, CELLS), f32(cells, LANES), i32(NEIGH, GHOST),
        i32(rows, LANES), i32(rows, LANES), i32(rows, LANES), i32(rows, LANES),
        f32(DOF, DOF), f32(768, CHILD * DOF), f32(6 * FACE_DOF, DOF), f32(6 * FACE_DOF, DOF),
        f32(CELLS, LANES),
        f32(8, LANES), f32(8, LANES), f32(8, LANES), f32(8, LANES), f32(16, LANES),
        f32(NEIGH, PACKED, LANES), f32(NEIGH, PACKED, LANES), f32(NEIGH, PACKED, LANES), f32(NEIGH, PACKED, LANES),
        f32(3 * THIRD, LANES),
        f32(FAMILIES * CHILD + 8, LANES), f32(FAMILIES * CHILD, LANES), f32(FAMILIES, 768), f32(FAMILIES, 768),
        f32(384, 256), bf16(768, 384), f32(3 * SLOTS, LANES), f32(FACES, LANES), f32(CHUNK, LANES), f32(CHUNK, LANES),
        bf16(768, 2304), bf16(LANES, GHOSTS),
        i32(rows, LANES), i32(rows, LANES), pltpu.SMEM((rows, LANES), I32), pltpu.SMEM((rows, LANES), I32),
        f32(cells, LANES), f32(NEIGH, 2, LANES), f32(NEIGH, 2, LANES), f32(len(STAGES), 1, LANES), f32(steps, 1, LANES),
        dma(13), dma(2), dma(2), dma(2), dma(NEIGH), dma(NEIGH), dma(NEIGH), dma(NEIGH),
        pltpu.SemaphoreType.DMA, pltpu.SemaphoreType.DMA, dma(len(STAGES)), dma(len(STAGES)),
    ]
    indicator, facts = pl.pallas_call(
        kernel,
        out_shape=[jax.ShapeDtypeStruct((cells, LANES), F32)] * 2,
        in_specs=[SMEM] * 2 + [ANY] * 13, out_specs=[VMEM] * 2, scratch_shapes=scratch,
        compiler_params=pltpu.CompilerParams(collective_id=0, has_side_effects=True,
                                             vmem_limit_bytes=56 * 1024 * 1024),
        name="indicators",
    )(cell_count, send, primal, dual, load, as_rows(cell_size), send, as_rows(face_cell), as_rows(face_other),
      as_rows(face_dir), as_rows(hanging), stiffness, recon, traction, trace)
    facts = facts.reshape(-1)
    indicator = jnp.where(facts < 0.0, 0.0, indicator.reshape(-1))
    return indicator, jnp.abs(indicator) / (jnp.abs(facts) + 1e-06)

def solution(mesh):
    in_specs = (P(None, "dom"), P(None, "dom"), P(None, "dom"), P("dom"), P(), P("dom", None, None), P("dom"), P("dom"),
                P("dom"), P("dom"), P(), P(), P(), P())
    return jax.shard_map(per_device, mesh=mesh, in_specs=in_specs, out_specs=(P("dom"), P("dom")), check_vma=False)
```

```python
import functools

import jax
import jax.numpy as jnp
from jax import lax
from jax.experimental import pallas as pl
from jax.experimental.pallas import tpu as pltpu
from jax.sharding import PartitionSpec as P

F32 = jnp.float32
BF16 = jnp.bfloat16
I32 = jnp.int32

DOF = 81
FACE_DOF = 27
CHILD = 8
CELLS = 2048
NEIGH = 8
GHOST = 256
GHOSTS = NEIGH * GHOST
SLOTS = CELLS + GHOSTS
FACES = 6144
LANES = 128
FAMILIES = 272
THIRD = 88
PACKED = 2 * THIRD
CHUNK = 256
CHUNKS = FACES // CHUNK
SPLIT = CHUNK // LANES


def split(x):
    high = x.astype(BF16)
    return high, (x - high.astype(F32)).astype(BF16)


def dot_nt(a, b):
    return lax.dot_general(a, b, (((1,), (1,)), ((), ())), preferred_element_type=F32)


def dot_nn(a, b):
    return lax.dot_general(a, b, (((1,), (0,)), ((), ())), preferred_element_type=F32)


def gather_rows(dst, dst_at, src, index_of, count):
    sub = lax.broadcasted_iota(I32, (8, LANES), 0)
    for base in range(0, count, 8):
        rows = [src[pl.ds(index_of(base + u), 1), :] for u in range(8)]
        tile = jnp.broadcast_to(rows[0], (8, LANES))
        for u in range(1, 8):
            tile = jnp.where(sub == u, jnp.broadcast_to(rows[u], (8, LANES)), tile)
        dst[pl.ds(pl.multiple_of(dst_at + base, 8), 8), :] = tile


def turned_block(src, at):
    return jnp.concatenate([src[:, pl.ds(at, 256)], jnp.zeros((LANES - DOF, 256), F32)], 0).T


def to_cell_major(dst, row, src, step):
    at = pl.multiple_of(step * 256, 256)
    dst[pl.ds(pl.multiple_of(row + at, CHILD), 256), :] = turned_block(src, at)


def pack(to, rows):
    lane = lax.broadcasted_iota(I32, (THIRD, LANES), 1)
    second = pltpu.roll(rows[THIRD : 2 * THIRD, :], DOF, 1)
    third = pltpu.roll(rows[2 * THIRD :, :], 2 * DOF - LANES, 1)
    upper = jnp.where(lane < DOF, rows[0:THIRD, :], second)
    to[...] = jnp.concatenate([upper, jnp.where(lane < 2 * DOF - LANES, second, third)], 0)


def pack_halves(to, j, rows):
    lane = lax.broadcasted_iota(I32, (THIRD, LANES), 1)
    second = pltpu.roll(rows[THIRD : 2 * THIRD, :], DOF, 1)
    third = pltpu.roll(rows[2 * THIRD :, :], 2 * DOF - LANES, 1)
    to[j, 0] = jnp.where(lane < DOF, rows[0:THIRD, :], second)
    to[j, 1] = jnp.where(lane < 2 * DOF - LANES, second, third)


def unpack(rows):
    lane = lax.broadcasted_iota(I32, (THIRD, LANES), 1)
    upper, lower = rows[:THIRD], rows[THIRD:]
    second = pltpu.roll(jnp.where(lane < 2 * DOF - LANES, lower, upper), LANES - DOF, 1)
    third = pltpu.roll(lower, 2 * LANES - 2 * DOF, 1)
    return jnp.concatenate([upper, second, third[: GHOST - PACKED]], 0)


def fill_operator(operator, traction, trace):
    operator[...] = jnp.zeros(operator.shape, F32)
    for d in range(6):
        rows = slice(d * FACE_DOF, (d + 1) * FACE_DOF)
        operator[64 * d : 64 * d + FACE_DOF, 0:DOF] = traction[rows, :]
        operator[64 * d + 32 : 64 * d + 32 + FACE_DOF, LANES : LANES + DOF] = trace[rows, :]


def fill_table(table, slot, p_rows, w_rows, operator):
    hi, lo = split(jnp.concatenate([p_rows, w_rows], 1))
    out = dot_nn(jnp.concatenate([hi, lo, hi], 1), operator[...])
    for pair in range(3):
        table[pl.ds(pl.multiple_of(pair * SLOTS + slot, 256), 256), :] = out[:, pair * LANES : (pair + 1) * LANES]


def take_residual(load, primal, stiffness, step):
    cells = pl.ds(pl.multiple_of(step * 256, 256), 256)
    s_hi, s_lo = split(stiffness[...])
    p_hi, p_lo = split(primal[:, cells])
    load[:, cells] = load[:, cells] - (dot_nn(s_hi, p_hi) + dot_nn(s_lo, p_hi) + dot_nn(s_hi, p_lo))


def cell_terms(out, residual, woven, skip, cell_size, step):
    cells = pl.ds(pl.multiple_of(step * 256, 256), 256)
    total = jnp.sum(residual[:, cells] * woven[pl.ds(skip + step * 256, 256), :].T[:DOF, :], axis=0, keepdims=True)
    for r in range(2):
        i = step * 2 + r
        out[pl.ds(i, 1), :] = cell_size[pl.ds(i, 1), :] * total[:, r * LANES : (r + 1) * LANES]


def lanes_of(ref, chunk):
    return jnp.concatenate([ref[pl.ds(chunk * SPLIT + i, 1), :] for i in range(SPLIT)], 1)


def low_onehot(index):
    low = lax.broadcasted_iota(I32, (LANES, index.shape[1]), 0) == index % LANES
    return jnp.where(low, 1.0, 0.0).astype(BF16)


def scatter(index, value, high_count, onehot):
    high = lax.broadcasted_iota(I32, (high_count, index.shape[1]), 0) == index // LANES
    both = dot_nt(jnp.concatenate(split(jnp.where(high, value, 0.0)), 0), onehot)
    return both[:high_count] + both[high_count:]


MESH = pl.DeviceIdType.MESH
RANKS = 128
SHIFTS = [(1 << which // 2) * (1 - 2 * (which % 2)) for which in range(NEIGH)]
FIRST_LIST = 4
FAR = (4, 5)
SEND_ORDER = [4, 5, 6, 7, 2, 3, 0, 1]
STAGES = ((1, 8), (8, 16))


def counts_of(counts, me):
    def body(i, carry):
        before, here, cells = carry
        c = counts[i]
        return before + jnp.where(i < me, c, 0), here + jnp.where(i == me, c, 0), cells + c

    return lax.fori_loop(0, RANKS, body, (jnp.int32(0), jnp.int32(0), jnp.int32(0)), unroll=32)


def behind(me, by):
    return lax.rem(me + (by + RANKS), RANKS)


def beside(me, way):
    return in_stage(me, 2, 4, 1 + 2 * way)


def shift_of(k):
    e = k // 2
    power = 1 + e + e * (e - 1) // 2 + e * (e - 1) * (e - 2) // 6
    return power * (1 - 2 * (k % 2))


def in_stage(me, stride, size, step):
    place = lax.rem(me // stride, size)
    return me + (lax.rem(place + step, size) - place) * stride


def gather_list(picked, source, send, k):
    gather_rows(picked, 0, source, lambda i: send[k, i], GHOST)


def rebuild(head, live, padded, after, after2, recon3, families, rebuilt, woven):
    after2[0:8, :] = jnp.zeros((8, LANES), F32)
    after2[8:16, :] = after[...]
    own = lax.rem(live - head + CHILD, CHILD)
    split_family = 1 + (live - head) // CHILD
    row = lax.broadcasted_iota(I32, (FAMILIES, LANES), 0)
    families[:, 640:768] = jnp.zeros((FAMILIES, LANES), F32)
    for m in range(CHILD):
        cells = padded[pl.ds(head + m, FAMILIES, stride=CHILD), :]
        late = after2[pl.ds(CHILD + m - own, 1), :]
        cells = jnp.where((row == split_family) & (m >= own), late, cells)
        families[:, m * DOF : (m + 1) * DOF] = cells[:, :DOF]
    hi, lo = split(families[...])
    rebuilt[:, : CHILD * DOF] = dot_nt(jnp.concatenate([hi, lo, hi], 1), recon3[0 : CHILD * DOF, :])
    lane = lax.broadcasted_iota(I32, (FAMILIES, LANES), 1)
    for m in range(CHILD):
        part = rebuilt[:, m * DOF : m * DOF + LANES]
        woven[pl.ds(m, FAMILIES, stride=CHILD), :] = jnp.where(lane < DOF, part, 0.0)


def kernel(counts, send, primal_in, dual_in, load_in, size_in, send_in, cell_in, other_in, dir_in, hanging_in,
           stiffness_in, recon_in, traction_in, trace_in,
           indicator, facts,
           primal, dual, load, cell_size, send_v, face_cell, face_other, face_dir, hanging, stiffness, recon, traction,
           trace, p_t, first, last, before, after, after2, p_out, p_in, w_out, w_in, far_p, far_p_mid, far_p_in, far_w, far_w_mid, far_w_in, far_sem, picked, padded, woven, families, rebuilt,
           operator, operator3, table, side_a, side_b0, side_b1, recon3, onehot, index_a, index_b, smem_a, smem_b, term, partial, returned, part, parts,
           in_sem, index_sem, edge_send, edge_recv, p_send, p_recv, w_send, w_recv, b_send, b_recv, r_send, r_recv):
    me = lax.axis_index("dom")
    staged = [(primal_in, primal), (dual_in, dual), (recon_in, recon.at[pl.ds(0, CHILD * DOF), :]), (traction_in, traction), (trace_in, trace),
              (load_in, load), (size_in, cell_size), (stiffness_in, stiffness), (cell_in, face_cell),
              (other_in, face_other), (dir_in, face_dir), (hanging_in, hanging), (send_in, send_v)]
    loads = {}
    for i, (source, to) in enumerate(staged):
        loads[i] = pltpu.make_async_copy(source, to, in_sem.at[i])
        loads[i].start()

    barrier = pltpu.get_barrier_semaphore()
    partners = [behind(me, shift) for shift in SHIFTS]
    partners += [beside(behind(me, -SHIFTS[k]), way) for k in FAR for way in range(2)]
    for stride, size in STAGES:
        partners += [in_stage(me, stride, size, step) for step in range(1, size)]
    for partner in partners:
        pl.semaphore_signal(barrier, inc=1, device_id=(partner,), device_id_type=MESH)

    start, live, cells = counts_of(counts, me)
    head = lax.rem(CHILD - lax.rem(start, CHILD), CHILD)

    def remote(source, to, send_sem, recv_sem, target):
        return pltpu.make_async_remote_copy(src_ref=source, dst_ref=to, send_sem=send_sem, recv_sem=recv_sem,
                                            device_id=(target,), device_id_type=MESH)

    def list_copy(source, to, send_sem, recv_sem, k):
        return remote(source.at[k], to.at[k], send_sem.at[k], recv_sem.at[k], behind(me, shift_of(k)))

    def far_first(field, j):
        out, mid = ((far_p, far_p_mid), (far_w, far_w_mid))[field]
        return [remote(out.at[j, way], mid.at[j, way], far_sem.at[field, 0, j, way], far_sem.at[field, 1, j, way],
                       beside(me, way)) for way in range(2)]

    def far_second(field, j):
        mid, to = ((far_p_mid, far_p_in), (far_w_mid, far_w_in))[field]
        return [remote(mid.at[j, way], to.at[j, way], far_sem.at[field, 2, j, way], far_sem.at[field, 3, j, way],
                       behind(beside(me, 1 - way), SHIFTS[FAR[j]])) for way in range(2)]

    def pass_on(field):
        for j in range(len(FAR)):
            for first_leg, second_leg in zip(far_first(field, j), far_second(field, j)):
                first_leg.wait()
                second_leg.start()

    def transpose_primal(step, carry):
        to_cell_major(p_t, 0, primal, step)
        return carry

    loads[0].wait()
    lax.fori_loop(0, 8, transpose_primal, 0)
    loads[1].wait()
    cell = lax.broadcasted_iota(I32, (16, CELLS), 1)
    row = lax.broadcasted_iota(I32, (16, CELLS), 0)
    picked_cell = jnp.where(row < CHILD, row, live - 2 * CHILD + row)
    chosen = jnp.where(cell == picked_cell, 1.0, 0.0).astype(BF16)
    hi, lo = split(dual[...])
    ends = dot_nt(chosen, hi) + dot_nt(chosen, lo)
    first[...] = jnp.zeros((8, LANES), F32)
    last[...] = jnp.zeros((8, LANES), F32)
    first[:, :DOF] = ends[:CHILD]
    last[:, :DOF] = ends[CHILD:]
    pl.semaphore_wait(barrier, len(partners))
    edges = [remote(last, before, edge_send.at[0], edge_recv.at[0], behind(me, 1)),
             remote(first, after, edge_send.at[1], edge_recv.at[1], behind(me, -1))]
    for copy in edges:
        copy.start()

    for j, k in enumerate(FAR):
        gather_list(picked, p_t, send, k)
        to_cell_major(padded, CHILD, dual, j)
        pack_halves(far_p, j, picked)
        for copy in far_first(0, j):
            copy.start()

    def send_primal(step, carry):
        k = lax.rem(step + FIRST_LIST, NEIGH)
        gather_list(picked, p_t, send, k)
        to_cell_major(padded, CHILD, dual, step)
        pack(p_out.at[k], picked)
        list_copy(p_out, p_in, p_send, p_recv, k).start()
        return carry

    lax.fori_loop(len(FAR), NEIGH, send_primal, 0)
    pass_on(0)
    padded[CELLS + 8 :, :] = jnp.zeros((padded.shape[0] - CELLS - 8, LANES), F32)

    def split_recon(step, carry):
        rows = pl.ds(pl.multiple_of(step * 96, 96), 96)
        wide = jnp.concatenate([recon[rows, :], jnp.zeros((96, 768 - CHILD * DOF), F32)], 1)
        hi, lo = split(wide)
        recon3[rows, 0:768] = hi
        recon3[rows, 768:1536] = hi
        recon3[rows, 1536:2304] = lo
        return carry

    loads[2].wait()
    lax.fori_loop(0, 7, split_recon, 0)
    for i in range(3, len(staged)):
        loads[i].wait()
    fill_operator(operator, traction, trace)
    hi, lo = split(operator[...].T)
    operator3[0:256, :] = hi
    operator3[256:512, :] = hi
    operator3[512:768, :] = lo
    pair = (face_dir[...] // 2) * SLOTS
    index_a[...] = pair + face_cell[...]
    index_b[...] = pair + face_other[...]
    copy_a = pltpu.make_async_copy(index_a, smem_a, index_sem.at[0])
    copy_b = pltpu.make_async_copy(index_b, smem_b, index_sem.at[1])
    copy_a.start()
    copy_b.start()

    def residuals(step, carry):
        take_residual(load, primal, stiffness, step)
        return carry

    lax.fori_loop(0, 8, residuals, 0)
    for k in range(NEIGH):
        onehot[:, k * GHOST : (k + 1) * GHOST] = low_onehot(send_v[k : k + 1, :])
    for copy in edges:
        copy.wait()
    padded[0:8, :] = before[...]
    rebuild(head, live, padded, after, after2, recon3, families, rebuilt, woven)

    def local_part(step):
        at = pl.multiple_of(step * 256, 256)
        fill_table(table, at, p_t[pl.ds(at, 256), :], woven[pl.ds(CHILD - head + at, 256), :], operator3)
        cell_terms(term, load, woven, CHILD - head, cell_size, step)

    for j, k in enumerate(FAR):
        gather_rows(picked, 0, woven, lambda i: send[k, i] + (CHILD - head), GHOST)
        pack_halves(far_w, j, picked)
        for copy in far_first(1, j):
            copy.start()
        local_part(jnp.int32(j))

    def send_weight(step, carry):
        k = lax.rem(step + FIRST_LIST, NEIGH)
        gather_rows(picked, 0, woven, lambda i: send[k, i] + (CHILD - head), GHOST)
        local_part(step)
        pack(w_out.at[k], picked)
        list_copy(w_out, w_in, w_send, w_recv, k).start()
        return carry

    lax.fori_loop(len(FAR), NEIGH, send_weight, 0)
    pass_on(1)
    copy_a.wait()
    copy_b.wait()

    def take_list(step, k, p_rows, w_rows):
        row = step * 6
        gather_rows(side_a, row * LANES, table, lambda i: smem_a[row + i // LANES, i % LANES], 256)
        fill_table(table, CELLS + k * GHOST, unpack(p_rows), unpack(w_rows), operator3)

        def rest(r, carry):
            gather_rows(side_a, r * LANES, table, lambda i: smem_a[r, i], LANES)
            return carry

        lax.fori_loop(row + 2, row + 6, rest, 0)

    def take_ghosts(step, carry):
        k = lax.rem(step + FIRST_LIST + len(FAR), NEIGH)
        list_copy(p_out, p_in, p_send, p_recv, k).wait()
        list_copy(w_out, w_in, w_send, w_recv, k).wait()
        take_list(step, k, p_in[k], w_in[k])
        return carry

    lax.fori_loop(0, NEIGH - len(FAR), take_ghosts, 0)
    for j, k in enumerate(FAR):
        for field in range(2):
            for copy in far_second(field, j):
                copy.wait()
        take_list(jnp.int32(NEIGH - len(FAR) + j), k, jnp.concatenate([far_p_in[j, 0], far_p_in[j, 1]], 0),
                  jnp.concatenate([far_w_in[j, 0], far_w_in[j, 1]], 0))

    lane = lax.broadcasted_iota(I32, (8, 2 * LANES), 1) % LANES
    sub = lax.broadcasted_iota(I32, (8, 2 * LANES), 0)
    pick = jnp.where(lane // 32 == sub, 1.0, 0.0).astype(BF16)
    upper = lax.broadcasted_iota(I32, (CHUNK, LANES), 1) % 64 >= 32

    def gather_b(to, c):
        gather_rows(to, 0, table, lambda i: smem_b[c * SPLIT + i // LANES, i % LANES], CHUNK)

    def raw_sums(side_b, c):
        a = side_a[pl.ds(pl.multiple_of(c * CHUNK, CHUNK), CHUNK), :]
        b = pltpu.roll(side_b[...], 64, 1)
        jump = pltpu.roll(a + b, 32, 1)
        hi, lo = split(jnp.where(upper, jump * a, pltpu.roll(jump * b, 96, 1)))
        return dot_nt(pick, jnp.concatenate([hi, lo], 1))

    def add_sums(raw, c, carry):
        sum_a, sum_b = carry
        face = c * CHUNK + lax.broadcasted_iota(I32, (1, CHUNK), 1)
        area = jnp.where(face < 3 * live, 0.5 * (1.0 - 0.75 * lanes_of(hanging, c).astype(F32)), 0.0)
        is_even = lanes_of(face_dir, c) % 2 == 0
        term_a = area * jnp.where(is_even, raw[1:2], raw[3:4])
        term_b = area * jnp.where(is_even, raw[0:1], raw[2:3])
        cell, other = lanes_of(face_cell, c), lanes_of(face_other, c)
        sum_a += scatter(cell, term_a, CELLS // LANES, low_onehot(cell))
        sum_b += scatter(other, term_b, SLOTS // LANES, low_onehot(other))
        return sum_a, sum_b

    def body(i, carry):
        raw_before, sums = carry
        gather_b(side_b1, 2 * i + 1)
        raw = raw_sums(side_b0, 2 * i)
        sums = add_sums(raw_before, jnp.maximum(2 * i - 1, 0), sums)
        gather_b(side_b0, jnp.minimum(2 * i + 2, CHUNKS - 1))
        raw_after = raw_sums(side_b1, 2 * i + 1)
        sums = add_sums(raw, 2 * i, sums)
        return raw_after, sums

    gather_b(side_b0, 0)
    zero = (jnp.zeros((CELLS // LANES, LANES), F32), jnp.zeros((SLOTS // LANES, LANES), F32))
    raw, sums = lax.fori_loop(0, CHUNKS // 2, body, (jnp.zeros((8, CHUNK), F32), zero))
    sum_a, sum_b = add_sums(raw, CHUNKS - 1, sums)
    for k in SEND_ORDER:
        at = CELLS // LANES + 2 * k
        partial[k] = sum_b[at : at + 2]
    backs = [remote(partial.at[k], returned.at[k], b_send, b_recv, behind(me, -SHIFTS[k])) for k in SEND_ORDER]
    for copy in backs:
        copy.start()
    index = jnp.concatenate([send_v[k : k + 1, :] for k in range(NEIGH)], 1)
    out = term[...] + sum_a + sum_b[: CELLS // LANES]
    remote(partial, returned, b_send, b_recv, behind(me, 1)).wait_recv()
    value = jnp.concatenate([returned[k, r : r + 1, :] for k in range(NEIGH) for r in range(2)], 1)
    out = out + scatter(index, value, CELLS // LANES, onehot[...])
    slot = lax.broadcasted_iota(I32, out.shape, 0) * LANES + lax.broadcasted_iota(I32, out.shape, 1)
    indicator[...] = out

    total = jnp.sum(jnp.where(slot < live, jnp.abs(out), 0.0), axis=0, keepdims=True)
    place = 0
    for stage, (stride, count) in enumerate(STAGES):
        part[stage] = total
        slots = pl.ds(place, count - 1)
        for step in range(1, count):
            remote(part.at[stage], parts.at[place + step - 1], r_send.at[stage], r_recv.at[stage],
                   in_stage(me, stride, count, step)).start()
        remote(parts.at[slots], parts.at[slots], r_send.at[stage], r_recv.at[stage], behind(me, 1)).wait_recv()
        total = total + jnp.sum(parts[place : place + count - 1], axis=0)
        place += count - 1

    mean = jnp.sum(total) / cells.astype(F32)
    facts[...] = jnp.where(slot < live, mean, -1.0)
    remote(partial, returned, b_send, b_recv, behind(me, 1)).wait_send()
    place = 0
    for stage, (stride, count) in enumerate(STAGES):
        slots = pl.ds(place, count - 1)
        remote(parts.at[slots], parts.at[slots], r_send.at[stage], r_recv.at[stage], behind(me, 1)).wait_send()
        place += count - 1


SMEM = pl.BlockSpec(memory_space=pltpu.SMEM)
VMEM = pl.BlockSpec(memory_space=pltpu.VMEM)
ANY = pl.BlockSpec(memory_space=pl.ANY)


def per_device(primal, dual, load, cell_size, cell_count, ghost_send, face_cell, face_other, face_dir, hanging,
               stiffness, recon, traction, trace):
    send = ghost_send[0]
    as_rows = lambda x: x.reshape(-1, LANES)
    f32 = lambda *shape: pltpu.VMEM(shape, F32)
    bf16 = lambda *shape: pltpu.VMEM(shape, BF16)
    i32 = lambda *shape: pltpu.VMEM(shape, I32)
    dma = lambda n: pltpu.SemaphoreType.DMA((n,))
    rows = FACES // LANES
    cells = CELLS // LANES
    steps = sum(size - 1 for _, size in STAGES)
    scratch = [
        f32(DOF, CELLS), f32(DOF, CELLS), f32(DOF, CELLS), f32(cells, LANES), i32(NEIGH, GHOST),
        i32(rows, LANES), i32(rows, LANES), i32(rows, LANES), i32(rows, LANES),
        f32(DOF, DOF), f32(768, CHILD * DOF), f32(6 * FACE_DOF, DOF), f32(6 * FACE_DOF, DOF),
        f32(CELLS, LANES),
        f32(8, LANES), f32(8, LANES), f32(8, LANES), f32(8, LANES), f32(16, LANES),
        f32(NEIGH, PACKED, LANES), f32(NEIGH, PACKED, LANES), f32(NEIGH, PACKED, LANES), f32(NEIGH, PACKED, LANES),
        *[f32(len(FAR), 2, THIRD, LANES)] * 6, pltpu.SemaphoreType.DMA((2, 4, len(FAR), 2)),
        f32(3 * THIRD, LANES),
        f32(FAMILIES * CHILD + 8, LANES), f32(FAMILIES * CHILD, LANES), f32(FAMILIES, 768), f32(FAMILIES, 768),
        f32(384, 256), bf16(768, 384), f32(3 * SLOTS, LANES), f32(FACES, LANES), f32(CHUNK, LANES), f32(CHUNK, LANES),
        bf16(768, 2304), bf16(LANES, GHOSTS),
        i32(rows, LANES), i32(rows, LANES), pltpu.SMEM((rows, LANES), I32), pltpu.SMEM((rows, LANES), I32),
        f32(cells, LANES), f32(NEIGH, 2, LANES), f32(NEIGH, 2, LANES), f32(len(STAGES), 1, LANES), f32(steps, 1, LANES),
        dma(13), dma(2), dma(2), dma(2), dma(NEIGH), dma(NEIGH), dma(NEIGH), dma(NEIGH),
        pltpu.SemaphoreType.DMA, pltpu.SemaphoreType.DMA, dma(len(STAGES)), dma(len(STAGES)),
    ]
    indicator, facts = pl.pallas_call(
        kernel,
        out_shape=[jax.ShapeDtypeStruct((cells, LANES), F32)] * 2,
        in_specs=[SMEM] * 2 + [ANY] * 13, out_specs=[VMEM] * 2, scratch_shapes=scratch,
        compiler_params=pltpu.CompilerParams(collective_id=0, has_side_effects=True,
                                             vmem_limit_bytes=56 * 1024 * 1024),
        name="indicators",
    )(cell_count, send, primal, dual, load, as_rows(cell_size), send, as_rows(face_cell), as_rows(face_other),
      as_rows(face_dir), as_rows(hanging), stiffness, recon, traction, trace)
    facts = facts.reshape(-1)
    indicator = jnp.where(facts < 0.0, 0.0, indicator.reshape(-1))
    return indicator, jnp.abs(indicator) / (jnp.abs(facts) + 1e-06)

def solution(mesh):
    in_specs = (P(None, "dom"), P(None, "dom"), P(None, "dom"), P("dom"), P(), P("dom", None, None), P("dom"), P("dom"),
                P("dom"), P("dom"), P(), P(), P(), P())
    return jax.shard_map(per_device, mesh=mesh, in_specs=in_specs, out_specs=(P("dom"), P("dom")), check_vma=False)
```

```python
import functools

import jax
import jax.numpy as jnp
from jax import lax
from jax.experimental import pallas as pl
from jax.experimental.pallas import tpu as pltpu
from jax.sharding import PartitionSpec as P

F32 = jnp.float32
BF16 = jnp.bfloat16
I32 = jnp.int32

DOF = 81
FACE_DOF = 27
CHILD = 8
CELLS = 2048
NEIGH = 8
GHOST = 256
GHOSTS = NEIGH * GHOST
SLOTS = CELLS + GHOSTS
FACES = 6144
LANES = 128
FAMILIES = 272
THIRD = 88
PACKED = 2 * THIRD
CHUNK = 256
CHUNKS = FACES // CHUNK
SPLIT = CHUNK // LANES


def split(x):
    high = x.astype(BF16)
    return high, (x - high.astype(F32)).astype(BF16)


def dot_nt(a, b):
    return lax.dot_general(a, b, (((1,), (1,)), ((), ())), preferred_element_type=F32)


def dot_nn(a, b):
    return lax.dot_general(a, b, (((1,), (0,)), ((), ())), preferred_element_type=F32)


def gather_rows(dst, dst_at, src, index_of, count):
    sub = lax.broadcasted_iota(I32, (8, LANES), 0)
    for base in range(0, count, 8):
        rows = [src[pl.ds(index_of(base + u), 1), :] for u in range(8)]
        tile = jnp.broadcast_to(rows[0], (8, LANES))
        for u in range(1, 8):
            tile = jnp.where(sub == u, jnp.broadcast_to(rows[u], (8, LANES)), tile)
        dst[pl.ds(pl.multiple_of(dst_at + base, 8), 8), :] = tile


def turned_block(src, at):
    return jnp.concatenate([src[:, pl.ds(at, 256)], jnp.zeros((LANES - DOF, 256), F32)], 0).T


def to_cell_major(dst, row, src, step):
    at = pl.multiple_of(step * 256, 256)
    dst[pl.ds(pl.multiple_of(row + at, CHILD), 256), :] = turned_block(src, at)


def pack(to, rows):
    lane = lax.broadcasted_iota(I32, (THIRD, LANES), 1)
    second = pltpu.roll(rows[THIRD : 2 * THIRD, :], DOF, 1)
    third = pltpu.roll(rows[2 * THIRD :, :], 2 * DOF - LANES, 1)
    upper = jnp.where(lane < DOF, rows[0:THIRD, :], second)
    to[...] = jnp.concatenate([upper, jnp.where(lane < 2 * DOF - LANES, second, third)], 0)


def unpack(rows):
    lane = lax.broadcasted_iota(I32, (THIRD, LANES), 1)
    upper, lower = rows[:THIRD], rows[THIRD:]
    second = pltpu.roll(jnp.where(lane < 2 * DOF - LANES, lower, upper), LANES - DOF, 1)
    third = pltpu.roll(lower, 2 * LANES - 2 * DOF, 1)
    return jnp.concatenate([upper, second, third[: GHOST - PACKED]], 0)


def fill_operator(operator, traction, trace):
    operator[...] = jnp.zeros(operator.shape, F32)
    for d in range(6):
        rows = slice(d * FACE_DOF, (d + 1) * FACE_DOF)
        operator[64 * d : 64 * d + FACE_DOF, 0:DOF] = traction[rows, :]
        operator[64 * d + 32 : 64 * d + 32 + FACE_DOF, LANES : LANES + DOF] = trace[rows, :]


def fill_table(table, slot, p_rows, w_rows, operator):
    hi, lo = split(jnp.concatenate([p_rows, w_rows], 1))
    out = dot_nn(jnp.concatenate([hi, lo, hi], 1), operator[...])
    for pair in range(3):
        table[pl.ds(pl.multiple_of(pair * SLOTS + slot, 256), 256), :] = out[:, pair * LANES : (pair + 1) * LANES]


def take_residual(load, primal, stiffness, step):
    cells = pl.ds(pl.multiple_of(step * 256, 256), 256)
    s_hi, s_lo = split(stiffness[...])
    p_hi, p_lo = split(primal[:, cells])
    load[:, cells] = load[:, cells] - (dot_nn(s_hi, p_hi) + dot_nn(s_lo, p_hi) + dot_nn(s_hi, p_lo))


def cell_terms(out, residual, woven, skip, cell_size, step):
    cells = pl.ds(pl.multiple_of(step * 256, 256), 256)
    total = jnp.sum(residual[:, cells] * woven[pl.ds(skip + step * 256, 256), :].T[:DOF, :], axis=0, keepdims=True)
    for r in range(2):
        i = step * 2 + r
        out[pl.ds(i, 1), :] = cell_size[pl.ds(i, 1), :] * total[:, r * LANES : (r + 1) * LANES]


def lanes_of(ref, chunk):
    return jnp.concatenate([ref[pl.ds(chunk * SPLIT + i, 1), :] for i in range(SPLIT)], 1)


def low_onehot(index):
    low = lax.broadcasted_iota(I32, (LANES, index.shape[1]), 0) == index % LANES
    return jnp.where(low, 1.0, 0.0).astype(BF16)


def scatter(index, value, high_count, onehot):
    high = lax.broadcasted_iota(I32, (high_count, index.shape[1]), 0) == index // LANES
    both = dot_nt(jnp.concatenate(split(jnp.where(high, value, 0.0)), 0), onehot)
    return both[:high_count] + both[high_count:]


MESH = pl.DeviceIdType.MESH
RANKS = 128
SHIFTS = [(1 << which // 2) * (1 - 2 * (which % 2)) for which in range(NEIGH)]
FIRST_LIST = 4
LATE = 2
EARLY = FACES // LANES - NEIGH * LATE
SEND_ORDER = [4, 5, 6, 7, 2, 3, 0, 1]
STAGES = ((1, 8), (8, 16))


def counts_of(counts, me):
    def body(i, carry):
        before, here, cells = carry
        c = counts[i]
        return before + jnp.where(i < me, c, 0), here + jnp.where(i == me, c, 0), cells + c

    return lax.fori_loop(0, RANKS, body, (jnp.int32(0), jnp.int32(0), jnp.int32(0)), unroll=32)


def behind(me, by):
    return lax.rem(me + (by + RANKS), RANKS)


def shift_of(k):
    e = k // 2
    power = 1 + e + e * (e - 1) // 2 + e * (e - 1) * (e - 2) // 6
    return power * (1 - 2 * (k % 2))


def in_stage(me, stride, size, step):
    place = lax.rem(me // stride, size)
    return me + (lax.rem(place + step, size) - place) * stride


def gather_list(picked, source, send, k):
    gather_rows(picked, 0, source, lambda i: send[k, i], GHOST)


def rebuild(head, live, padded, after, after2, recon3, families, rebuilt, woven):
    after2[0:8, :] = jnp.zeros((8, LANES), F32)
    after2[8:16, :] = after[...]
    own = lax.rem(live - head + CHILD, CHILD)
    split_family = 1 + (live - head) // CHILD
    row = lax.broadcasted_iota(I32, (FAMILIES, LANES), 0)
    families[:, 640:768] = jnp.zeros((FAMILIES, LANES), F32)
    for m in range(CHILD):
        cells = padded[pl.ds(head + m, FAMILIES, stride=CHILD), :]
        late = after2[pl.ds(CHILD + m - own, 1), :]
        cells = jnp.where((row == split_family) & (m >= own), late, cells)
        families[:, m * DOF : (m + 1) * DOF] = cells[:, :DOF]
    hi, lo = split(families[...])
    rebuilt[:, : CHILD * DOF] = dot_nt(jnp.concatenate([hi, lo, hi], 1), recon3[0 : CHILD * DOF, :])
    lane = lax.broadcasted_iota(I32, (FAMILIES, LANES), 1)
    for m in range(CHILD):
        part = rebuilt[:, m * DOF : m * DOF + LANES]
        woven[pl.ds(m, FAMILIES, stride=CHILD), :] = jnp.where(lane < DOF, part, 0.0)


def kernel(counts, send, primal_in, dual_in, load_in, size_in, send_in, cell_in, other_in, dir_in, hanging_in,
           stiffness_in, recon_in, traction_in, trace_in,
           indicator, facts,
           primal, dual, load, cell_size, send_v, face_cell, face_other, face_dir, hanging, stiffness, recon, traction,
           trace, p_t, first, last, before, after, after2, p_out, p_in, w_out, w_in, picked, padded, woven, families, rebuilt,
           operator, operator3, table, side_a, side_b0, side_b1, recon3, onehot, index_a, index_b, smem_a, smem_b, term, partial, returned, part, parts,
           in_sem, index_sem, edge_send, edge_recv, p_send, p_recv, w_send, w_recv, b_send, b_recv, r_send, r_recv):
    me = lax.axis_index("dom")
    staged = [(primal_in, primal), (dual_in, dual), (recon_in, recon.at[pl.ds(0, CHILD * DOF), :]), (traction_in, traction), (trace_in, trace),
              (load_in, load), (size_in, cell_size), (stiffness_in, stiffness), (cell_in, face_cell),
              (other_in, face_other), (dir_in, face_dir), (hanging_in, hanging), (send_in, send_v)]
    loads = {}
    for i, (source, to) in enumerate(staged):
        loads[i] = pltpu.make_async_copy(source, to, in_sem.at[i])
        loads[i].start()

    barrier = pltpu.get_barrier_semaphore()
    partners = [behind(me, shift) for shift in SHIFTS]
    for stride, size in STAGES:
        partners += [in_stage(me, stride, size, step) for step in range(1, size)]
    for partner in partners:
        pl.semaphore_signal(barrier, inc=1, device_id=(partner,), device_id_type=MESH)

    start, live, cells = counts_of(counts, me)
    head = lax.rem(CHILD - lax.rem(start, CHILD), CHILD)

    def remote(source, to, send_sem, recv_sem, target):
        return pltpu.make_async_remote_copy(src_ref=source, dst_ref=to, send_sem=send_sem, recv_sem=recv_sem,
                                            device_id=(target,), device_id_type=MESH)

    def list_copy(source, to, send_sem, recv_sem, k):
        return remote(source.at[k], to.at[k], send_sem.at[k], recv_sem.at[k], behind(me, shift_of(k)))

    def transpose_primal(step, carry):
        to_cell_major(p_t, 0, primal, step)
        return carry

    loads[0].wait()
    lax.fori_loop(0, 8, transpose_primal, 0)
    loads[1].wait()
    cell = lax.broadcasted_iota(I32, (16, CELLS), 1)
    row = lax.broadcasted_iota(I32, (16, CELLS), 0)
    picked_cell = jnp.where(row < CHILD, row, live - 2 * CHILD + row)
    chosen = jnp.where(cell == picked_cell, 1.0, 0.0).astype(BF16)
    hi, lo = split(dual[...])
    ends = dot_nt(chosen, hi) + dot_nt(chosen, lo)
    first[...] = jnp.zeros((8, LANES), F32)
    last[...] = jnp.zeros((8, LANES), F32)
    first[:, :DOF] = ends[:CHILD]
    last[:, :DOF] = ends[CHILD:]
    pl.semaphore_wait(barrier, len(partners))
    edges = [remote(last, before, edge_send.at[0], edge_recv.at[0], behind(me, 1)),
             remote(first, after, edge_send.at[1], edge_recv.at[1], behind(me, -1))]
    for copy in edges:
        copy.start()

    def send_primal(step, carry):
        k = lax.rem(step + FIRST_LIST, NEIGH)
        gather_list(picked, p_t, send, k)
        to_cell_major(padded, CHILD, dual, step)
        pack(p_out.at[k], picked)
        list_copy(p_out, p_in, p_send, p_recv, k).start()
        return carry

    lax.fori_loop(0, NEIGH, send_primal, 0)
    padded[CELLS + 8 :, :] = jnp.zeros((padded.shape[0] - CELLS - 8, LANES), F32)

    def split_recon(step, carry):
        rows = pl.ds(pl.multiple_of(step * 96, 96), 96)
        wide = jnp.concatenate([recon[rows, :], jnp.zeros((96, 768 - CHILD * DOF), F32)], 1)
        hi, lo = split(wide)
        recon3[rows, 0:768] = hi
        recon3[rows, 768:1536] = hi
        recon3[rows, 1536:2304] = lo
        return carry

    loads[2].wait()
    lax.fori_loop(0, 7, split_recon, 0)
    for i in range(3, len(staged)):
        loads[i].wait()
    fill_operator(operator, traction, trace)
    hi, lo = split(operator[...].T)
    operator3[0:256, :] = hi
    operator3[256:512, :] = hi
    operator3[512:768, :] = lo
    pair = (face_dir[...] // 2) * SLOTS
    index_a[...] = pair + face_cell[...]
    index_b[...] = pair + face_other[...]
    copy_a = pltpu.make_async_copy(index_a, smem_a, index_sem.at[0])
    copy_b = pltpu.make_async_copy(index_b, smem_b, index_sem.at[1])
    copy_a.start()
    copy_b.start()

    def residuals(step, carry):
        take_residual(load, primal, stiffness, step)
        return carry

    lax.fori_loop(0, 8, residuals, 0)
    for k in range(NEIGH):
        onehot[:, k * GHOST : (k + 1) * GHOST] = low_onehot(send_v[k : k + 1, :])
    for copy in edges:
        copy.wait()
    padded[0:8, :] = before[...]
    rebuild(head, live, padded, after, after2, recon3, families, rebuilt, woven)

    def send_weight(step, carry):
        k = lax.rem(step + FIRST_LIST, NEIGH)
        at = pl.multiple_of(step * 256, 256)
        gather_rows(picked, 0, woven, lambda i: send[k, i] + (CHILD - head), GHOST)
        fill_table(table, at, p_t[pl.ds(at, 256), :], woven[pl.ds(CHILD - head + at, 256), :], operator3)
        cell_terms(term, load, woven, CHILD - head, cell_size, step)
        pack(w_out.at[k], picked)
        list_copy(w_out, w_in, w_send, w_recv, k).start()
        return carry

    lax.fori_loop(0, NEIGH, send_weight, 0)
    copy_a.wait()
    copy_b.wait()

    def gather_a(r, carry):
        gather_rows(side_a, r * LANES, table, lambda i: smem_a[r, i], LANES)
        return carry

    def take_ghosts(step, carry):
        k = lax.rem(step + FIRST_LIST, NEIGH)
        list_copy(p_out, p_in, p_send, p_recv, k).wait()
        list_copy(w_out, w_in, w_send, w_recv, k).wait()
        row = EARLY + step * LATE
        gather_rows(side_a, row * LANES, table, lambda i: smem_a[row + i // LANES, i % LANES], LATE * LANES)
        fill_table(table, CELLS + k * GHOST, unpack(p_in[k]), unpack(w_in[k]), operator3)
        return carry

    lax.fori_loop(0, EARLY, gather_a, 0)
    lax.fori_loop(0, NEIGH, take_ghosts, 0)

    lane = lax.broadcasted_iota(I32, (8, 2 * LANES), 1) % LANES
    sub = lax.broadcasted_iota(I32, (8, 2 * LANES), 0)
    pick = jnp.where(lane // 32 == sub, 1.0, 0.0).astype(BF16)
    upper = lax.broadcasted_iota(I32, (CHUNK, LANES), 1) % 64 >= 32

    def gather_b(to, c):
        gather_rows(to, 0, table, lambda i: smem_b[c * SPLIT + i // LANES, i % LANES], CHUNK)

    def raw_sums(side_b, c):
        a = side_a[pl.ds(pl.multiple_of(c * CHUNK, CHUNK), CHUNK), :]
        b = pltpu.roll(side_b[...], 64, 1)
        jump = pltpu.roll(a + b, 32, 1)
        hi, lo = split(jnp.where(upper, jump * a, pltpu.roll(jump * b, 96, 1)))
        return dot_nt(pick, jnp.concatenate([hi, lo], 1))

    def add_sums(raw, c, carry):
        sum_a, sum_b = carry
        face = c * CHUNK + lax.broadcasted_iota(I32, (1, CHUNK), 1)
        area = jnp.where(face < 3 * live, 0.5 * (1.0 - 0.75 * lanes_of(hanging, c).astype(F32)), 0.0)
        is_even = lanes_of(face_dir, c) % 2 == 0
        term_a = area * jnp.where(is_even, raw[1:2], raw[3:4])
        term_b = area * jnp.where(is_even, raw[0:1], raw[2:3])
        cell, other = lanes_of(face_cell, c), lanes_of(face_other, c)
        sum_a += scatter(cell, term_a, CELLS // LANES, low_onehot(cell))
        sum_b += scatter(other, term_b, SLOTS // LANES, low_onehot(other))
        return sum_a, sum_b

    def body(i, carry):
        raw_before, sums = carry
        gather_b(side_b1, 2 * i + 1)
        raw = raw_sums(side_b0, 2 * i)
        sums = add_sums(raw_before, jnp.maximum(2 * i - 1, 0), sums)
        gather_b(side_b0, jnp.minimum(2 * i + 2, CHUNKS - 1))
        raw_after = raw_sums(side_b1, 2 * i + 1)
        sums = add_sums(raw, 2 * i, sums)
        return raw_after, sums

    gather_b(side_b0, 0)
    zero = (jnp.zeros((CELLS // LANES, LANES), F32), jnp.zeros((SLOTS // LANES, LANES), F32))
    raw, sums = lax.fori_loop(0, CHUNKS // 2, body, (jnp.zeros((8, CHUNK), F32), zero))
    sum_a, sum_b = add_sums(raw, CHUNKS - 1, sums)
    for k in SEND_ORDER:
        at = CELLS // LANES + 2 * k
        partial[k] = sum_b[at : at + 2]
    backs = [remote(partial.at[k], returned.at[k], b_send, b_recv, behind(me, -SHIFTS[k])) for k in SEND_ORDER]
    for copy in backs:
        copy.start()
    index = jnp.concatenate([send_v[k : k + 1, :] for k in range(NEIGH)], 1)
    out = term[...] + sum_a + sum_b[: CELLS // LANES]
    remote(partial, returned, b_send, b_recv, behind(me, 1)).wait_recv()
    value = jnp.concatenate([returned[k, r : r + 1, :] for k in range(NEIGH) for r in range(2)], 1)
    out = out + scatter(index, value, CELLS // LANES, onehot[...])
    slot = lax.broadcasted_iota(I32, out.shape, 0) * LANES + lax.broadcasted_iota(I32, out.shape, 1)
    indicator[...] = out

    total = jnp.sum(jnp.where(slot < live, jnp.abs(out), 0.0), axis=0, keepdims=True)
    place = 0
    for stage, (stride, count) in enumerate(STAGES):
        part[stage] = total
        slots = pl.ds(place, count - 1)
        for step in range(1, count):
            remote(part.at[stage], parts.at[place + step - 1], r_send.at[stage], r_recv.at[stage],
                   in_stage(me, stride, count, step)).start()
        remote(parts.at[slots], parts.at[slots], r_send.at[stage], r_recv.at[stage], behind(me, 1)).wait_recv()
        total = total + jnp.sum(parts[place : place + count - 1], axis=0)
        place += count - 1

    mean = jnp.sum(total) / cells.astype(F32)
    facts[...] = jnp.where(slot < live, mean, -1.0)
    remote(partial, returned, b_send, b_recv, behind(me, 1)).wait_send()
    place = 0
    for stage, (stride, count) in enumerate(STAGES):
        slots = pl.ds(place, count - 1)
        remote(parts.at[slots], parts.at[slots], r_send.at[stage], r_recv.at[stage], behind(me, 1)).wait_send()
        place += count - 1


SMEM = pl.BlockSpec(memory_space=pltpu.SMEM)
VMEM = pl.BlockSpec(memory_space=pltpu.VMEM)
ANY = pl.BlockSpec(memory_space=pl.ANY)


def per_device(primal, dual, load, cell_size, cell_count, ghost_send, face_cell, face_other, face_dir, hanging,
               stiffness, recon, traction, trace):
    send = ghost_send[0]
    as_rows = lambda x: x.reshape(-1, LANES)
    f32 = lambda *shape: pltpu.VMEM(shape, F32)
    bf16 = lambda *shape: pltpu.VMEM(shape, BF16)
    i32 = lambda *shape: pltpu.VMEM(shape, I32)
    dma = lambda n: pltpu.SemaphoreType.DMA((n,))
    rows = FACES // LANES
    cells = CELLS // LANES
    steps = sum(size - 1 for _, size in STAGES)
    scratch = [
        f32(DOF, CELLS), f32(DOF, CELLS), f32(DOF, CELLS), f32(cells, LANES), i32(NEIGH, GHOST),
        i32(rows, LANES), i32(rows, LANES), i32(rows, LANES), i32(rows, LANES),
        f32(DOF, DOF), f32(768, CHILD * DOF), f32(6 * FACE_DOF, DOF), f32(6 * FACE_DOF, DOF),
        f32(CELLS, LANES),
        f32(8, LANES), f32(8, LANES), f32(8, LANES), f32(8, LANES), f32(16, LANES),
        f32(NEIGH, PACKED, LANES), f32(NEIGH, PACKED, LANES), f32(NEIGH, PACKED, LANES), f32(NEIGH, PACKED, LANES),
        f32(3 * THIRD, LANES),
        f32(FAMILIES * CHILD + 8, LANES), f32(FAMILIES * CHILD, LANES), f32(FAMILIES, 768), f32(FAMILIES, 768),
        f32(384, 256), bf16(768, 384), f32(3 * SLOTS, LANES), f32(FACES, LANES), f32(CHUNK, LANES), f32(CHUNK, LANES),
        bf16(768, 2304), bf16(LANES, GHOSTS),
        i32(rows, LANES), i32(rows, LANES), pltpu.SMEM((rows, LANES), I32), pltpu.SMEM((rows, LANES), I32),
        f32(cells, LANES), f32(NEIGH, 2, LANES), f32(NEIGH, 2, LANES), f32(len(STAGES), 1, LANES), f32(steps, 1, LANES),
        dma(13), dma(2), dma(2), dma(2), dma(NEIGH), dma(NEIGH), dma(NEIGH), dma(NEIGH),
        pltpu.SemaphoreType.DMA, pltpu.SemaphoreType.DMA, dma(len(STAGES)), dma(len(STAGES)),
    ]
    indicator, facts = pl.pallas_call(
        kernel,
        out_shape=[jax.ShapeDtypeStruct((cells, LANES), F32)] * 2,
        in_specs=[SMEM] * 2 + [ANY] * 13, out_specs=[VMEM] * 2, scratch_shapes=scratch,
        compiler_params=pltpu.CompilerParams(collective_id=0, has_side_effects=True,
                                             vmem_limit_bytes=56 * 1024 * 1024),
        name="indicators",
    )(cell_count, send, primal, dual, load, as_rows(cell_size), send, as_rows(face_cell), as_rows(face_other),
      as_rows(face_dir), as_rows(hanging), stiffness, recon, traction, trace)
    facts = facts.reshape(-1)
    indicator = jnp.where(facts < 0.0, 0.0, indicator.reshape(-1))
    return indicator, jnp.abs(indicator) / (jnp.abs(facts) + 1e-06)

def solution(mesh):
    in_specs = (P(None, "dom"), P(None, "dom"), P(None, "dom"), P("dom"), P(), P("dom", None, None), P("dom"), P("dom"),
                P("dom"), P("dom"), P(), P(), P(), P())
    return jax.shard_map(per_device, mesh=mesh, in_specs=in_specs, out_specs=(P("dom"), P("dom")), check_vma=False)
```

```python
import functools

import jax
import jax.numpy as jnp
from jax import lax
from jax.experimental import pallas as pl
from jax.experimental.pallas import tpu as pltpu
from jax.sharding import PartitionSpec as P

F32 = jnp.float32
BF16 = jnp.bfloat16
I32 = jnp.int32

DOF = 81
FACE_DOF = 27
CHILD = 8
CELLS = 2048
NEIGH = 8
GHOST = 256
GHOSTS = NEIGH * GHOST
SLOTS = CELLS + GHOSTS
FACES = 6144
LANES = 128
FAMILIES = 272
THIRD = 88
PACKED = 2 * THIRD
CHUNK = 256
CHUNKS = FACES // CHUNK
SPLIT = CHUNK // LANES


def split(x):
    high = x.astype(BF16)
    return high, (x - high.astype(F32)).astype(BF16)


def dot_nt(a, b):
    return lax.dot_general(a, b, (((1,), (1,)), ((), ())), preferred_element_type=F32)


def dot_nn(a, b):
    return lax.dot_general(a, b, (((1,), (0,)), ((), ())), preferred_element_type=F32)


def gather_rows(dst, dst_at, src, index_of, count):
    sub = lax.broadcasted_iota(I32, (8, LANES), 0)
    for base in range(0, count, 8):
        rows = [src[pl.ds(index_of(base + u), 1), :] for u in range(8)]
        tile = jnp.broadcast_to(rows[0], (8, LANES))
        for u in range(1, 8):
            tile = jnp.where(sub == u, jnp.broadcast_to(rows[u], (8, LANES)), tile)
        dst[pl.ds(pl.multiple_of(dst_at + base, 8), 8), :] = tile


def turned_block(src, at):
    return jnp.concatenate([src[:, pl.ds(at, 256)], jnp.zeros((LANES - DOF, 256), F32)], 0).T


def to_cell_major(dst, row, src, step):
    at = pl.multiple_of(step * 256, 256)
    dst[pl.ds(pl.multiple_of(row + at, CHILD), 256), :] = turned_block(src, at)


def pack(to, rows):
    lane = lax.broadcasted_iota(I32, (THIRD, LANES), 1)
    second = pltpu.roll(rows[THIRD : 2 * THIRD, :], DOF, 1)
    third = pltpu.roll(rows[2 * THIRD :, :], 2 * DOF - LANES, 1)
    upper = jnp.where(lane < DOF, rows[0:THIRD, :], second)
    to[...] = jnp.concatenate([upper, jnp.where(lane < 2 * DOF - LANES, second, third)], 0)


def unpack(rows):
    lane = lax.broadcasted_iota(I32, (THIRD, LANES), 1)
    upper, lower = rows[:THIRD], rows[THIRD:]
    second = pltpu.roll(jnp.where(lane < 2 * DOF - LANES, lower, upper), LANES - DOF, 1)
    third = pltpu.roll(lower, 2 * LANES - 2 * DOF, 1)
    return jnp.concatenate([upper, second, third[: GHOST - PACKED]], 0)


def fill_operator(operator, traction, trace):
    operator[...] = jnp.zeros(operator.shape, F32)
    for d in range(6):
        rows = slice(d * FACE_DOF, (d + 1) * FACE_DOF)
        operator[64 * d : 64 * d + FACE_DOF, 0:DOF] = traction[rows, :]
        operator[64 * d + 32 : 64 * d + 32 + FACE_DOF, LANES : LANES + DOF] = trace[rows, :]


def fill_table(table, slot, p_rows, w_rows, operator):
    hi, lo = split(jnp.concatenate([p_rows, w_rows], 1))
    out = dot_nn(jnp.concatenate([hi, lo, hi], 1), operator[...])
    for pair in range(3):
        table[pl.ds(pl.multiple_of(pair * SLOTS + slot, 256), 256), :] = out[:, pair * LANES : (pair + 1) * LANES]


def take_residual(load, primal, stiffness, step):
    cells = pl.ds(pl.multiple_of(step * 256, 256), 256)
    s_hi, s_lo = split(stiffness[...])
    p_hi, p_lo = split(primal[:, cells])
    load[:, cells] = load[:, cells] - (dot_nn(s_hi, p_hi) + dot_nn(s_lo, p_hi) + dot_nn(s_hi, p_lo))


def cell_terms(out, residual, woven, skip, cell_size, step):
    cells = pl.ds(pl.multiple_of(step * 256, 256), 256)
    total = jnp.sum(residual[:, cells] * woven[pl.ds(skip + step * 256, 256), :].T[:DOF, :], axis=0, keepdims=True)
    for r in range(2):
        i = step * 2 + r
        out[pl.ds(i, 1), :] = cell_size[pl.ds(i, 1), :] * total[:, r * LANES : (r + 1) * LANES]


def lanes_of(ref, chunk):
    return jnp.concatenate([ref[pl.ds(chunk * SPLIT + i, 1), :] for i in range(SPLIT)], 1)


def low_onehot(index):
    low = lax.broadcasted_iota(I32, (LANES, index.shape[1]), 0) == index % LANES
    return jnp.where(low, 1.0, 0.0).astype(BF16)


def scatter(index, value, high_count, onehot):
    high = lax.broadcasted_iota(I32, (high_count, index.shape[1]), 0) == index // LANES
    both = dot_nt(jnp.concatenate(split(jnp.where(high, value, 0.0)), 0), onehot)
    return both[:high_count] + both[high_count:]


MESH = pl.DeviceIdType.MESH
RANKS = 128
SHIFTS = [(1 << which // 2) * (1 - 2 * (which % 2)) for which in range(NEIGH)]
FIRST_LIST = 4
LATE = 2
EARLY = FACES // LANES - NEIGH * LATE
SEND_ORDER = [4, 5, 6, 7, 2, 3, 0, 1]
STAGES = ((1, 8), (8, 16))


def counts_of(counts, me):
    def body(i, carry):
        before, here, cells = carry
        c = counts[i]
        return before + jnp.where(i < me, c, 0), here + jnp.where(i == me, c, 0), cells + c

    return lax.fori_loop(0, RANKS, body, (jnp.int32(0), jnp.int32(0), jnp.int32(0)), unroll=32)


def behind(me, by):
    return lax.rem(me + (by + RANKS), RANKS)


def shift_of(k):
    e = k // 2
    power = 1 + e + e * (e - 1) // 2 + e * (e - 1) * (e - 2) // 6
    return power * (1 - 2 * (k % 2))


def in_stage(me, stride, size, step):
    place = lax.rem(me // stride, size)
    return me + (lax.rem(place + step, size) - place) * stride


def gather_list(picked, source, send, k):
    gather_rows(picked, 0, source, lambda i: send[k, i], GHOST)


def rebuild(head, live, padded, after, after2, recon3, families, rebuilt, woven):
    after2[0:8, :] = jnp.zeros((8, LANES), F32)
    after2[8:16, :] = after[...]
    own = lax.rem(live - head + CHILD, CHILD)
    split_family = 1 + (live - head) // CHILD
    row = lax.broadcasted_iota(I32, (FAMILIES, LANES), 0)
    families[:, 640:768] = jnp.zeros((FAMILIES, LANES), F32)
    for m in range(CHILD):
        cells = padded[pl.ds(head + m, FAMILIES, stride=CHILD), :]
        late = after2[pl.ds(CHILD + m - own, 1), :]
        cells = jnp.where((row == split_family) & (m >= own), late, cells)
        families[:, m * DOF : (m + 1) * DOF] = cells[:, :DOF]
    hi, lo = split(families[...])
    rebuilt[:, : CHILD * DOF] = dot_nt(jnp.concatenate([hi, lo, hi], 1), recon3[0 : CHILD * DOF, :])
    lane = lax.broadcasted_iota(I32, (FAMILIES, LANES), 1)
    for m in range(CHILD):
        part = rebuilt[:, m * DOF : m * DOF + LANES]
        woven[pl.ds(m, FAMILIES, stride=CHILD), :] = jnp.where(lane < DOF, part, 0.0)


def kernel(counts, send, primal_in, dual_in, load_in, size_in, send_in, cell_in, other_in, dir_in, hanging_in,
           stiffness_in, recon_in, traction_in, trace_in,
           indicator, facts,
           primal, dual, load, cell_size, send_v, face_cell, face_other, face_dir, hanging, stiffness, recon, traction,
           trace, p_t, first, last, before, after, after2, p_out, p_in, w_out, w_in, picked, padded, woven, families, rebuilt,
           operator, operator3, table, side_a, side_b0, side_b1, recon3, onehot, index_a, index_b, smem_a, smem_b, term, partial, returned, part, parts,
           in_sem, index_sem, edge_send, edge_recv, p_send, p_recv, w_send, w_recv, b_send, b_recv, r_send, r_recv):
    me = lax.axis_index("dom")
    staged = [(primal_in, primal), (dual_in, dual), (recon_in, recon.at[pl.ds(0, CHILD * DOF), :]), (traction_in, traction), (trace_in, trace),
              (load_in, load), (size_in, cell_size), (stiffness_in, stiffness), (cell_in, face_cell),
              (other_in, face_other), (dir_in, face_dir), (hanging_in, hanging), (send_in, send_v)]
    loads = {}
    for i, (source, to) in enumerate(staged):
        loads[i] = pltpu.make_async_copy(source, to, in_sem.at[i])
        loads[i].start()

    barrier = pltpu.get_barrier_semaphore()
    partners = [behind(me, shift) for shift in SHIFTS]
    for stride, size in STAGES:
        partners += [in_stage(me, stride, size, step) for step in range(1, size)]
    for partner in partners:
        pl.semaphore_signal(barrier, inc=1, device_id=(partner,), device_id_type=MESH)

    start, live, cells = counts_of(counts, me)
    head = lax.rem(CHILD - lax.rem(start, CHILD), CHILD)

    def remote(source, to, send_sem, recv_sem, target):
        return pltpu.make_async_remote_copy(src_ref=source, dst_ref=to, send_sem=send_sem, recv_sem=recv_sem,
                                            device_id=(target,), device_id_type=MESH)

    def list_copy(source, to, send_sem, recv_sem, k):
        return remote(source.at[k], to.at[k], send_sem.at[k], recv_sem.at[k], behind(me, shift_of(k)))

    def transpose_primal(step, carry):
        to_cell_major(p_t, 0, primal, step)
        return carry

    loads[0].wait()
    lax.fori_loop(0, 8, transpose_primal, 0)
    loads[1].wait()
    cell = lax.broadcasted_iota(I32, (16, CELLS), 1)
    row = lax.broadcasted_iota(I32, (16, CELLS), 0)
    picked_cell = jnp.where(row < CHILD, row, live - 2 * CHILD + row)
    chosen = jnp.where(cell == picked_cell, 1.0, 0.0).astype(BF16)
    hi, lo = split(dual[...])
    ends = dot_nt(chosen, hi) + dot_nt(chosen, lo)
    first[...] = jnp.zeros((8, LANES), F32)
    last[...] = jnp.zeros((8, LANES), F32)
    first[:, :DOF] = ends[:CHILD]
    last[:, :DOF] = ends[CHILD:]
    pl.semaphore_wait(barrier, len(partners))
    edges = [remote(last, before, edge_send.at[0], edge_recv.at[0], behind(me, 1)),
             remote(first, after, edge_send.at[1], edge_recv.at[1], behind(me, -1))]
    for copy in edges:
        copy.start()

    def send_primal(step, carry):
        k = lax.rem(step + FIRST_LIST, NEIGH)
        gather_list(picked, p_t, send, k)
        to_cell_major(padded, CHILD, dual, step)
        pack(p_out.at[k], picked)
        list_copy(p_out, p_in, p_send, p_recv, k).start()
        return carry

    lax.fori_loop(0, NEIGH, send_primal, 0)
    padded[CELLS + 8 :, :] = jnp.zeros((padded.shape[0] - CELLS - 8, LANES), F32)

    def split_recon(step, carry):
        rows = pl.ds(pl.multiple_of(step * 96, 96), 96)
        wide = jnp.concatenate([recon[rows, :], jnp.zeros((96, 768 - CHILD * DOF), F32)], 1)
        hi, lo = split(wide)
        recon3[rows, 0:768] = hi
        recon3[rows, 768:1536] = hi
        recon3[rows, 1536:2304] = lo
        return carry

    loads[2].wait()
    lax.fori_loop(0, 7, split_recon, 0)
    for i in range(3, len(staged)):
        loads[i].wait()
    fill_operator(operator, traction, trace)
    hi, lo = split(operator[...].T)
    operator3[0:256, :] = hi
    operator3[256:512, :] = hi
    operator3[512:768, :] = lo
    pair = (face_dir[...] // 2) * SLOTS
    index_a[...] = pair + face_cell[...]
    index_b[...] = pair + face_other[...]
    copy_a = pltpu.make_async_copy(index_a, smem_a, index_sem.at[0])
    copy_b = pltpu.make_async_copy(index_b, smem_b, index_sem.at[1])
    copy_a.start()
    copy_b.start()

    def residuals(step, carry):
        take_residual(load, primal, stiffness, step)
        return carry

    lax.fori_loop(0, 8, residuals, 0)
    for k in range(NEIGH):
        onehot[:, k * GHOST : (k + 1) * GHOST] = low_onehot(send_v[k : k + 1, :])
    for copy in edges:
        copy.wait()
    padded[0:8, :] = before[...]
    rebuild(head, live, padded, after, after2, recon3, families, rebuilt, woven)

    def send_weight(step, carry):
        k = lax.rem(step + FIRST_LIST, NEIGH)
        gather_rows(picked, 0, woven, lambda i: send[k, i] + (CHILD - head), GHOST)
        pack(w_out.at[k], picked)
        list_copy(w_out, w_in, w_send, w_recv, k).start()
        return carry

    def local_part(step, carry):
        at = pl.multiple_of(step * 256, 256)
        fill_table(table, at, p_t[pl.ds(at, 256), :], woven[pl.ds(CHILD - head + at, 256), :], operator3)
        cell_terms(term, load, woven, CHILD - head, cell_size, step)
        return carry

    lax.fori_loop(0, NEIGH, send_weight, 0)
    lax.fori_loop(0, NEIGH, local_part, 0)
    copy_a.wait()
    copy_b.wait()

    def gather_a(r, carry):
        gather_rows(side_a, r * LANES, table, lambda i: smem_a[r, i], LANES)
        return carry

    def take_ghosts(step, carry):
        k = lax.rem(step + FIRST_LIST, NEIGH)
        list_copy(p_out, p_in, p_send, p_recv, k).wait()
        list_copy(w_out, w_in, w_send, w_recv, k).wait()
        row = EARLY + step * LATE
        gather_rows(side_a, row * LANES, table, lambda i: smem_a[row + i // LANES, i % LANES], LATE * LANES)
        fill_table(table, CELLS + k * GHOST, unpack(p_in[k]), unpack(w_in[k]), operator3)
        return carry

    lax.fori_loop(0, EARLY, gather_a, 0)
    lax.fori_loop(0, NEIGH, take_ghosts, 0)

    lane = lax.broadcasted_iota(I32, (8, 2 * LANES), 1) % LANES
    sub = lax.broadcasted_iota(I32, (8, 2 * LANES), 0)
    pick = jnp.where(lane // 32 == sub, 1.0, 0.0).astype(BF16)
    upper = lax.broadcasted_iota(I32, (CHUNK, LANES), 1) % 64 >= 32

    def gather_b(to, c):
        gather_rows(to, 0, table, lambda i: smem_b[c * SPLIT + i // LANES, i % LANES], CHUNK)

    def raw_sums(side_b, c):
        a = side_a[pl.ds(pl.multiple_of(c * CHUNK, CHUNK), CHUNK), :]
        b = pltpu.roll(side_b[...], 64, 1)
        jump = pltpu.roll(a + b, 32, 1)
        hi, lo = split(jnp.where(upper, jump * a, pltpu.roll(jump * b, 96, 1)))
        return dot_nt(pick, jnp.concatenate([hi, lo], 1))

    def add_sums(raw, c, carry):
        sum_a, sum_b = carry
        face = c * CHUNK + lax.broadcasted_iota(I32, (1, CHUNK), 1)
        area = jnp.where(face < 3 * live, 0.5 * (1.0 - 0.75 * lanes_of(hanging, c).astype(F32)), 0.0)
        is_even = lanes_of(face_dir, c) % 2 == 0
        term_a = area * jnp.where(is_even, raw[1:2], raw[3:4])
        term_b = area * jnp.where(is_even, raw[0:1], raw[2:3])
        cell, other = lanes_of(face_cell, c), lanes_of(face_other, c)
        sum_a += scatter(cell, term_a, CELLS // LANES, low_onehot(cell))
        sum_b += scatter(other, term_b, SLOTS // LANES, low_onehot(other))
        return sum_a, sum_b

    def body(i, carry):
        raw_before, sums = carry
        gather_b(side_b1, 2 * i + 1)
        raw = raw_sums(side_b0, 2 * i)
        sums = add_sums(raw_before, jnp.maximum(2 * i - 1, 0), sums)
        gather_b(side_b0, jnp.minimum(2 * i + 2, CHUNKS - 1))
        raw_after = raw_sums(side_b1, 2 * i + 1)
        sums = add_sums(raw, 2 * i, sums)
        return raw_after, sums

    gather_b(side_b0, 0)
    zero = (jnp.zeros((CELLS // LANES, LANES), F32), jnp.zeros((SLOTS // LANES, LANES), F32))
    raw, sums = lax.fori_loop(0, CHUNKS // 2, body, (jnp.zeros((8, CHUNK), F32), zero))
    sum_a, sum_b = add_sums(raw, CHUNKS - 1, sums)
    for k in SEND_ORDER:
        at = CELLS // LANES + 2 * k
        partial[k] = sum_b[at : at + 2]
    backs = [remote(partial.at[k], returned.at[k], b_send, b_recv, behind(me, -SHIFTS[k])) for k in SEND_ORDER]
    for copy in backs:
        copy.start()
    index = jnp.concatenate([send_v[k : k + 1, :] for k in range(NEIGH)], 1)
    out = term[...] + sum_a + sum_b[: CELLS // LANES]
    remote(partial, returned, b_send, b_recv, behind(me, 1)).wait_recv()
    value = jnp.concatenate([returned[k, r : r + 1, :] for k in range(NEIGH) for r in range(2)], 1)
    out = out + scatter(index, value, CELLS // LANES, onehot[...])
    slot = lax.broadcasted_iota(I32, out.shape, 0) * LANES + lax.broadcasted_iota(I32, out.shape, 1)
    indicator[...] = out

    total = jnp.sum(jnp.where(slot < live, jnp.abs(out), 0.0), axis=0, keepdims=True)
    place = 0
    for stage, (stride, count) in enumerate(STAGES):
        part[stage] = total
        slots = pl.ds(place, count - 1)
        for step in range(1, count):
            remote(part.at[stage], parts.at[place + step - 1], r_send.at[stage], r_recv.at[stage],
                   in_stage(me, stride, count, step)).start()
        remote(parts.at[slots], parts.at[slots], r_send.at[stage], r_recv.at[stage], behind(me, 1)).wait_recv()
        total = total + jnp.sum(parts[place : place + count - 1], axis=0)
        place += count - 1

    mean = jnp.sum(total) / cells.astype(F32)
    facts[...] = jnp.where(slot < live, mean, -1.0)
    remote(partial, returned, b_send, b_recv, behind(me, 1)).wait_send()
    place = 0
    for stage, (stride, count) in enumerate(STAGES):
        slots = pl.ds(place, count - 1)
        remote(parts.at[slots], parts.at[slots], r_send.at[stage], r_recv.at[stage], behind(me, 1)).wait_send()
        place += count - 1


SMEM = pl.BlockSpec(memory_space=pltpu.SMEM)
VMEM = pl.BlockSpec(memory_space=pltpu.VMEM)
ANY = pl.BlockSpec(memory_space=pl.ANY)


def per_device(primal, dual, load, cell_size, cell_count, ghost_send, face_cell, face_other, face_dir, hanging,
               stiffness, recon, traction, trace):
    send = ghost_send[0]
    as_rows = lambda x: x.reshape(-1, LANES)
    f32 = lambda *shape: pltpu.VMEM(shape, F32)
    bf16 = lambda *shape: pltpu.VMEM(shape, BF16)
    i32 = lambda *shape: pltpu.VMEM(shape, I32)
    dma = lambda n: pltpu.SemaphoreType.DMA((n,))
    rows = FACES // LANES
    cells = CELLS // LANES
    steps = sum(size - 1 for _, size in STAGES)
    scratch = [
        f32(DOF, CELLS), f32(DOF, CELLS), f32(DOF, CELLS), f32(cells, LANES), i32(NEIGH, GHOST),
        i32(rows, LANES), i32(rows, LANES), i32(rows, LANES), i32(rows, LANES),
        f32(DOF, DOF), f32(768, CHILD * DOF), f32(6 * FACE_DOF, DOF), f32(6 * FACE_DOF, DOF),
        f32(CELLS, LANES),
        f32(8, LANES), f32(8, LANES), f32(8, LANES), f32(8, LANES), f32(16, LANES),
        f32(NEIGH, PACKED, LANES), f32(NEIGH, PACKED, LANES), f32(NEIGH, PACKED, LANES), f32(NEIGH, PACKED, LANES),
        f32(3 * THIRD, LANES),
        f32(FAMILIES * CHILD + 8, LANES), f32(FAMILIES * CHILD, LANES), f32(FAMILIES, 768), f32(FAMILIES, 768),
        f32(384, 256), bf16(768, 384), f32(3 * SLOTS, LANES), f32(FACES, LANES), f32(CHUNK, LANES), f32(CHUNK, LANES),
        bf16(768, 2304), bf16(LANES, GHOSTS),
        i32(rows, LANES), i32(rows, LANES), pltpu.SMEM((rows, LANES), I32), pltpu.SMEM((rows, LANES), I32),
        f32(cells, LANES), f32(NEIGH, 2, LANES), f32(NEIGH, 2, LANES), f32(len(STAGES), 1, LANES), f32(steps, 1, LANES),
        dma(13), dma(2), dma(2), dma(2), dma(NEIGH), dma(NEIGH), dma(NEIGH), dma(NEIGH),
        pltpu.SemaphoreType.DMA, pltpu.SemaphoreType.DMA, dma(len(STAGES)), dma(len(STAGES)),
    ]
    indicator, facts = pl.pallas_call(
        kernel,
        out_shape=[jax.ShapeDtypeStruct((cells, LANES), F32)] * 2,
        in_specs=[SMEM] * 2 + [ANY] * 13, out_specs=[VMEM] * 2, scratch_shapes=scratch,
        compiler_params=pltpu.CompilerParams(collective_id=0, has_side_effects=True,
                                             vmem_limit_bytes=56 * 1024 * 1024),
        name="indicators",
    )(cell_count, send, primal, dual, load, as_rows(cell_size), send, as_rows(face_cell), as_rows(face_other),
      as_rows(face_dir), as_rows(hanging), stiffness, recon, traction, trace)
    facts = facts.reshape(-1)
    indicator = jnp.where(facts < 0.0, 0.0, indicator.reshape(-1))
    return indicator, jnp.abs(indicator) / (jnp.abs(facts) + 1e-06)

def solution(mesh):
    in_specs = (P(None, "dom"), P(None, "dom"), P(None, "dom"), P("dom"), P(), P("dom", None, None), P("dom"), P("dom"),
                P("dom"), P("dom"), P(), P(), P(), P())
    return jax.shard_map(per_device, mesh=mesh, in_specs=in_specs, out_specs=(P("dom"), P("dom")), check_vma=False)
```

```python
import functools

import jax
import jax.numpy as jnp
from jax import lax
from jax.experimental import pallas as pl
from jax.experimental.pallas import tpu as pltpu
from jax.sharding import PartitionSpec as P

F32 = jnp.float32
BF16 = jnp.bfloat16
I32 = jnp.int32

DOF = 81
FACE_DOF = 27
CHILD = 8
CELLS = 2048
NEIGH = 8
GHOST = 256
GHOSTS = NEIGH * GHOST
SLOTS = CELLS + GHOSTS
FACES = 6144
LANES = 128
FAMILIES = 272
THIRD = 88
PACKED = 2 * THIRD
CHUNK = 256
CHUNKS = FACES // CHUNK
SPLIT = CHUNK // LANES


def split(x):
    high = x.astype(BF16)
    return high, (x - high.astype(F32)).astype(BF16)


def dot_nt(a, b):
    return lax.dot_general(a, b, (((1,), (1,)), ((), ())), preferred_element_type=F32)


def dot_nn(a, b):
    return lax.dot_general(a, b, (((1,), (0,)), ((), ())), preferred_element_type=F32)


def gather_rows(dst, dst_at, src, index_of, count):
    sub = lax.broadcasted_iota(I32, (8, LANES), 0)
    for base in range(0, count, 8):
        rows = [src[pl.ds(index_of(base + u), 1), :] for u in range(8)]
        tile = jnp.broadcast_to(rows[0], (8, LANES))
        for u in range(1, 8):
            tile = jnp.where(sub == u, jnp.broadcast_to(rows[u], (8, LANES)), tile)
        dst[pl.ds(pl.multiple_of(dst_at + base, 8), 8), :] = tile


def turned_block(src, at):
    return jnp.concatenate([src[:, pl.ds(at, 256)], jnp.zeros((LANES - DOF, 256), F32)], 0).T


def to_cell_major(dst, row, src, step):
    at = pl.multiple_of(step * 256, 256)
    dst[pl.ds(pl.multiple_of(row + at, CHILD), 256), :] = turned_block(src, at)


def pack(to, rows):
    lane = lax.broadcasted_iota(I32, (THIRD, LANES), 1)
    second = pltpu.roll(rows[THIRD : 2 * THIRD, :], DOF, 1)
    third = pltpu.roll(rows[2 * THIRD :, :], 2 * DOF - LANES, 1)
    upper = jnp.where(lane < DOF, rows[0:THIRD, :], second)
    to[...] = jnp.concatenate([upper, jnp.where(lane < 2 * DOF - LANES, second, third)], 0)


def unpack(rows):
    lane = lax.broadcasted_iota(I32, (THIRD, LANES), 1)
    upper, lower = rows[:THIRD], rows[THIRD:]
    second = pltpu.roll(jnp.where(lane < 2 * DOF - LANES, lower, upper), LANES - DOF, 1)
    third = pltpu.roll(lower, 2 * LANES - 2 * DOF, 1)
    return jnp.concatenate([upper, second, third[: GHOST - PACKED]], 0)


def fill_operator(operator, traction, trace):
    operator[...] = jnp.zeros(operator.shape, F32)
    for d in range(6):
        rows = slice(d * FACE_DOF, (d + 1) * FACE_DOF)
        operator[64 * d : 64 * d + FACE_DOF, 0:DOF] = traction[rows, :]
        operator[64 * d + 32 : 64 * d + 32 + FACE_DOF, LANES : LANES + DOF] = trace[rows, :]


def fill_table(table, slot, p_rows, w_rows, operator):
    hi, lo = split(jnp.concatenate([p_rows, w_rows], 1))
    out = dot_nn(jnp.concatenate([hi, lo, hi], 1), operator[...])
    for pair in range(3):
        table[pl.ds(pl.multiple_of(pair * SLOTS + slot, 256), 256), :] = out[:, pair * LANES : (pair + 1) * LANES]


def take_residual(load, primal, stiffness, step):
    cells = pl.ds(pl.multiple_of(step * 256, 256), 256)
    s_hi, s_lo = split(stiffness[...])
    p_hi, p_lo = split(primal[:, cells])
    load[:, cells] = load[:, cells] - (dot_nn(s_hi, p_hi) + dot_nn(s_lo, p_hi) + dot_nn(s_hi, p_lo))


def cell_terms(out, residual, woven, skip, cell_size, step):
    cells = pl.ds(pl.multiple_of(step * 256, 256), 256)
    total = jnp.sum(residual[:, cells] * woven[pl.ds(skip + step * 256, 256), :].T[:DOF, :], axis=0, keepdims=True)
    for r in range(2):
        i = step * 2 + r
        out[pl.ds(i, 1), :] = cell_size[pl.ds(i, 1), :] * total[:, r * LANES : (r + 1) * LANES]


def lanes_of(ref, chunk):
    return jnp.concatenate([ref[pl.ds(chunk * SPLIT + i, 1), :] for i in range(SPLIT)], 1)


def low_onehot(index):
    low = lax.broadcasted_iota(I32, (LANES, index.shape[1]), 0) == index % LANES
    return jnp.where(low, 1.0, 0.0).astype(BF16)


def scatter(index, value, high_count, onehot):
    high = lax.broadcasted_iota(I32, (high_count, index.shape[1]), 0) == index // LANES
    both = dot_nt(jnp.concatenate(split(jnp.where(high, value, 0.0)), 0), onehot)
    return both[:high_count] + both[high_count:]


MESH = pl.DeviceIdType.MESH
RANKS = 128
SHIFTS = [(1 << which // 2) * (1 - 2 * (which % 2)) for which in range(NEIGH)]
FIRST_LIST = 4
LATE = 2
EARLY = FACES // LANES - NEIGH * LATE
SEND_ORDER = [4, 5, 6, 7, 2, 3, 0, 1]
STAGES = ((1, 8), (8, 16))


def counts_of(counts, me):
    def body(i, carry):
        before, here, cells = carry
        c = counts[i]
        return before + jnp.where(i < me, c, 0), here + jnp.where(i == me, c, 0), cells + c

    return lax.fori_loop(0, RANKS, body, (jnp.int32(0), jnp.int32(0), jnp.int32(0)), unroll=32)


def behind(me, by):
    return lax.rem(me + (by + RANKS), RANKS)


def shift_of(k):
    e = k // 2
    power = 1 + e + e * (e - 1) // 2 + e * (e - 1) * (e - 2) // 6
    return power * (1 - 2 * (k % 2))


def in_stage(me, stride, size, step):
    place = lax.rem(me // stride, size)
    return me + (lax.rem(place + step, size) - place) * stride


def gather_list(picked, source, send, k):
    gather_rows(picked, 0, source, lambda i: send[k, i], GHOST)


def rebuild(head, live, padded, after, after2, recon3, families, rebuilt, woven):
    after2[0:8, :] = jnp.zeros((8, LANES), F32)
    after2[8:16, :] = after[...]
    own = lax.rem(live - head + CHILD, CHILD)
    split_family = 1 + (live - head) // CHILD
    row = lax.broadcasted_iota(I32, (FAMILIES, LANES), 0)
    families[:, 640:768] = jnp.zeros((FAMILIES, LANES), F32)
    for m in range(CHILD):
        cells = padded[pl.ds(head + m, FAMILIES, stride=CHILD), :]
        late = after2[pl.ds(CHILD + m - own, 1), :]
        cells = jnp.where((row == split_family) & (m >= own), late, cells)
        families[:, m * DOF : (m + 1) * DOF] = cells[:, :DOF]
    hi, lo = split(families[...])
    rebuilt[:, : CHILD * DOF] = dot_nt(jnp.concatenate([hi, lo, hi], 1), recon3[0 : CHILD * DOF, :])
    lane = lax.broadcasted_iota(I32, (FAMILIES, LANES), 1)
    for m in range(CHILD):
        part = rebuilt[:, m * DOF : m * DOF + LANES]
        woven[pl.ds(m, FAMILIES, stride=CHILD), :] = jnp.where(lane < DOF, part, 0.0)


def kernel(counts, send, primal_in, dual_in, load_in, size_in, send_in, cell_in, other_in, dir_in, hanging_in,
           stiffness_in, recon_in, traction_in, trace_in,
           indicator, facts,
           primal, dual, load, cell_size, send_v, face_cell, face_other, face_dir, hanging, stiffness, recon, traction,
           trace, p_t, first, last, before, after, after2, p_out, p_in, w_out, w_in, picked, padded, woven, families, rebuilt,
           operator, operator3, table, side_a, side_b0, side_b1, recon3, onehot, index_a, index_b, smem_a, smem_b, term, partial, returned, part, parts,
           in_sem, index_sem, edge_send, edge_recv, p_send, p_recv, w_send, w_recv, b_send, b_recv, r_send, r_recv):
    me = lax.axis_index("dom")
    staged = [(primal_in, primal), (dual_in, dual), (recon_in, recon.at[pl.ds(0, CHILD * DOF), :]), (traction_in, traction), (trace_in, trace),
              (load_in, load), (size_in, cell_size), (stiffness_in, stiffness), (cell_in, face_cell),
              (other_in, face_other), (dir_in, face_dir), (hanging_in, hanging), (send_in, send_v)]
    loads = {}
    for i, (source, to) in enumerate(staged):
        loads[i] = pltpu.make_async_copy(source, to, in_sem.at[i])
        loads[i].start()

    barrier = pltpu.get_barrier_semaphore()
    partners = [behind(me, shift) for shift in SHIFTS]
    for stride, size in STAGES:
        partners += [in_stage(me, stride, size, step) for step in range(1, size)]
    for partner in partners:
        pl.semaphore_signal(barrier, inc=1, device_id=(partner,), device_id_type=MESH)

    start, live, cells = counts_of(counts, me)
    head = lax.rem(CHILD - lax.rem(start, CHILD), CHILD)

    def remote(source, to, send_sem, recv_sem, target):
        return pltpu.make_async_remote_copy(src_ref=source, dst_ref=to, send_sem=send_sem, recv_sem=recv_sem,
                                            device_id=(target,), device_id_type=MESH)

    def list_copy(source, to, send_sem, recv_sem, k):
        return remote(source.at[k], to.at[k], send_sem.at[k], recv_sem.at[k], behind(me, shift_of(k)))

    def transpose_primal(step, carry):
        to_cell_major(p_t, 0, primal, step)
        return carry

    loads[0].wait()
    lax.fori_loop(0, 8, transpose_primal, 0)
    loads[1].wait()
    cell = lax.broadcasted_iota(I32, (16, CELLS), 1)
    row = lax.broadcasted_iota(I32, (16, CELLS), 0)
    picked_cell = jnp.where(row < CHILD, row, live - 2 * CHILD + row)
    chosen = jnp.where(cell == picked_cell, 1.0, 0.0).astype(BF16)
    hi, lo = split(dual[...])
    ends = dot_nt(chosen, hi) + dot_nt(chosen, lo)
    first[...] = jnp.zeros((8, LANES), F32)
    last[...] = jnp.zeros((8, LANES), F32)
    first[:, :DOF] = ends[:CHILD]
    last[:, :DOF] = ends[CHILD:]
    pl.semaphore_wait(barrier, len(partners))
    edges = [remote(last, before, edge_send.at[0], edge_recv.at[0], behind(me, 1)),
             remote(first, after, edge_send.at[1], edge_recv.at[1], behind(me, -1))]
    for copy in edges:
        copy.start()

    for i in range(2, len(staged)):
        loads[i].wait()

    def send_primal(step, carry):
        k = lax.rem(step + FIRST_LIST, NEIGH)
        gather_list(picked, p_t, send, k)
        to_cell_major(padded, CHILD, dual, step)
        take_residual(load, primal, stiffness, step)
        onehot[:, pl.ds(pl.multiple_of(step * GHOST, GHOST), GHOST)] = low_onehot(send_v[pl.ds(step, 1), :])
        rows = pl.ds(pl.multiple_of(step * 96, 96), 96)
        wide = jnp.concatenate([recon[rows, :], jnp.zeros((96, 768 - CHILD * DOF), F32)], 1)
        hi, lo = split(wide)
        recon3[rows, 0:768] = hi
        recon3[rows, 768:1536] = hi
        recon3[rows, 1536:2304] = lo
        pack(p_out.at[k], picked)
        list_copy(p_out, p_in, p_send, p_recv, k).start()
        return carry

    lax.fori_loop(0, NEIGH, send_primal, 0)
    padded[CELLS + 8 :, :] = jnp.zeros((padded.shape[0] - CELLS - 8, LANES), F32)

    fill_operator(operator, traction, trace)
    hi, lo = split(operator[...].T)
    operator3[0:256, :] = hi
    operator3[256:512, :] = hi
    operator3[512:768, :] = lo
    pair = (face_dir[...] // 2) * SLOTS
    index_a[...] = pair + face_cell[...]
    index_b[...] = pair + face_other[...]
    copy_a = pltpu.make_async_copy(index_a, smem_a, index_sem.at[0])
    copy_b = pltpu.make_async_copy(index_b, smem_b, index_sem.at[1])
    copy_a.start()
    copy_b.start()

    for copy in edges:
        copy.wait()
    padded[0:8, :] = before[...]
    rebuild(head, live, padded, after, after2, recon3, families, rebuilt, woven)

    def send_weight(step, carry):
        k = lax.rem(step + FIRST_LIST, NEIGH)
        at = pl.multiple_of(step * 256, 256)
        gather_rows(picked, 0, woven, lambda i: send[k, i] + (CHILD - head), GHOST)
        fill_table(table, at, p_t[pl.ds(at, 256), :], woven[pl.ds(CHILD - head + at, 256), :], operator3)
        cell_terms(term, load, woven, CHILD - head, cell_size, step)
        pack(w_out.at[k], picked)
        list_copy(w_out, w_in, w_send, w_recv, k).start()
        return carry

    lax.fori_loop(0, NEIGH, send_weight, 0)
    copy_a.wait()
    copy_b.wait()

    def gather_a(r, carry):
        gather_rows(side_a, r * LANES, table, lambda i: smem_a[r, i], LANES)
        return carry

    def take_ghosts(step, carry):
        k = lax.rem(step + FIRST_LIST, NEIGH)
        list_copy(p_out, p_in, p_send, p_recv, k).wait()
        list_copy(w_out, w_in, w_send, w_recv, k).wait()
        row = EARLY + step * LATE
        gather_rows(side_a, row * LANES, table, lambda i: smem_a[row + i // LANES, i % LANES], LATE * LANES)
        fill_table(table, CELLS + k * GHOST, unpack(p_in[k]), unpack(w_in[k]), operator3)
        return carry

    lax.fori_loop(0, EARLY, gather_a, 0)
    lax.fori_loop(0, NEIGH, take_ghosts, 0)

    lane = lax.broadcasted_iota(I32, (8, 2 * LANES), 1) % LANES
    sub = lax.broadcasted_iota(I32, (8, 2 * LANES), 0)
    pick = jnp.where(lane // 32 == sub, 1.0, 0.0).astype(BF16)
    upper = lax.broadcasted_iota(I32, (CHUNK, LANES), 1) % 64 >= 32

    def gather_b(to, c):
        gather_rows(to, 0, table, lambda i: smem_b[c * SPLIT + i // LANES, i % LANES], CHUNK)

    def raw_sums(side_b, c):
        a = side_a[pl.ds(pl.multiple_of(c * CHUNK, CHUNK), CHUNK), :]
        b = pltpu.roll(side_b[...], 64, 1)
        jump = pltpu.roll(a + b, 32, 1)
        hi, lo = split(jnp.where(upper, jump * a, pltpu.roll(jump * b, 96, 1)))
        return dot_nt(pick, jnp.concatenate([hi, lo], 1))

    def add_sums(raw, c, carry):
        sum_a, sum_b = carry
        face = c * CHUNK + lax.broadcasted_iota(I32, (1, CHUNK), 1)
        area = jnp.where(face < 3 * live, 0.5 * (1.0 - 0.75 * lanes_of(hanging, c).astype(F32)), 0.0)
        is_even = lanes_of(face_dir, c) % 2 == 0
        term_a = area * jnp.where(is_even, raw[1:2], raw[3:4])
        term_b = area * jnp.where(is_even, raw[0:1], raw[2:3])
        cell, other = lanes_of(face_cell, c), lanes_of(face_other, c)
        sum_a += scatter(cell, term_a, CELLS // LANES, low_onehot(cell))
        sum_b += scatter(other, term_b, SLOTS // LANES, low_onehot(other))
        return sum_a, sum_b

    def body(i, carry):
        raw_before, sums = carry
        gather_b(side_b1, 2 * i + 1)
        raw = raw_sums(side_b0, 2 * i)
        sums = add_sums(raw_before, jnp.maximum(2 * i - 1, 0), sums)
        gather_b(side_b0, jnp.minimum(2 * i + 2, CHUNKS - 1))
        raw_after = raw_sums(side_b1, 2 * i + 1)
        sums = add_sums(raw, 2 * i, sums)
        return raw_after, sums

    gather_b(side_b0, 0)
    zero = (jnp.zeros((CELLS // LANES, LANES), F32), jnp.zeros((SLOTS // LANES, LANES), F32))
    raw, sums = lax.fori_loop(0, CHUNKS // 2, body, (jnp.zeros((8, CHUNK), F32), zero))
    sum_a, sum_b = add_sums(raw, CHUNKS - 1, sums)
    for k in SEND_ORDER:
        at = CELLS // LANES + 2 * k
        partial[k] = sum_b[at : at + 2]
    backs = [remote(partial.at[k], returned.at[k], b_send, b_recv, behind(me, -SHIFTS[k])) for k in SEND_ORDER]
    for copy in backs:
        copy.start()
    index = jnp.concatenate([send_v[k : k + 1, :] for k in range(NEIGH)], 1)
    out = term[...] + sum_a + sum_b[: CELLS // LANES]
    remote(partial, returned, b_send, b_recv, behind(me, 1)).wait_recv()
    value = jnp.concatenate([returned[k, r : r + 1, :] for k in range(NEIGH) for r in range(2)], 1)
    out = out + scatter(index, value, CELLS // LANES, onehot[...])
    slot = lax.broadcasted_iota(I32, out.shape, 0) * LANES + lax.broadcasted_iota(I32, out.shape, 1)
    indicator[...] = out

    total = jnp.sum(jnp.where(slot < live, jnp.abs(out), 0.0), axis=0, keepdims=True)
    place = 0
    for stage, (stride, count) in enumerate(STAGES):
        part[stage] = total
        slots = pl.ds(place, count - 1)
        for step in range(1, count):
            remote(part.at[stage], parts.at[place + step - 1], r_send.at[stage], r_recv.at[stage],
                   in_stage(me, stride, count, step)).start()
        remote(parts.at[slots], parts.at[slots], r_send.at[stage], r_recv.at[stage], behind(me, 1)).wait_recv()
        total = total + jnp.sum(parts[place : place + count - 1], axis=0)
        place += count - 1

    mean = jnp.sum(total) / cells.astype(F32)
    facts[...] = jnp.where(slot < live, mean, -1.0)
    remote(partial, returned, b_send, b_recv, behind(me, 1)).wait_send()
    place = 0
    for stage, (stride, count) in enumerate(STAGES):
        slots = pl.ds(place, count - 1)
        remote(parts.at[slots], parts.at[slots], r_send.at[stage], r_recv.at[stage], behind(me, 1)).wait_send()
        place += count - 1


SMEM = pl.BlockSpec(memory_space=pltpu.SMEM)
VMEM = pl.BlockSpec(memory_space=pltpu.VMEM)
ANY = pl.BlockSpec(memory_space=pl.ANY)


def per_device(primal, dual, load, cell_size, cell_count, ghost_send, face_cell, face_other, face_dir, hanging,
               stiffness, recon, traction, trace):
    send = ghost_send[0]
    as_rows = lambda x: x.reshape(-1, LANES)
    f32 = lambda *shape: pltpu.VMEM(shape, F32)
    bf16 = lambda *shape: pltpu.VMEM(shape, BF16)
    i32 = lambda *shape: pltpu.VMEM(shape, I32)
    dma = lambda n: pltpu.SemaphoreType.DMA((n,))
    rows = FACES // LANES
    cells = CELLS // LANES
    steps = sum(size - 1 for _, size in STAGES)
    scratch = [
        f32(DOF, CELLS), f32(DOF, CELLS), f32(DOF, CELLS), f32(cells, LANES), i32(NEIGH, GHOST),
        i32(rows, LANES), i32(rows, LANES), i32(rows, LANES), i32(rows, LANES),
        f32(DOF, DOF), f32(768, CHILD * DOF), f32(6 * FACE_DOF, DOF), f32(6 * FACE_DOF, DOF),
        f32(CELLS, LANES),
        f32(8, LANES), f32(8, LANES), f32(8, LANES), f32(8, LANES), f32(16, LANES),
        f32(NEIGH, PACKED, LANES), f32(NEIGH, PACKED, LANES), f32(NEIGH, PACKED, LANES), f32(NEIGH, PACKED, LANES),
        f32(3 * THIRD, LANES),
        f32(FAMILIES * CHILD + 8, LANES), f32(FAMILIES * CHILD, LANES), f32(FAMILIES, 768), f32(FAMILIES, 768),
        f32(384, 256), bf16(768, 384), f32(3 * SLOTS, LANES), f32(FACES, LANES), f32(CHUNK, LANES), f32(CHUNK, LANES),
        bf16(768, 2304), bf16(LANES, GHOSTS),
        i32(rows, LANES), i32(rows, LANES), pltpu.SMEM((rows, LANES), I32), pltpu.SMEM((rows, LANES), I32),
        f32(cells, LANES), f32(NEIGH, 2, LANES), f32(NEIGH, 2, LANES), f32(len(STAGES), 1, LANES), f32(steps, 1, LANES),
        dma(13), dma(2), dma(2), dma(2), dma(NEIGH), dma(NEIGH), dma(NEIGH), dma(NEIGH),
        pltpu.SemaphoreType.DMA, pltpu.SemaphoreType.DMA, dma(len(STAGES)), dma(len(STAGES)),
    ]
    indicator, facts = pl.pallas_call(
        kernel,
        out_shape=[jax.ShapeDtypeStruct((cells, LANES), F32)] * 2,
        in_specs=[SMEM] * 2 + [ANY] * 13, out_specs=[VMEM] * 2, scratch_shapes=scratch,
        compiler_params=pltpu.CompilerParams(collective_id=0, has_side_effects=True,
                                             vmem_limit_bytes=56 * 1024 * 1024),
        name="indicators",
    )(cell_count, send, primal, dual, load, as_rows(cell_size), send, as_rows(face_cell), as_rows(face_other),
      as_rows(face_dir), as_rows(hanging), stiffness, recon, traction, trace)
    facts = facts.reshape(-1)
    indicator = jnp.where(facts < 0.0, 0.0, indicator.reshape(-1))
    return indicator, jnp.abs(indicator) / (jnp.abs(facts) + 1e-06)

def solution(mesh):
    in_specs = (P(None, "dom"), P(None, "dom"), P(None, "dom"), P("dom"), P(), P("dom", None, None), P("dom"), P("dom"),
                P("dom"), P("dom"), P(), P(), P(), P())
    return jax.shard_map(per_device, mesh=mesh, in_specs=in_specs, out_specs=(P("dom"), P("dom")), check_vma=False)
```

```python
import functools

import jax
import jax.numpy as jnp
from jax import lax
from jax.experimental import pallas as pl
from jax.experimental.pallas import tpu as pltpu
from jax.sharding import PartitionSpec as P

F32 = jnp.float32
BF16 = jnp.bfloat16
I32 = jnp.int32

DOF = 81
FACE_DOF = 27
CHILD = 8
CELLS = 2048
NEIGH = 8
GHOST = 256
GHOSTS = NEIGH * GHOST
SLOTS = CELLS + GHOSTS
FACES = 6144
LANES = 128
FAMILIES = 272
THIRD = 88
PACKED = 2 * THIRD
CHUNK = 256
CHUNKS = FACES // CHUNK
SPLIT = CHUNK // LANES


def split(x):
    high = x.astype(BF16)
    return high, (x - high.astype(F32)).astype(BF16)


def dot_nt(a, b):
    return lax.dot_general(a, b, (((1,), (1,)), ((), ())), preferred_element_type=F32)


def dot_nn(a, b):
    return lax.dot_general(a, b, (((1,), (0,)), ((), ())), preferred_element_type=F32)


def gather_rows(dst, dst_at, src, index_of, count):
    sub = lax.broadcasted_iota(I32, (8, LANES), 0)
    for base in range(0, count, 8):
        rows = [src[pl.ds(index_of(base + u), 1), :] for u in range(8)]
        tile = jnp.broadcast_to(rows[0], (8, LANES))
        for u in range(1, 8):
            tile = jnp.where(sub == u, jnp.broadcast_to(rows[u], (8, LANES)), tile)
        dst[pl.ds(pl.multiple_of(dst_at + base, 8), 8), :] = tile


def turned_block(src, at):
    return jnp.concatenate([src[:, pl.ds(at, 256)], jnp.zeros((LANES - DOF, 256), F32)], 0).T


def to_cell_major(dst, row, src, step):
    at = pl.multiple_of(step * 256, 256)
    dst[pl.ds(pl.multiple_of(row + at, CHILD), 256), :] = turned_block(src, at)


def pack(to, rows):
    lane = lax.broadcasted_iota(I32, (THIRD, LANES), 1)
    second = pltpu.roll(rows[THIRD : 2 * THIRD, :], DOF, 1)
    third = pltpu.roll(rows[2 * THIRD :, :], 2 * DOF - LANES, 1)
    upper = jnp.where(lane < DOF, rows[0:THIRD, :], second)
    to[...] = jnp.concatenate([upper, jnp.where(lane < 2 * DOF - LANES, second, third)], 0)


def unpack(rows):
    lane = lax.broadcasted_iota(I32, (THIRD, LANES), 1)
    upper, lower = rows[:THIRD], rows[THIRD:]
    second = pltpu.roll(jnp.where(lane < 2 * DOF - LANES, lower, upper), LANES - DOF, 1)
    third = pltpu.roll(lower, 2 * LANES - 2 * DOF, 1)
    return jnp.concatenate([upper, second, third[: GHOST - PACKED]], 0)


def fill_operator(operator, traction, trace):
    operator[...] = jnp.zeros(operator.shape, F32)
    for d in range(6):
        rows = slice(d * FACE_DOF, (d + 1) * FACE_DOF)
        operator[64 * d : 64 * d + FACE_DOF, 0:DOF] = traction[rows, :]
        operator[64 * d + 32 : 64 * d + 32 + FACE_DOF, LANES : LANES + DOF] = trace[rows, :]


def fill_table(table, slot, p_rows, w_rows, operator):
    hi, lo = split(jnp.concatenate([p_rows, w_rows], 1))
    out = dot_nn(jnp.concatenate([hi, lo, hi], 1), operator[...])
    for pair in range(3):
        table[pl.ds(pl.multiple_of(pair * SLOTS + slot, 256), 256), :] = out[:, pair * LANES : (pair + 1) * LANES]
    return hi[:, LANES:], lo[:, LANES:]


def take_residual(load, primal, stiffness, step):
    cells = pl.ds(pl.multiple_of(step * 256, 256), 256)
    s_hi, s_lo = split(stiffness[...])
    p_hi, p_lo = split(primal[:, cells])
    load[:, cells] = load[:, cells] - (dot_nn(s_hi, p_hi) + dot_nn(s_lo, p_hi) + dot_nn(s_hi, p_lo))


def cell_terms(out, residual, w_hi, w_lo, cell_size, step):
    r_hi, r_lo = split(residual[:, pl.ds(pl.multiple_of(step * 256, 256), 256)])
    square = (LANES, LANES)
    same = lax.broadcasted_iota(I32, square, 0) == lax.broadcasted_iota(I32, square, 1)
    for r in range(2):
        part = slice(r * LANES, (r + 1) * LANES)
        w_h, w_l, r_h, r_l = w_hi[part, :DOF], w_lo[part, :DOF], r_hi[:, part], r_lo[:, part]
        pairs = dot_nn(w_h, r_h) + dot_nn(w_l, r_h) + dot_nn(w_h, r_l)
        total = jnp.sum(jnp.where(same, pairs, 0.0), axis=0, keepdims=True)
        i = step * 2 + r
        out[pl.ds(i, 1), :] = cell_size[pl.ds(i, 1), :] * total


def lanes_of(ref, chunk):
    return jnp.concatenate([ref[pl.ds(chunk * SPLIT + i, 1), :] for i in range(SPLIT)], 1)


def low_onehot(index):
    low = lax.broadcasted_iota(I32, (LANES, index.shape[1]), 0) == index % LANES
    return jnp.where(low, 1.0, 0.0).astype(BF16)


def scatter(index, value, high_count, onehot):
    high = lax.broadcasted_iota(I32, (high_count, index.shape[1]), 0) == index // LANES
    both = dot_nt(jnp.concatenate(split(jnp.where(high, value, 0.0)), 0), onehot)
    return both[:high_count] + both[high_count:]


MESH = pl.DeviceIdType.MESH
RANKS = 128
SHIFTS = [(1 << which // 2) * (1 - 2 * (which % 2)) for which in range(NEIGH)]
FIRST_LIST = 4
LATE = 2
EARLY = FACES // LANES - NEIGH * LATE
SEND_ORDER = [4, 5, 6, 7, 2, 3, 0, 1]
STAGES = ((1, 8), (8, 16))


def counts_of(counts, me):
    def body(i, carry):
        before, here, cells = carry
        c = counts[i]
        return before + jnp.where(i < me, c, 0), here + jnp.where(i == me, c, 0), cells + c

    return lax.fori_loop(0, RANKS, body, (jnp.int32(0), jnp.int32(0), jnp.int32(0)), unroll=32)


def behind(me, by):
    return lax.rem(me + (by + RANKS), RANKS)


def shift_of(k):
    e = k // 2
    power = 1 + e + e * (e - 1) // 2 + e * (e - 1) * (e - 2) // 6
    return power * (1 - 2 * (k % 2))


def in_stage(me, stride, size, step):
    place = lax.rem(me // stride, size)
    return me + (lax.rem(place + step, size) - place) * stride


def gather_list(picked, source, send, k):
    gather_rows(picked, 0, source, lambda i: send[k, i], GHOST)


def rebuild(head, live, padded, after, after2, recon3, families, rebuilt, woven):
    after2[0:8, :] = jnp.zeros((8, LANES), F32)
    after2[8:16, :] = after[...]
    own = lax.rem(live - head + CHILD, CHILD)
    split_family = 1 + (live - head) // CHILD
    row = lax.broadcasted_iota(I32, (FAMILIES, LANES), 0)
    families[:, 640:768] = jnp.zeros((FAMILIES, LANES), F32)
    for m in range(CHILD):
        cells = padded[pl.ds(head + m, FAMILIES, stride=CHILD), :]
        late = after2[pl.ds(CHILD + m - own, 1), :]
        cells = jnp.where((row == split_family) & (m >= own), late, cells)
        families[:, m * DOF : (m + 1) * DOF] = cells[:, :DOF]
    hi, lo = split(families[...])
    rebuilt[:, : CHILD * DOF] = dot_nt(jnp.concatenate([hi, lo, hi], 1), recon3[0 : CHILD * DOF, :])
    lane = lax.broadcasted_iota(I32, (FAMILIES, LANES), 1)
    for m in range(CHILD):
        part = rebuilt[:, m * DOF : m * DOF + LANES]
        woven[pl.ds(m, FAMILIES, stride=CHILD), :] = jnp.where(lane < DOF, part, 0.0)


def kernel(counts, send, primal_in, dual_in, load_in, size_in, send_in, cell_in, other_in, dir_in, hanging_in,
           stiffness_in, recon_in, traction_in, trace_in,
           indicator, facts,
           primal, dual, load, cell_size, send_v, face_cell, face_other, face_dir, hanging, stiffness, recon, traction,
           trace, p_t, first, last, before, after, after2, p_out, p_in, w_out, w_in, picked, padded, woven, families, rebuilt,
           operator, operator3, table, side_a, side_b0, side_b1, recon3, onehot, index_a, index_b, smem_a, smem_b, term, partial, returned, part, parts,
           in_sem, index_sem, edge_send, edge_recv, p_send, p_recv, w_send, w_recv, b_send, b_recv, r_send, r_recv):
    me = lax.axis_index("dom")
    staged = [(primal_in, primal), (dual_in, dual), (recon_in, recon.at[pl.ds(0, CHILD * DOF), :]), (traction_in, traction), (trace_in, trace),
              (load_in, load), (size_in, cell_size), (stiffness_in, stiffness), (cell_in, face_cell),
              (other_in, face_other), (dir_in, face_dir), (hanging_in, hanging), (send_in, send_v)]
    loads = {}
    for i, (source, to) in enumerate(staged):
        loads[i] = pltpu.make_async_copy(source, to, in_sem.at[i])
        loads[i].start()

    barrier = pltpu.get_barrier_semaphore()
    partners = [behind(me, shift) for shift in SHIFTS]
    for stride, size in STAGES:
        partners += [in_stage(me, stride, size, step) for step in range(1, size)]
    for partner in partners:
        pl.semaphore_signal(barrier, inc=1, device_id=(partner,), device_id_type=MESH)

    start, live, cells = counts_of(counts, me)
    head = lax.rem(CHILD - lax.rem(start, CHILD), CHILD)

    def remote(source, to, send_sem, recv_sem, target):
        return pltpu.make_async_remote_copy(src_ref=source, dst_ref=to, send_sem=send_sem, recv_sem=recv_sem,
                                            device_id=(target,), device_id_type=MESH)

    def list_copy(source, to, send_sem, recv_sem, k):
        return remote(source.at[k], to.at[k], send_sem.at[k], recv_sem.at[k], behind(me, shift_of(k)))

    loads[0].wait()
    loads[1].wait()
    for step in range(8):
        to_cell_major(p_t, 0, primal, step)
    cell = lax.broadcasted_iota(I32, (16, CELLS), 1)
    row = lax.broadcasted_iota(I32, (16, CELLS), 0)
    picked_cell = jnp.where(row < CHILD, row, live - 2 * CHILD + row)
    chosen = jnp.where(cell == picked_cell, 1.0, 0.0).astype(BF16)
    hi, lo = split(dual[...])
    ends = dot_nt(chosen, hi) + dot_nt(chosen, lo)
    first[...] = jnp.zeros((8, LANES), F32)
    last[...] = jnp.zeros((8, LANES), F32)
    first[:, :DOF] = ends[:CHILD]
    last[:, :DOF] = ends[CHILD:]
    pl.semaphore_wait(barrier, len(partners))
    edges = [remote(last, before, edge_send.at[0], edge_recv.at[0], behind(me, 1)),
             remote(first, after, edge_send.at[1], edge_recv.at[1], behind(me, -1))]
    for copy in edges:
        copy.start()

    for i in range(2, len(staged)):
        loads[i].wait()

    def send_primal(step, carry):
        k = lax.rem(step + FIRST_LIST, NEIGH)
        gather_list(picked, p_t, send, k)
        to_cell_major(padded, CHILD, dual, step)
        take_residual(load, primal, stiffness, step)
        onehot[:, pl.ds(pl.multiple_of(step * GHOST, GHOST), GHOST)] = low_onehot(send_v[pl.ds(step, 1), :])
        rows = pl.ds(pl.multiple_of(step * 96, 96), 96)
        wide = jnp.concatenate([recon[rows, :], jnp.zeros((96, 768 - CHILD * DOF), F32)], 1)
        hi, lo = split(wide)
        recon3[rows, 0:768] = hi
        recon3[rows, 768:1536] = hi
        recon3[rows, 1536:2304] = lo
        pack(p_out.at[k], picked)
        list_copy(p_out, p_in, p_send, p_recv, k).start()
        return carry

    lax.fori_loop(0, NEIGH, send_primal, 0)
    padded[CELLS + 8 :, :] = jnp.zeros((padded.shape[0] - CELLS - 8, LANES), F32)

    fill_operator(operator, traction, trace)
    hi, lo = split(operator[...].T)
    operator3[0:256, :] = hi
    operator3[256:512, :] = hi
    operator3[512:768, :] = lo
    pair = (face_dir[...] // 2) * SLOTS
    index_a[...] = pair + face_cell[...]
    index_b[...] = pair + face_other[...]
    copy_a = pltpu.make_async_copy(index_a, smem_a, index_sem.at[0])
    copy_b = pltpu.make_async_copy(index_b, smem_b, index_sem.at[1])
    copy_a.start()
    copy_b.start()

    for copy in edges:
        copy.wait()
    padded[0:8, :] = before[...]
    rebuild(head, live, padded, after, after2, recon3, families, rebuilt, woven)

    def send_weight(step, carry):
        k = lax.rem(step + FIRST_LIST, NEIGH)
        at = pl.multiple_of(step * 256, 256)
        gather_rows(picked, 0, woven, lambda i: send[k, i] + (CHILD - head), GHOST)
        w_hi, w_lo = fill_table(table, at, p_t[pl.ds(at, 256), :], woven[pl.ds(CHILD - head + at, 256), :], operator3)
        cell_terms(term, load, w_hi, w_lo, cell_size, step)
        pack(w_out.at[k], picked)
        list_copy(w_out, w_in, w_send, w_recv, k).start()
        return carry

    lax.fori_loop(0, NEIGH, send_weight, 0)
    copy_a.wait()
    copy_b.wait()

    def gather_a(r, carry):
        gather_rows(side_a, r * LANES, table, lambda i: smem_a[r, i], LANES)
        return carry

    def take_ghosts(step, carry):
        k = lax.rem(step + FIRST_LIST, NEIGH)
        list_copy(p_out, p_in, p_send, p_recv, k).wait()
        list_copy(w_out, w_in, w_send, w_recv, k).wait()
        row = EARLY + step * LATE
        gather_rows(side_a, row * LANES, table, lambda i: smem_a[row + i // LANES, i % LANES], LATE * LANES)
        fill_table(table, CELLS + k * GHOST, unpack(p_in[k]), unpack(w_in[k]), operator3)
        return carry

    lax.fori_loop(0, EARLY, gather_a, 0)
    lax.fori_loop(0, NEIGH, take_ghosts, 0)

    lane = lax.broadcasted_iota(I32, (8, 2 * LANES), 1) % LANES
    sub = lax.broadcasted_iota(I32, (8, 2 * LANES), 0)
    pick = jnp.where(lane // 32 == sub, 1.0, 0.0).astype(BF16)
    upper = lax.broadcasted_iota(I32, (CHUNK, LANES), 1) % 64 >= 32

    def gather_b(to, c):
        gather_rows(to, 0, table, lambda i: smem_b[c * SPLIT + i // LANES, i % LANES], CHUNK)

    def raw_sums(side_b, c):
        a = side_a[pl.ds(pl.multiple_of(c * CHUNK, CHUNK), CHUNK), :]
        b = pltpu.roll(side_b[...], 64, 1)
        jump = pltpu.roll(a + b, 32, 1)
        hi, lo = split(jnp.where(upper, jump * a, pltpu.roll(jump * b, 96, 1)))
        return dot_nt(pick, jnp.concatenate([hi, lo], 1))

    def add_sums(raw, c, carry):
        sum_a, sum_b = carry
        face = c * CHUNK + lax.broadcasted_iota(I32, (1, CHUNK), 1)
        area = jnp.where(face < 3 * live, 0.5 * (1.0 - 0.75 * lanes_of(hanging, c).astype(F32)), 0.0)
        is_even = lanes_of(face_dir, c) % 2 == 0
        term_a = area * jnp.where(is_even, raw[1:2], raw[3:4])
        term_b = area * jnp.where(is_even, raw[0:1], raw[2:3])
        cell, other = lanes_of(face_cell, c), lanes_of(face_other, c)
        sum_a += scatter(cell, term_a, CELLS // LANES, low_onehot(cell))
        sum_b += scatter(other, term_b, SLOTS // LANES, low_onehot(other))
        return sum_a, sum_b

    def body(i, carry):
        raw_before, sums = carry
        gather_b(side_b1, 2 * i + 1)
        raw = raw_sums(side_b0, 2 * i)
        sums = add_sums(raw_before, jnp.maximum(2 * i - 1, 0), sums)
        gather_b(side_b0, jnp.minimum(2 * i + 2, CHUNKS - 1))
        raw_after = raw_sums(side_b1, 2 * i + 1)
        sums = add_sums(raw, 2 * i, sums)
        return raw_after, sums

    gather_b(side_b0, 0)
    zero = (jnp.zeros((CELLS // LANES, LANES), F32), jnp.zeros((SLOTS // LANES, LANES), F32))
    raw, sums = lax.fori_loop(0, CHUNKS // 2, body, (jnp.zeros((8, CHUNK), F32), zero))
    sum_a, sum_b = add_sums(raw, CHUNKS - 1, sums)
    for k in SEND_ORDER:
        at = CELLS // LANES + 2 * k
        partial[k] = sum_b[at : at + 2]
    backs = [remote(partial.at[k], returned.at[k], b_send, b_recv, behind(me, -SHIFTS[k])) for k in SEND_ORDER]
    for copy in backs:
        copy.start()
    index = jnp.concatenate([send_v[k : k + 1, :] for k in range(NEIGH)], 1)
    out = term[...] + sum_a + sum_b[: CELLS // LANES]
    remote(partial, returned, b_send, b_recv, behind(me, 1)).wait_recv()
    value = jnp.concatenate([returned[k, r : r + 1, :] for k in range(NEIGH) for r in range(2)], 1)
    out = out + scatter(index, value, CELLS // LANES, onehot[...])
    slot = lax.broadcasted_iota(I32, out.shape, 0) * LANES + lax.broadcasted_iota(I32, out.shape, 1)
    indicator[...] = out

    total = jnp.sum(jnp.where(slot < live, jnp.abs(out), 0.0), axis=0, keepdims=True)
    place = 0
    for stage, (stride, count) in enumerate(STAGES):
        part[stage] = total
        slots = pl.ds(place, count - 1)
        for step in range(1, count):
            remote(part.at[stage], parts.at[place + step - 1], r_send.at[stage], r_recv.at[stage],
                   in_stage(me, stride, count, step)).start()
        remote(parts.at[slots], parts.at[slots], r_send.at[stage], r_recv.at[stage], behind(me, 1)).wait_recv()
        total = total + jnp.sum(parts[place : place + count - 1], axis=0)
        place += count - 1

    mean = jnp.sum(total) / cells.astype(F32)
    facts[...] = jnp.where(slot < live, mean, -1.0)
    remote(partial, returned, b_send, b_recv, behind(me, 1)).wait_send()
    place = 0
    for stage, (stride, count) in enumerate(STAGES):
        slots = pl.ds(place, count - 1)
        remote(parts.at[slots], parts.at[slots], r_send.at[stage], r_recv.at[stage], behind(me, 1)).wait_send()
        place += count - 1


SMEM = pl.BlockSpec(memory_space=pltpu.SMEM)
VMEM = pl.BlockSpec(memory_space=pltpu.VMEM)
ANY = pl.BlockSpec(memory_space=pl.ANY)


def per_device(primal, dual, load, cell_size, cell_count, ghost_send, face_cell, face_other, face_dir, hanging,
               stiffness, recon, traction, trace):
    send = ghost_send[0]
    as_rows = lambda x: x.reshape(-1, LANES)
    f32 = lambda *shape: pltpu.VMEM(shape, F32)
    bf16 = lambda *shape: pltpu.VMEM(shape, BF16)
    i32 = lambda *shape: pltpu.VMEM(shape, I32)
    dma = lambda n: pltpu.SemaphoreType.DMA((n,))
    rows = FACES // LANES
    cells = CELLS // LANES
    steps = sum(size - 1 for _, size in STAGES)
    scratch = [
        f32(DOF, CELLS), f32(DOF, CELLS), f32(DOF, CELLS), f32(cells, LANES), i32(NEIGH, GHOST),
        i32(rows, LANES), i32(rows, LANES), i32(rows, LANES), i32(rows, LANES),
        f32(DOF, DOF), f32(768, CHILD * DOF), f32(6 * FACE_DOF, DOF), f32(6 * FACE_DOF, DOF),
        f32(CELLS, LANES),
        f32(8, LANES), f32(8, LANES), f32(8, LANES), f32(8, LANES), f32(16, LANES),
        f32(NEIGH, PACKED, LANES), f32(NEIGH, PACKED, LANES), f32(NEIGH, PACKED, LANES), f32(NEIGH, PACKED, LANES),
        f32(3 * THIRD, LANES),
        f32(FAMILIES * CHILD + 8, LANES), f32(FAMILIES * CHILD, LANES), f32(FAMILIES, 768), f32(FAMILIES, 768),
        f32(384, 256), bf16(768, 384), f32(3 * SLOTS, LANES), f32(FACES, LANES), f32(CHUNK, LANES), f32(CHUNK, LANES),
        bf16(768, 2304), bf16(LANES, GHOSTS),
        i32(rows, LANES), i32(rows, LANES), pltpu.SMEM((rows, LANES), I32), pltpu.SMEM((rows, LANES), I32),
        f32(cells, LANES), f32(NEIGH, 2, LANES), f32(NEIGH, 2, LANES), f32(len(STAGES), 1, LANES), f32(steps, 1, LANES),
        dma(13), dma(2), dma(2), dma(2), dma(NEIGH), dma(NEIGH), dma(NEIGH), dma(NEIGH),
        pltpu.SemaphoreType.DMA, pltpu.SemaphoreType.DMA, dma(len(STAGES)), dma(len(STAGES)),
    ]
    indicator, facts = pl.pallas_call(
        kernel,
        out_shape=[jax.ShapeDtypeStruct((cells, LANES), F32)] * 2,
        in_specs=[SMEM] * 2 + [ANY] * 13, out_specs=[VMEM] * 2, scratch_shapes=scratch,
        compiler_params=pltpu.CompilerParams(collective_id=0, has_side_effects=True,
                                             vmem_limit_bytes=56 * 1024 * 1024),
        name="indicators",
    )(cell_count, send, primal, dual, load, as_rows(cell_size), send, as_rows(face_cell), as_rows(face_other),
      as_rows(face_dir), as_rows(hanging), stiffness, recon, traction, trace)
    facts = facts.reshape(-1)
    indicator = jnp.where(facts < 0.0, 0.0, indicator.reshape(-1))
    return indicator, jnp.abs(indicator) / (jnp.abs(facts) + 1e-06)

def solution(mesh):
    in_specs = (P(None, "dom"), P(None, "dom"), P(None, "dom"), P("dom"), P(), P("dom", None, None), P("dom"), P("dom"),
                P("dom"), P("dom"), P(), P(), P(), P())
    return jax.shard_map(per_device, mesh=mesh, in_specs=in_specs, out_specs=(P("dom"), P("dom")), check_vma=False)
```

```python
import functools

import jax
import jax.numpy as jnp
from jax import lax
from jax.experimental import pallas as pl
from jax.experimental.pallas import tpu as pltpu
from jax.sharding import PartitionSpec as P

F32 = jnp.float32
BF16 = jnp.bfloat16
I32 = jnp.int32

DOF = 81
FACE_DOF = 27
CHILD = 8
CELLS = 2048
NEIGH = 8
GHOST = 256
GHOSTS = NEIGH * GHOST
SLOTS = CELLS + GHOSTS
FACES = 6144
LANES = 128
FAMILIES = 272
THIRD = 88
PACKED = 2 * THIRD
CHUNK = 256
CHUNKS = FACES // CHUNK
SPLIT = CHUNK // LANES


def split(x):
    high = x.astype(BF16)
    return high, (x - high.astype(F32)).astype(BF16)


def dot_nt(a, b):
    return lax.dot_general(a, b, (((1,), (1,)), ((), ())), preferred_element_type=F32)


def dot_nn(a, b):
    return lax.dot_general(a, b, (((1,), (0,)), ((), ())), preferred_element_type=F32)


def gather_rows(dst, dst_at, src, index_of, count):
    sub = lax.broadcasted_iota(I32, (8, LANES), 0)
    for base in range(0, count, 8):
        rows = [src[pl.ds(index_of(base + u), 1), :] for u in range(8)]
        tile = jnp.broadcast_to(rows[0], (8, LANES))
        for u in range(1, 8):
            tile = jnp.where(sub == u, jnp.broadcast_to(rows[u], (8, LANES)), tile)
        dst[pl.ds(pl.multiple_of(dst_at + base, 8), 8), :] = tile


def turned_block(src, at):
    return jnp.concatenate([src[:, pl.ds(at, 256)], jnp.zeros((LANES - DOF, 256), F32)], 0).T


def to_cell_major(dst, row, src, step):
    at = pl.multiple_of(step * 256, 256)
    dst[pl.ds(pl.multiple_of(row + at, CHILD), 256), :] = turned_block(src, at)


def pack(to, rows):
    lane = lax.broadcasted_iota(I32, (THIRD, LANES), 1)
    second = pltpu.roll(rows[THIRD : 2 * THIRD, :], DOF, 1)
    third = pltpu.roll(rows[2 * THIRD :, :], 2 * DOF - LANES, 1)
    upper = jnp.where(lane < DOF, rows[0:THIRD, :], second)
    to[...] = jnp.concatenate([upper, jnp.where(lane < 2 * DOF - LANES, second, third)], 0)


def unpack(rows):
    lane = lax.broadcasted_iota(I32, (THIRD, LANES), 1)
    upper, lower = rows[:THIRD], rows[THIRD:]
    second = pltpu.roll(jnp.where(lane < 2 * DOF - LANES, lower, upper), LANES - DOF, 1)
    third = pltpu.roll(lower, 2 * LANES - 2 * DOF, 1)
    return jnp.concatenate([upper, second, third[: GHOST - PACKED]], 0)


def fill_operator(operator, traction, trace):
    operator[...] = jnp.zeros(operator.shape, F32)
    for d in range(6):
        rows = slice(d * FACE_DOF, (d + 1) * FACE_DOF)
        operator[64 * d : 64 * d + FACE_DOF, 0:DOF] = traction[rows, :]
        operator[64 * d + 32 : 64 * d + 32 + FACE_DOF, LANES : LANES + DOF] = trace[rows, :]


def fill_table(table, slot, p_rows, w_rows, operator):
    hi, lo = split(jnp.concatenate([p_rows, w_rows], 1))
    out = dot_nn(jnp.concatenate([hi, lo, hi], 1), operator[...])
    for pair in range(3):
        table[pl.ds(pl.multiple_of(pair * SLOTS + slot, 256), 256), :] = out[:, pair * LANES : (pair + 1) * LANES]


def take_residual(load, primal, stiffness, step):
    cells = pl.ds(pl.multiple_of(step * 256, 256), 256)
    s_hi, s_lo = split(stiffness[...])
    p_hi, p_lo = split(primal[:, cells])
    load[:, cells] = load[:, cells] - (dot_nn(s_hi, p_hi) + dot_nn(s_lo, p_hi) + dot_nn(s_hi, p_lo))


def cell_terms(out, residual, woven, skip, cell_size, step):
    cells = pl.ds(pl.multiple_of(step * 256, 256), 256)
    total = jnp.sum(residual[:, cells] * woven[pl.ds(skip + step * 256, 256), :].T[:DOF, :], axis=0, keepdims=True)
    for r in range(2):
        i = step * 2 + r
        out[pl.ds(i, 1), :] = cell_size[pl.ds(i, 1), :] * total[:, r * LANES : (r + 1) * LANES]


def lanes_of(ref, chunk):
    return jnp.concatenate([ref[pl.ds(chunk * SPLIT + i, 1), :] for i in range(SPLIT)], 1)


def low_onehot(index):
    low = lax.broadcasted_iota(I32, (LANES, index.shape[1]), 0) == index % LANES
    return jnp.where(low, 1.0, 0.0).astype(BF16)


def scatter(index, value, high_count, onehot):
    high = lax.broadcasted_iota(I32, (high_count, index.shape[1]), 0) == index // LANES
    both = dot_nt(jnp.concatenate(split(jnp.where(high, value, 0.0)), 0), onehot)
    return both[:high_count] + both[high_count:]


MESH = pl.DeviceIdType.MESH
RANKS = 128
SHIFTS = [(1 << which // 2) * (1 - 2 * (which % 2)) for which in range(NEIGH)]
FIRST_LIST = 4
LATE = 3
EARLY = FACES // LANES - NEIGH * LATE
SEND_ORDER = [4, 5, 6, 7, 2, 3, 0, 1]
STAGES = ((1, 8), (8, 16))


def counts_of(counts, me):
    def body(i, carry):
        before, here, cells = carry
        c = counts[i]
        return before + jnp.where(i < me, c, 0), here + jnp.where(i == me, c, 0), cells + c

    return lax.fori_loop(0, RANKS, body, (jnp.int32(0), jnp.int32(0), jnp.int32(0)), unroll=32)


def behind(me, by):
    return lax.rem(me + (by + RANKS), RANKS)


def shift_of(k):
    e = k // 2
    power = 1 + e + e * (e - 1) // 2 + e * (e - 1) * (e - 2) // 6
    return power * (1 - 2 * (k % 2))


def in_stage(me, stride, size, step):
    place = lax.rem(me // stride, size)
    return me + (lax.rem(place + step, size) - place) * stride


def gather_list(picked, source, send, k):
    gather_rows(picked, 0, source, lambda i: send[k, i], GHOST)


def rebuild(head, live, padded, after, after2, recon3, families, rebuilt, woven):
    after2[0:8, :] = jnp.zeros((8, LANES), F32)
    after2[8:16, :] = after[...]
    own = lax.rem(live - head + CHILD, CHILD)
    split_family = 1 + (live - head) // CHILD
    row = lax.broadcasted_iota(I32, (FAMILIES, LANES), 0)
    families[:, 640:768] = jnp.zeros((FAMILIES, LANES), F32)
    for m in range(CHILD):
        cells = padded[pl.ds(head + m, FAMILIES, stride=CHILD), :]
        late = after2[pl.ds(CHILD + m - own, 1), :]
        cells = jnp.where((row == split_family) & (m >= own), late, cells)
        families[:, m * DOF : (m + 1) * DOF] = cells[:, :DOF]
    hi, lo = split(families[...])
    rebuilt[:, : CHILD * DOF] = dot_nt(jnp.concatenate([hi, lo, hi], 1), recon3[0 : CHILD * DOF, :])
    lane = lax.broadcasted_iota(I32, (FAMILIES, LANES), 1)
    for m in range(CHILD):
        part = rebuilt[:, m * DOF : m * DOF + LANES]
        woven[pl.ds(m, FAMILIES, stride=CHILD), :] = jnp.where(lane < DOF, part, 0.0)


def kernel(counts, send, primal_in, dual_in, load_in, size_in, send_in, cell_in, other_in, dir_in, hanging_in,
           stiffness_in, recon_in, traction_in, trace_in,
           indicator, facts,
           primal, dual, load, cell_size, send_v, face_cell, face_other, face_dir, hanging, stiffness, recon, traction,
           trace, p_t, first, last, before, after, after2, p_out, p_in, w_out, w_in, picked, padded, woven, families, rebuilt,
           operator, operator3, table, side_a, side_b0, side_b1, recon3, onehot, index_a, index_b, smem_a, smem_b, term, partial, returned, part, parts,
           in_sem, index_sem, edge_send, edge_recv, p_send, p_recv, w_send, w_recv, b_send, b_recv, r_send, r_recv):
    me = lax.axis_index("dom")
    staged = [(primal_in, primal), (dual_in, dual), (recon_in, recon.at[pl.ds(0, CHILD * DOF), :]), (traction_in, traction), (trace_in, trace),
              (load_in, load), (size_in, cell_size), (stiffness_in, stiffness), (cell_in, face_cell),
              (other_in, face_other), (dir_in, face_dir), (hanging_in, hanging), (send_in, send_v)]
    loads = {}
    for i, (source, to) in enumerate(staged):
        loads[i] = pltpu.make_async_copy(source, to, in_sem.at[i])
        loads[i].start()

    barrier = pltpu.get_barrier_semaphore()
    partners = [behind(me, shift) for shift in SHIFTS]
    for stride, size in STAGES:
        partners += [in_stage(me, stride, size, step) for step in range(1, size)]
    for partner in partners:
        pl.semaphore_signal(barrier, inc=1, device_id=(partner,), device_id_type=MESH)

    start, live, cells = counts_of(counts, me)
    head = lax.rem(CHILD - lax.rem(start, CHILD), CHILD)

    def remote(source, to, send_sem, recv_sem, target):
        return pltpu.make_async_remote_copy(src_ref=source, dst_ref=to, send_sem=send_sem, recv_sem=recv_sem,
                                            device_id=(target,), device_id_type=MESH)

    def list_copy(source, to, send_sem, recv_sem, k):
        return remote(source.at[k], to.at[k], send_sem.at[k], recv_sem.at[k], behind(me, shift_of(k)))

    def transpose_primal(step, carry):
        to_cell_major(p_t, 0, primal, step)
        return carry

    loads[0].wait()
    lax.fori_loop(0, 8, transpose_primal, 0)
    loads[1].wait()
    cell = lax.broadcasted_iota(I32, (16, CELLS), 1)
    row = lax.broadcasted_iota(I32, (16, CELLS), 0)
    picked_cell = jnp.where(row < CHILD, row, live - 2 * CHILD + row)
    chosen = jnp.where(cell == picked_cell, 1.0, 0.0).astype(BF16)
    hi, lo = split(dual[...])
    ends = dot_nt(chosen, hi) + dot_nt(chosen, lo)
    first[...] = jnp.zeros((8, LANES), F32)
    last[...] = jnp.zeros((8, LANES), F32)
    first[:, :DOF] = ends[:CHILD]
    last[:, :DOF] = ends[CHILD:]
    pl.semaphore_wait(barrier, len(partners))
    edges = [remote(last, before, edge_send.at[0], edge_recv.at[0], behind(me, 1)),
             remote(first, after, edge_send.at[1], edge_recv.at[1], behind(me, -1))]
    for copy in edges:
        copy.start()

    for i in range(2, len(staged)):
        loads[i].wait()

    def send_primal(step, carry):
        k = lax.rem(step + FIRST_LIST, NEIGH)
        gather_list(picked, p_t, send, k)
        to_cell_major(padded, CHILD, dual, step)
        take_residual(load, primal, stiffness, step)
        onehot[:, pl.ds(pl.multiple_of(step * GHOST, GHOST), GHOST)] = low_onehot(send_v[pl.ds(step, 1), :])
        rows = pl.ds(pl.multiple_of(step * 96, 96), 96)
        wide = jnp.concatenate([recon[rows, :], jnp.zeros((96, 768 - CHILD * DOF), F32)], 1)
        hi, lo = split(wide)
        recon3[rows, 0:768] = hi
        recon3[rows, 768:1536] = hi
        recon3[rows, 1536:2304] = lo
        pack(p_out.at[k], picked)
        list_copy(p_out, p_in, p_send, p_recv, k).start()
        return carry

    lax.fori_loop(0, NEIGH, send_primal, 0)
    padded[CELLS + 8 :, :] = jnp.zeros((padded.shape[0] - CELLS - 8, LANES), F32)

    fill_operator(operator, traction, trace)
    hi, lo = split(operator[...].T)
    operator3[0:256, :] = hi
    operator3[256:512, :] = hi
    operator3[512:768, :] = lo
    pair = (face_dir[...] // 2) * SLOTS
    index_a[...] = pair + face_cell[...]
    index_b[...] = pair + face_other[...]
    copy_a = pltpu.make_async_copy(index_a, smem_a, index_sem.at[0])
    copy_b = pltpu.make_async_copy(index_b, smem_b, index_sem.at[1])
    copy_a.start()
    copy_b.start()

    for copy in edges:
        copy.wait()
    padded[0:8, :] = before[...]
    rebuild(head, live, padded, after, after2, recon3, families, rebuilt, woven)

    def send_weight(step, carry):
        k = lax.rem(step + FIRST_LIST, NEIGH)
        at = pl.multiple_of(step * 256, 256)
        gather_rows(picked, 0, woven, lambda i: send[k, i] + (CHILD - head), GHOST)
        fill_table(table, at, p_t[pl.ds(at, 256), :], woven[pl.ds(CHILD - head + at, 256), :], operator3)
        cell_terms(term, load, woven, CHILD - head, cell_size, step)
        pack(w_out.at[k], picked)
        list_copy(w_out, w_in, w_send, w_recv, k).start()
        return carry

    lax.fori_loop(0, NEIGH, send_weight, 0)
    copy_a.wait()
    copy_b.wait()

    def gather_a(r, carry):
        gather_rows(side_a, r * LANES, table, lambda i: smem_a[r, i], LANES)
        return carry

    def take_ghosts(step, carry):
        k = lax.rem(step + FIRST_LIST, NEIGH)
        list_copy(p_out, p_in, p_send, p_recv, k).wait()
        list_copy(w_out, w_in, w_send, w_recv, k).wait()
        row = EARLY + step * LATE
        gather_rows(side_a, row * LANES, table, lambda i: smem_a[row + i // LANES, i % LANES], LATE * LANES)
        fill_table(table, CELLS + k * GHOST, unpack(p_in[k]), unpack(w_in[k]), operator3)
        return carry

    lax.fori_loop(0, EARLY, gather_a, 0)
    lax.fori_loop(0, NEIGH, take_ghosts, 0)

    lane = lax.broadcasted_iota(I32, (8, 2 * LANES), 1) % LANES
    sub = lax.broadcasted_iota(I32, (8, 2 * LANES), 0)
    pick = jnp.where(lane // 32 == sub, 1.0, 0.0).astype(BF16)
    upper = lax.broadcasted_iota(I32, (CHUNK, LANES), 1) % 64 >= 32

    def gather_b(to, c):
        gather_rows(to, 0, table, lambda i: smem_b[c * SPLIT + i // LANES, i % LANES], CHUNK)

    def raw_sums(side_b, c):
        a = side_a[pl.ds(pl.multiple_of(c * CHUNK, CHUNK), CHUNK), :]
        b = pltpu.roll(side_b[...], 64, 1)
        jump = pltpu.roll(a + b, 32, 1)
        hi, lo = split(jnp.where(upper, jump * a, pltpu.roll(jump * b, 96, 1)))
        return dot_nt(pick, jnp.concatenate([hi, lo], 1))

    def add_sums(raw, c, carry):
        sum_a, sum_b = carry
        face = c * CHUNK + lax.broadcasted_iota(I32, (1, CHUNK), 1)
        area = jnp.where(face < 3 * live, 0.5 * (1.0 - 0.75 * lanes_of(hanging, c).astype(F32)), 0.0)
        is_even = lanes_of(face_dir, c) % 2 == 0
        term_a = area * jnp.where(is_even, raw[1:2], raw[3:4])
        term_b = area * jnp.where(is_even, raw[0:1], raw[2:3])
        cell, other = lanes_of(face_cell, c), lanes_of(face_other, c)
        sum_a += scatter(cell, term_a, CELLS // LANES, low_onehot(cell))
        sum_b += scatter(other, term_b, SLOTS // LANES, low_onehot(other))
        return sum_a, sum_b

    def body(i, carry):
        raw_before, sums = carry
        gather_b(side_b1, 2 * i + 1)
        raw = raw_sums(side_b0, 2 * i)
        sums = add_sums(raw_before, jnp.maximum(2 * i - 1, 0), sums)
        gather_b(side_b0, jnp.minimum(2 * i + 2, CHUNKS - 1))
        raw_after = raw_sums(side_b1, 2 * i + 1)
        sums = add_sums(raw, 2 * i, sums)
        return raw_after, sums

    gather_b(side_b0, 0)
    zero = (jnp.zeros((CELLS // LANES, LANES), F32), jnp.zeros((SLOTS // LANES, LANES), F32))
    raw, sums = lax.fori_loop(0, CHUNKS // 2, body, (jnp.zeros((8, CHUNK), F32), zero))
    sum_a, sum_b = add_sums(raw, CHUNKS - 1, sums)
    for k in SEND_ORDER:
        at = CELLS // LANES + 2 * k
        partial[k] = sum_b[at : at + 2]
    backs = [remote(partial.at[k], returned.at[k], b_send, b_recv, behind(me, -SHIFTS[k])) for k in SEND_ORDER]
    for copy in backs:
        copy.start()
    index = jnp.concatenate([send_v[k : k + 1, :] for k in range(NEIGH)], 1)
    out = term[...] + sum_a + sum_b[: CELLS // LANES]
    remote(partial, returned, b_send, b_recv, behind(me, 1)).wait_recv()
    value = jnp.concatenate([returned[k, r : r + 1, :] for k in range(NEIGH) for r in range(2)], 1)
    out = out + scatter(index, value, CELLS // LANES, onehot[...])
    slot = lax.broadcasted_iota(I32, out.shape, 0) * LANES + lax.broadcasted_iota(I32, out.shape, 1)
    indicator[...] = out

    total = jnp.sum(jnp.where(slot < live, jnp.abs(out), 0.0), axis=0, keepdims=True)
    place = 0
    for stage, (stride, count) in enumerate(STAGES):
        part[stage] = total
        slots = pl.ds(place, count - 1)
        for step in range(1, count):
            remote(part.at[stage], parts.at[place + step - 1], r_send.at[stage], r_recv.at[stage],
                   in_stage(me, stride, count, step)).start()
        remote(parts.at[slots], parts.at[slots], r_send.at[stage], r_recv.at[stage], behind(me, 1)).wait_recv()
        total = total + jnp.sum(parts[place : place + count - 1], axis=0)
        place += count - 1

    mean = jnp.sum(total) / cells.astype(F32)
    facts[...] = jnp.where(slot < live, mean, -1.0)
    remote(partial, returned, b_send, b_recv, behind(me, 1)).wait_send()
    place = 0
    for stage, (stride, count) in enumerate(STAGES):
        slots = pl.ds(place, count - 1)
        remote(parts.at[slots], parts.at[slots], r_send.at[stage], r_recv.at[stage], behind(me, 1)).wait_send()
        place += count - 1


SMEM = pl.BlockSpec(memory_space=pltpu.SMEM)
VMEM = pl.BlockSpec(memory_space=pltpu.VMEM)
ANY = pl.BlockSpec(memory_space=pl.ANY)


def per_device(primal, dual, load, cell_size, cell_count, ghost_send, face_cell, face_other, face_dir, hanging,
               stiffness, recon, traction, trace):
    send = ghost_send[0]
    as_rows = lambda x: x.reshape(-1, LANES)
    f32 = lambda *shape: pltpu.VMEM(shape, F32)
    bf16 = lambda *shape: pltpu.VMEM(shape, BF16)
    i32 = lambda *shape: pltpu.VMEM(shape, I32)
    dma = lambda n: pltpu.SemaphoreType.DMA((n,))
    rows = FACES // LANES
    cells = CELLS // LANES
    steps = sum(size - 1 for _, size in STAGES)
    scratch = [
        f32(DOF, CELLS), f32(DOF, CELLS), f32(DOF, CELLS), f32(cells, LANES), i32(NEIGH, GHOST),
        i32(rows, LANES), i32(rows, LANES), i32(rows, LANES), i32(rows, LANES),
        f32(DOF, DOF), f32(768, CHILD * DOF), f32(6 * FACE_DOF, DOF), f32(6 * FACE_DOF, DOF),
        f32(CELLS, LANES),
        f32(8, LANES), f32(8, LANES), f32(8, LANES), f32(8, LANES), f32(16, LANES),
        f32(NEIGH, PACKED, LANES), f32(NEIGH, PACKED, LANES), f32(NEIGH, PACKED, LANES), f32(NEIGH, PACKED, LANES),
        f32(3 * THIRD, LANES),
        f32(FAMILIES * CHILD + 8, LANES), f32(FAMILIES * CHILD, LANES), f32(FAMILIES, 768), f32(FAMILIES, 768),
        f32(384, 256), bf16(768, 384), f32(3 * SLOTS, LANES), f32(FACES, LANES), f32(CHUNK, LANES), f32(CHUNK, LANES),
        bf16(768, 2304), bf16(LANES, GHOSTS),
        i32(rows, LANES), i32(rows, LANES), pltpu.SMEM((rows, LANES), I32), pltpu.SMEM((rows, LANES), I32),
        f32(cells, LANES), f32(NEIGH, 2, LANES), f32(NEIGH, 2, LANES), f32(len(STAGES), 1, LANES), f32(steps, 1, LANES),
        dma(13), dma(2), dma(2), dma(2), dma(NEIGH), dma(NEIGH), dma(NEIGH), dma(NEIGH),
        pltpu.SemaphoreType.DMA, pltpu.SemaphoreType.DMA, dma(len(STAGES)), dma(len(STAGES)),
    ]
    indicator, facts = pl.pallas_call(
        kernel,
        out_shape=[jax.ShapeDtypeStruct((cells, LANES), F32)] * 2,
        in_specs=[SMEM] * 2 + [ANY] * 13, out_specs=[VMEM] * 2, scratch_shapes=scratch,
        compiler_params=pltpu.CompilerParams(collective_id=0, has_side_effects=True,
                                             vmem_limit_bytes=56 * 1024 * 1024),
        name="indicators",
    )(cell_count, send, primal, dual, load, as_rows(cell_size), send, as_rows(face_cell), as_rows(face_other),
      as_rows(face_dir), as_rows(hanging), stiffness, recon, traction, trace)
    facts = facts.reshape(-1)
    indicator = jnp.where(facts < 0.0, 0.0, indicator.reshape(-1))
    return indicator, jnp.abs(indicator) / (jnp.abs(facts) + 1e-06)

def solution(mesh):
    in_specs = (P(None, "dom"), P(None, "dom"), P(None, "dom"), P("dom"), P(), P("dom", None, None), P("dom"), P("dom"),
                P("dom"), P("dom"), P(), P(), P(), P())
    return jax.shard_map(per_device, mesh=mesh, in_specs=in_specs, out_specs=(P("dom"), P("dom")), check_vma=False)
```
